32 devices in a mesh: seq: 8 (over z, y), mp: 4 (over x, core).
Axes of the slice: x: 2, y: 2, z: 4, core: 2. Of those that a mesh axis runs over, the one named last changes fastest.
Arguments:
- hidden_rows: bfloat16 [2048, 1536], P('seq', 'mp'), may hold values from -6 to 6
- norm_gain: bfloat16 [1536], P('mp'), may hold values from 0.099609375 to 1.8984375
- encodings: bfloat16 [16, 128, 1536], P('seq', None, 'mp'), may hold values from -56 to 56
- w_query: bfloat16 [1536, 1536], P('seq', 'mp'), may hold values from -0.15625 to 0.15625
- w_key: bfloat16 [1536, 1536], P('seq', 'mp'), may hold values from -0.15625 to 0.15625
- w_value: bfloat16 [1536, 1536], P('seq', 'mp'), may hold values from -0.625 to 0.625
- w_out: bfloat16 [1536, 1536], P('mp', 'seq'), may hold values from -0.4375 to 0.4375
- neighbours: int32 [32, 2], P('seq'), may hold values from 0 to 15, as said below
- grad_out: bfloat16 [2048, 1536], P('seq', 'mp'), may hold values from -6 to 6
Outputs:
- branch_out: bfloat16 [2048, 1536], P('seq', 'mp')
- grad_rows: bfloat16 [2048, 1536], P('seq', 'mp')
- grad_encodings: bfloat16 [16, 128, 1536], P('seq', None, 'mp')
The draws below stay inside these ranges and needn't reach their ends.
Inputs may be any that keep to these rules, and one draw needn't show every extreme that they name: `neighbours`: A stretch of seq device d names only encoded stretches whose owner, id // 2, is one of the devices d - 2 to d + 2 along seq, counted around the axis. On every device the first stretch names an encoded stretch of owner d - 2 first and, second, the last encoded stretch (local index 1) of owner d + 2.
All inputs are finite; a program needn't handle non-finite values.
Results may differ from the reference program's by a relative error of at most 0.023.
The reference program's roundings to bfloat16 on the way (of `normed`, `queries`, `weights_low`, `attended`, `d_attended`, `d_scores` and `d_queries`) count: a program that leaves them out, or rounds other values in their place, can miss the bound.
Values may be sent and summed in bfloat16 or wider, within the bound.
No kernel may reach another device: no remote copies, remote signals or barrier semaphores. Data moves between devices by JAX's collectives and lax.ppermute only.
A program may use at most 64 MiB of HBM per device.

```python
import jax
import jax.numpy as jnp
from jax import lax

D = 1536
HEADS = 12
HD = 128
STRETCH = 64
NBR = 2
RET = 128
SPAN = 2
CH_DEV = 4
OWN_DEV = 2
STRETCHES = 32
TOKENS = 2048
BASE = 16
N_MP = 4


def draw_encodings(key, part):
    first_key = jax.random.fold_in(key, 0)
    return jnp.clip(jax.random.normal(first_key, (BASE, RET, D), jnp.float32), -6.0, 6.0).astype(jnp.bfloat16)


def draw_neighbours(key, part):
    split_keys = jax.random.split(key, 4)
    device_count = STRETCHES // CH_DEV
    span_width = 2 * SPAN + 1
    offsets = jnp.minimum(jax.random.randint(split_keys[0], (STRETCHES, NBR), 0, span_width), jax.random.randint(split_keys[1], (STRETCHES, NBR), 0, span_width)) - SPAN
    local_index = jnp.minimum(jax.random.randint(split_keys[2], (STRETCHES, NBR), 0, OWN_DEV), jax.random.randint(split_keys[3], (STRETCHES, NBR), 0, OWN_DEV))
    leading = (jnp.arange(STRETCHES) % CH_DEV == 0)[:, None]
    column = jnp.arange(NBR)[None, :]
    forced = jnp.where(column == 0, -SPAN, SPAN)
    offsets = jnp.where(leading, forced, offsets)
    local_index = jnp.where(leading & (column == 1), OWN_DEV - 1, local_index)
    device = (jnp.arange(STRETCHES) // CH_DEV)[:, None]
    owner = (device + offsets) % device_count
    return (owner * OWN_DEV + local_index).astype(jnp.int32)


def block_scale(key, dims, shards, low, high):
    loudness = 1.0
    for position, shards_of in shards:
        draws = jax.random.uniform(jax.random.fold_in(jax.random.fold_in(key, 6), position), (shards_of,), jnp.float32, low / len(shards), high / len(shards))
        loudness = loudness * jnp.repeat(jnp.exp(draws), dims[position] // shards_of).reshape((-1,) + (1,) * (len(dims) - 1 - position))
    return loudness


def scatter_about(own_key, extent, deviation, reach, shards=(), dtype=jnp.bfloat16):
    result = jax.random.normal(own_key, extent, jnp.float32) * deviation
    if len(shards) > 0:
        result = block_scale(own_key, extent, shards, -0.22, 0.18) * result
    return jnp.clip(result, min=-reach, max=reach).astype(dtype)


def setup_inputs(seed: int = 0) -> dict:
    keys = jax.random.split(jax.random.key(seed), 10)
    hidden_rows = scatter_about(keys[0], (TOKENS, D), 1.0, 6.0, ((0, 8), (1, 4)))
    norm_gain = jnp.clip(1.0 + 0.18 * jax.random.normal(keys[1], (D,), jnp.float32), 0.099609375, 1.8984375).astype(jnp.bfloat16)
    encodings = draw_encodings(jax.random.fold_in(keys[9], 71), 0)
    w_query = scatter_about(keys[3], (D, D), D ** -0.5, 0.15625, ((0, 8), (1, 4)))
    w_key = scatter_about(keys[4], (D, D), D ** -0.5, 0.15625, ((0, 8), (1, 4)))
    w_value = scatter_about(keys[5], (D, D), (D // 16) ** -0.5, 0.625, ((0, 8), (1, 4)))
    w_out = scatter_about(keys[6], (D, D), (D // 8) ** -0.5, 0.4375, ((0, 4), (1, 8)))
    neighbours = draw_neighbours(jax.random.fold_in(keys[9], 71), 0)
    grad_out = scatter_about(keys[8], (TOKENS, D), 1.0, 6.0, ((0, 8), (1, 4)))
    return {"hidden_rows": hidden_rows, "norm_gain": norm_gain, "encodings": encodings, "w_query": w_query, "w_key": w_key, "w_value": w_value, "w_out": w_out, "neighbours": neighbours, "grad_out": grad_out}


epsilon = 1e-05

def round_low(values):
    return lax.optimization_barrier(values.astype(jnp.bfloat16)).astype(jnp.float32)

def grouped_sum(left, right, transpose_right):
    group_width = D // N_MP
    summed = jnp.zeros((left.shape[0], D), jnp.float32)
    for group in range(N_MP):
        begin = group * group_width
        left_part = left[:, begin:begin + group_width]
        if transpose_right:
            right_part = right[:, begin:begin + group_width].T
        else:
            right_part = right[begin:begin + group_width, :]
        summed = summed + round_low(jnp.dot(left_part, right_part, preferred_element_type=jnp.float32))
    return summed

def reference(hidden_rows, norm_gain, encodings, w_query, w_key, w_value, w_out, neighbours, grad_out):
    rows_float = hidden_rows.astype(jnp.float32)
    gain_float = norm_gain.astype(jnp.float32)
    inv_rms = lax.rsqrt(lax.optimization_barrier(jnp.mean(rows_float * rows_float, axis=1, keepdims=True)) + epsilon)
    normed = (rows_float * inv_rms * gain_float).astype(jnp.bfloat16)
    queries = jnp.dot(normed, w_query, preferred_element_type=jnp.float32).astype(jnp.bfloat16)
    enc_flat = encodings.reshape(BASE * RET, D)
    key_table = jnp.dot(enc_flat, w_key, preferred_element_type=jnp.float32).astype(jnp.bfloat16).reshape(BASE, RET, HEADS, HD)
    value_table = jnp.dot(enc_flat, w_value, preferred_element_type=jnp.float32).astype(jnp.bfloat16).reshape(BASE, RET, HEADS, HD)
    d_attended = jnp.dot(grad_out, w_out.T, preferred_element_type=jnp.float32).astype(jnp.bfloat16)
    score_scale = HD ** (-0.5)

    def one_stretch(carry, item):
        key_grads, value_grads = carry
        query_block, grad_block, chosen = item
        key_rows = key_table[chosen].reshape(NBR * RET, HEADS, HD).astype(jnp.float32)
        value_rows = value_table[chosen].reshape(NBR * RET, HEADS, HD).astype(jnp.float32)
        query_float = query_block.astype(jnp.float32)
        grad_float = grad_block.astype(jnp.float32)
        scores = jnp.einsum('mhe,she->hms', query_float, key_rows) * score_scale
        row_peak = lax.optimization_barrier(jnp.max(scores, axis=2, keepdims=True))
        exponent = jnp.exp(scores - row_peak)
        weights = exponent / lax.optimization_barrier(jnp.sum(exponent, axis=2, keepdims=True))
        weights_low = round_low(weights)
        attended = jnp.einsum('hms,she->mhe', weights_low, value_rows).astype(jnp.bfloat16)
        d_weights = jnp.einsum('mhe,she->hms', grad_float, value_rows)
        d_scores = round_low(weights * (d_weights - lax.optimization_barrier(jnp.sum(d_weights * weights, axis=2, keepdims=True))) * score_scale)
        d_queries = jnp.einsum('hms,she->mhe', d_scores, key_rows).astype(jnp.bfloat16)
        d_keys = jnp.einsum('hms,mhe->she', d_scores, query_float).reshape(NBR, RET, HEADS, HD)
        d_values = jnp.einsum('hms,mhe->she', weights_low, grad_float).reshape(NBR, RET, HEADS, HD)
        key_grads = key_grads.at[chosen].add(d_keys)
        value_grads = value_grads.at[chosen].add(d_values)
        return ((key_grads, value_grads), (attended, d_queries))
    zeros_table = jnp.zeros((BASE, RET, HEADS, HD), jnp.float32)
    items = (queries.reshape(STRETCHES, STRETCH, HEADS, HD), d_attended.reshape(STRETCHES, STRETCH, HEADS, HD), neighbours.astype(jnp.int32))
    (key_grads, value_grads), (attended, d_queries) = lax.scan(one_stretch, (zeros_table, zeros_table), items)
    attended = attended.reshape(TOKENS, D)
    d_queries = d_queries.reshape(TOKENS, D)
    branch_out = grouped_sum(attended, w_out, False).astype(jnp.bfloat16)
    d_normed = grouped_sum(d_queries, w_query, True)
    statistic = lax.optimization_barrier(jnp.mean(rows_float * gain_float * d_normed, axis=1, keepdims=True))
    grad_rows = (inv_rms * gain_float * d_normed - rows_float * inv_rms ** 3 * statistic).astype(jnp.bfloat16)
    key_low = key_grads.astype(jnp.bfloat16).reshape(BASE * RET, D)
    value_low = value_grads.astype(jnp.bfloat16).reshape(BASE * RET, D)
    group_width = D // N_MP
    enc_summed = jnp.zeros((BASE * RET, D), jnp.float32)
    for group in range(N_MP):
        begin = group * group_width
        product = jnp.dot(key_low[:, begin:begin + group_width], w_key[:, begin:begin + group_width].T, preferred_element_type=jnp.float32)
        product = product + jnp.dot(value_low[:, begin:begin + group_width], w_value[:, begin:begin + group_width].T, preferred_element_type=jnp.float32)
        enc_summed = enc_summed + round_low(product)
    grad_encodings = enc_summed.astype(jnp.bfloat16).reshape(BASE, RET, D)
    return (branch_out, grad_rows, grad_encodings)
```

```python
import jax
import jax.numpy as jnp
from jax import lax
from jax.experimental import pallas as pl
from jax.experimental.pallas import tpu as pltpu
from jax.sharding import PartitionSpec as P

HD = 128
STRETCH = 64
NBR = 2
RET = 128
OWN_DEV = 2
OWN_ROWS = OWN_DEV * RET
GAIN_ROWS = 16
LOW = jnp.bfloat16
F32 = jnp.float32
epsilon = 1e-05


def joint(step):
    seq_count, mp_count = lax.axis_size("seq"), lax.axis_size("mp")
    pairs = []
    for d in range(seq_count):
        for m in range(mp_count):
            target = step(d // 2, d % 2, m // 2, m % 2)
            if target is not None:
                z, y, x, c = target
                pairs.append((d * mp_count + m, ((z % (seq_count // 2)) * 2 + y) * mp_count + 2 * x + c))
    return pairs


def move(value, step):
    return lax.ppermute(value, ("seq", "mp"), joint(step))


def swap(z, y, x, c):
    return (z, c, x, y)


def cross(z, y, x, c):
    return (z, c, x, 1 - y)


def flip_x(z, y, x, c):
    return (z, y, 1 - x, c)


def flip_y(z, y, x, c):
    return (z, 1 - y, x, c)


def flip_core(z, y, x, c):
    return (z, y, x, 1 - c)


def ring_up(z, y, x, c):
    return (z + 1, y, x, c)


def ring_down(z, y, x, c):
    return (z - 1, y, x, c)


def place():
    d, m = lax.axis_index("seq"), lax.axis_index("mp")
    return d // 2, d % 2, m // 2, m % 2


def spread(value, x_first):
    first, second = (flip_x, flip_y) if x_first else (flip_y, flip_x)
    near = move(value, first)
    other = move(value, second)
    far = move(near, second)
    if x_first:
        return [value, other, near, far]
    return [value, near, other, far]


def line_pieces(own, z):
    from_below = move(own, lambda z, y, x, c: (z + 1, y, x, c) if z < 3 else None)
    from_above = move(own, lambda z, y, x, c: (z - 1, y, x, c) if z > 0 else None)
    below_two = move(from_below, lambda z, y, x, c: (z + 1, y, x, c) if z in (1, 2) else None)
    above_two = move(from_above, lambda z, y, x, c: (z - 1, y, x, c) if z in (1, 2) else None)
    two = jnp.where(z <= 1, above_two, below_two)
    three = move(two, lambda z, y, x, c: {1: (0, y, x, c), 2: (3, y, x, c)}.get(z))
    pieces = [own, from_below, from_above, two, three]
    return pieces + [move(piece, flip_core) for piece in pieces]


def any_pieces(own, z, y, g):
    seq_count = lax.axis_size("seq")
    z_count = seq_count // 2
    groups = [[2 * i + j for i in range(z_count)] for j in range(2)]
    mine = lax.all_gather(own, "seq", axis=0, axis_index_groups=groups)
    theirs = move(mine, flip_core)
    c = lax.axis_index("mp") % 2
    both = jnp.stack([jnp.where(c == 0, mine, theirs), jnp.where(c == 0, theirs, mine)], axis=1)
    rows = own.shape[0] // 2
    both = both.reshape(seq_count, 2, rows, -1)
    both = jnp.moveaxis(both, 1, 2).reshape(4, seq_count * rows // 4, 2, -1)
    ordered = jnp.take(both, g ^ jnp.arange(4), axis=0)
    width = ordered.shape[-1]
    return [ordered.reshape(seq_count * rows, 2 * width)]


def assemble(pieces, whole, z, c, g):
    if len(pieces) == 1:
        whole[...] = pieces[0][...]
        return
    rows = pieces[0].shape[0] // 2
    width = pieces[0].shape[1]
    half = len(pieces) // 2

    def put(piece, from_z, from_c):
        start = pl.multiple_of(((from_z ^ g) * 2 + from_c) * rows, 64)
        whole[pl.ds(start, rows), 0:width] = piece[0:rows, :]
        whole[pl.ds(start, rows), width : 2 * width] = piece[rows : 2 * rows, :]

    for side in range(2):
        own, below, above, two, three = pieces[side * half : (side + 1) * half]
        side_c = c if side == 0 else 1 - c
        put(own, z, side_c)
        put(two, (z + 2) % 4, side_c)

        @pl.when(z > 0)
        def _():
            put(below, z - 1, side_c)

        @pl.when(z < 3)
        def _():
            put(above, z + 1, side_c)

        @pl.when(jnp.logical_or(z == 0, z == 3))
        def _():
            put(three, 3 - z, side_c)


def table_kernel(piece_count, token_count, *refs):
    z, y, x, c = place()
    g = 2 * x + y
    rows_refs, refs = refs[:4], refs[4:]
    enc_refs, refs = refs[:12], refs[12:]
    pieces, refs = refs[:piece_count], refs[piece_count:]
    normed_out, inv_out, whole, tables, shared = refs
    full_width = 4 * rows_refs[0].shape[1]
    total = None
    for ref in rows_refs:
        rows = ref[0:token_count, :].astype(F32)
        part = jnp.sum(rows * rows, axis=1, keepdims=True)
        total = part if total is None else total + part
    inv_rms = lax.rsqrt(total / full_width + epsilon)
    inv_out[...] = inv_rms
    for k, ref in enumerate(rows_refs):
        width = ref.shape[1]
        rows = ref[0:token_count, :].astype(F32)
        gain = ref[token_count : token_count + 1, :].astype(F32)
        normed_out[:, k * width : (k + 1) * width] = (rows * inv_rms * gain).astype(LOW)
    assemble(pieces, whole, z, c, g)
    for i in range(3):
        enc = jnp.concatenate([ref[...] for ref in enc_refs[4 * i : 4 * i + 4]], axis=1)
        tables[i * OWN_ROWS : (i + 1) * OWN_ROWS, :] = jnp.dot(
            enc, whole[...], preferred_element_type=F32
        ).astype(LOW)
    shared[0:OWN_ROWS, :] = tables[OWN_ROWS : 2 * OWN_ROWS, :]
    start = pl.multiple_of(jnp.where(c == 1, 0, 2 * OWN_ROWS), OWN_ROWS)
    shared[OWN_ROWS : 2 * OWN_ROWS, :] = tables[pl.ds(start, OWN_ROWS), :]


def attention_kernel(piece_count, seq_count, *refs):
    z, y, x, c = place()
    g = 2 * x + y
    chosen, normed, refs = refs[0], refs[1], refs[2:]
    grad_refs, refs = refs[:4], refs[4:]
    pieces, refs = refs[:piece_count], refs[piece_count:]
    tables, shared, attended, d_queries, whole, d_own, d_shared, queries, d_attended, window, d_window = refs
    token_count = normed.shape[0]
    width = attended.shape[1]
    assemble(pieces, whole, z, c, g)
    queries[...] = jnp.dot(normed[...], whole[:, 0:width], preferred_element_type=F32).astype(LOW)
    grads = jnp.concatenate([ref[...] for ref in grad_refs], axis=1)
    d_attended[...] = jnp.dot(grads, whole[:, width:], preferred_element_type=F32).astype(LOW)
    window[0 : 3 * OWN_ROWS, :] = tables[...]
    window[3 * OWN_ROWS : 5 * OWN_ROWS, :] = shared[...]
    d_window[...] = jnp.zeros_like(d_window)
    scale = HD ** (-0.5)
    t = 2 * z + c
    across = (((1,), (1,)), ((), ()))
    down = (((0,), (0,)), ((), ()))
    for s in range(token_count // STRETCH):
        starts = []
        for j in range(NBR):
            name = chosen[s, j]
            away = (name // OWN_DEV - t + 2 + seq_count) % seq_count
            odd = 3 + jnp.where(away == 1, 1 - c, c)
            index = jnp.where(away % 2 == 0, away // 2, odd)
            starts.append(pl.multiple_of(index * OWN_ROWS + (name % OWN_DEV) * RET, RET))
        tokens = slice(s * STRETCH, (s + 1) * STRETCH)
        for h in range(width // HD):
            left = slice(h * HD, (h + 1) * HD)
            right = slice(width + h * HD, width + (h + 1) * HD)
            keys = jnp.concatenate([window[pl.ds(a, RET), left] for a in starts], axis=0)
            values = jnp.concatenate([window[pl.ds(a, RET), right] for a in starts], axis=0)
            query = queries[tokens, left]
            d_att = d_attended[tokens, left]
            scores = lax.dot_general(query, keys, across, preferred_element_type=F32) * scale
            exponent = jnp.exp(scores - jnp.max(scores, axis=1, keepdims=True))
            weights = exponent / jnp.sum(exponent, axis=1, keepdims=True)
            weights_low = weights.astype(LOW)
            attended[tokens, left] = jnp.dot(
                weights_low, values, preferred_element_type=F32
            ).astype(LOW)
            d_weights = lax.dot_general(d_att, values, across, preferred_element_type=F32)
            inner = jnp.sum(d_weights * weights, axis=1, keepdims=True)
            d_scores = (weights * (d_weights - inner) * scale).astype(LOW)
            d_queries[tokens, left] = jnp.dot(d_scores, keys, preferred_element_type=F32).astype(LOW)
            d_keys = lax.dot_general(d_scores, query, down, preferred_element_type=F32)
            d_values = lax.dot_general(weights_low, d_att, down, preferred_element_type=F32)
            for j, a in enumerate(starts):
                d_window[pl.ds(a, RET), left] += d_keys[j * RET : (j + 1) * RET, :]
                d_window[pl.ds(a, RET), right] += d_values[j * RET : (j + 1) * RET, :]
    d_own[...] = d_window[0 : 3 * OWN_ROWS, :]
    d_shared[...] = d_window[3 * OWN_ROWS : 5 * OWN_ROWS, :].astype(LOW)


def product_kernel(*refs):
    attended, d_queries, whole = refs[:3]
    rows_refs = refs[3:7]
    near, far, partial = refs[7:]
    token_count, width = attended.shape
    across = (((1,), (1,)), ((), ()))
    total = None
    for k in range(4):
        block = slice(k * width, (k + 1) * width)
        out = lax.dot_general(
            attended[...], whole[block, width:], across, preferred_element_type=F32
        ).astype(LOW)
        back = lax.dot_general(
            d_queries[...], whole[block, 0:width], across, preferred_element_type=F32
        ).astype(LOW)
        target = near if k < 2 else far
        target[0, k % 2] = out
        target[1, k % 2] = back
        rows = rows_refs[k][0:token_count, :].astype(F32)
        gain = rows_refs[k][token_count : token_count + 1, :].astype(F32)
        part = jnp.sum(rows * gain * back.astype(F32), axis=1, keepdims=True)
        total = part if total is None else total + part
    partial[...] = total


def encoding_kernel(own, up, down, whole, near, far):
    width = whole.shape[1] // 2
    own_low = (own[...] + up[...].astype(F32) + down[...].astype(F32)).astype(LOW)
    across = (((1,), (1,)), ((), ()))
    for k in range(4):
        target = near if k < 2 else far
        target[k % 2] = lax.dot_general(
            own_low, whole[k * width : (k + 1) * width, :], across, preferred_element_type=F32
        ).astype(LOW)


def call(kernel, operands, outs, scratch=(), first_small=False):
    in_vmem = pl.BlockSpec(memory_space=pltpu.VMEM)
    specs = [in_vmem] * len(operands)
    if first_small:
        specs[0] = pl.BlockSpec(memory_space=pltpu.SMEM)
    return pl.pallas_call(
        kernel,
        out_shape=[jax.ShapeDtypeStruct(shape, dtype) for shape, dtype in outs],
        in_specs=specs,
        out_specs=[in_vmem] * len(outs),
        scratch_shapes=list(scratch),
        compiler_params=pltpu.CompilerParams(vmem_limit_bytes=40 * 1024 * 1024),
    )(*operands)


def reduce_blocks(near, far):
    arrived = move(far, flip_x)
    both = (near.astype(F32) + arrived.astype(F32)).astype(LOW)
    first = move(both[..., 0, :, :], swap)
    second = move(both[..., 1, :, :], cross)
    return first.astype(F32) + second.astype(F32)


def shards(hidden_rows, norm_gain, encodings, w_query, w_key, w_value, w_out, neighbours, grad_out):
    seq_count = lax.axis_size("seq")
    z, y, x, c = place()
    g = 2 * x + y
    token_count, width = hidden_rows.shape
    full_width = 4 * width

    key_value = move(jnp.concatenate([w_key, w_value], axis=0), swap)
    own_enc = move(encodings.reshape(OWN_ROWS, width), swap)
    query_out = move(jnp.concatenate([w_query, w_out.T], axis=0), swap)
    gain_rows = jnp.broadcast_to(norm_gain[None, :], (GAIN_ROWS, width))
    tokens = move(jnp.concatenate([hidden_rows, gain_rows], axis=0), swap)
    grads = move(grad_out, swap)
    chosen = move(neighbours, swap)

    enc_below = move(own_enc, ring_up)
    enc_above = move(own_enc, ring_down)
    if seq_count == 8:
        kv_pieces = line_pieces(key_value, z)
        qo_pieces = line_pieces(query_out, z)
    else:
        kv_pieces = any_pieces(key_value, z, y, g)
        qo_pieces = any_pieces(query_out, z, y, g)
    enc_blocks = spread(enc_below, True) + spread(own_enc, False) + spread(enc_above, True)
    token_blocks = spread(tokens, False)
    grad_blocks = spread(grads, False)

    normed, inv_rms, whole_kv, tables, shared = call(
        lambda *refs: table_kernel(len(kv_pieces), token_count, *refs),
        token_blocks + enc_blocks + kv_pieces,
        [
            ((token_count, full_width), LOW),
            ((token_count, 1), F32),
            ((full_width, 2 * width), LOW),
            ((3 * OWN_ROWS, 2 * width), LOW),
            ((2 * OWN_ROWS, 2 * width), LOW),
        ],
    )
    shared = move(shared, flip_core)
    inv_rms = inv_rms.reshape(token_count // 128, 128)
    inv_rms = jnp.where(c == y, inv_rms, move(inv_rms, flip_core)).reshape(token_count, 1)
    attended, d_queries, whole_qo, d_own, d_shared = call(
        lambda *refs: attention_kernel(len(qo_pieces), seq_count, *refs),
        [chosen, normed] + grad_blocks + qo_pieces + [tables, shared],
        [
            ((token_count, width), LOW),
            ((token_count, width), LOW),
            ((full_width, 2 * width), LOW),
            ((3 * OWN_ROWS, 2 * width), F32),
            ((2 * OWN_ROWS, 2 * width), LOW),
        ],
        [
            pltpu.VMEM((token_count, width), LOW),
            pltpu.VMEM((token_count, width), LOW),
            pltpu.VMEM((5 * OWN_ROWS, 2 * width), LOW),
            pltpu.VMEM((5 * OWN_ROWS, 2 * width), F32),
        ],
        first_small=True,
    )
    from_core = move(d_shared, flip_core)
    outer = from_core[OWN_ROWS:].astype(F32)
    to_below = (d_own[:OWN_ROWS] + jnp.where(c == 1, outer, 0.0)).astype(LOW)
    to_above = (d_own[2 * OWN_ROWS :] + jnp.where(c == 0, outer, 0.0)).astype(LOW)
    kept = d_own[OWN_ROWS : 2 * OWN_ROWS] + from_core[:OWN_ROWS].astype(F32)
    up = move(to_above, ring_up)
    down = move(to_below, ring_down)

    near, far, partial = call(
        product_kernel,
        [attended, d_queries, whole_qo] + token_blocks,
        [
            ((2, 2, token_count, width), LOW),
            ((2, 2, token_count, width), LOW),
            ((token_count, 1), F32),
        ],
    )
    sums = reduce_blocks(near, far)
    branch_out = sums[0].astype(LOW)
    partial = partial.reshape(token_count // 128, 128)
    partial = partial + move(partial, flip_x)
    partial = move(partial, swap) + move(partial, cross)
    statistic = partial.reshape(token_count, 1) / full_width
    gain = norm_gain.astype(F32)[None, :]
    grad_rows = (
        inv_rms * gain * sums[1] - hidden_rows.astype(F32) * inv_rms**3 * statistic
    ).astype(LOW)

    near_enc, far_enc = call(
        encoding_kernel,
        [kept, up, down, whole_kv],
        [((2, OWN_ROWS, width), LOW), ((2, OWN_ROWS, width), LOW)],
    )
    grad_encodings = reduce_blocks(near_enc, far_enc).astype(LOW).reshape(encodings.shape)
    return (branch_out, grad_rows, grad_encodings)


def solution(mesh):
    placed = (
        P("seq", "mp"),
        P("mp"),
        P("seq", None, "mp"),
        P("seq", "mp"),
        P("seq", "mp"),
        P("seq", "mp"),
        P("mp", "seq"),
        P("seq", None),
        P("seq", "mp"),
    )
    return jax.shard_map(
        shards,
        mesh=mesh,
        in_specs=placed,
        out_specs=(P("seq", "mp"), P("seq", "mp"), P("seq", None, "mp")),
        check_vma=False,
    )
```

```python
import jax
import jax.numpy as jnp
from jax import lax
from jax.experimental import pallas as pl
from jax.experimental.pallas import tpu as pltpu
from jax.sharding import PartitionSpec as P

HD = 128
STRETCH = 64
NBR = 2
RET = 128
OWN_DEV = 2
OWN_ROWS = OWN_DEV * RET
EXTRA = 16
LOW = jnp.bfloat16
F32 = jnp.float32
epsilon = 1e-05
ANY = pl.BlockSpec(memory_space=pl.ANY)
VMEM = pl.BlockSpec(memory_space=pltpu.VMEM)
SMEM = pl.BlockSpec(memory_space=pltpu.SMEM)
ACROSS = (((1,), (1,)), ((), ()))
DOWN = (((0,), (0,)), ((), ()))


def move(value, step):
    seq_count, mp_count = lax.axis_size("seq"), lax.axis_size("mp")
    z_count = seq_count // 2
    pairs = []
    for d in range(seq_count):
        for m in range(mp_count):
            target = step(d // 2, d % 2, m // 2, m % 2)
            if target is not None:
                z, y, x, c = target
                pairs.append((d * mp_count + m, ((z % z_count) * 2 + y) * mp_count + 2 * x + c))
    return lax.ppermute(value, ("seq", "mp"), pairs)


def spread(k):
    return lambda z, y, x, c: (z, c ^ (k % 2), x ^ (k // 2), y)


def gather_back(k):
    return lambda z, y, x, c: (z, c, x ^ (k // 2), y ^ (k % 2))


def flip_core(z, y, x, c):
    return (z, y, x, 1 - c)


def ring_up(z, y, x, c):
    return (z + 1, y, x, c)


def ring_down(z, y, x, c):
    return (z - 1, y, x, c)


def place():
    d, m = lax.axis_index("seq"), lax.axis_index("mp")
    return d // 2, d % 2, m // 2, m % 2


def tie(*values):
    return lax.optimization_barrier(values)


def any_weights(own, c, g):
    seq_count = lax.axis_size("seq")
    z_count = seq_count // 2
    rows, width = own.shape[0] // 4, own.shape[1]
    groups = [[2 * i + j for i in range(z_count)] for j in range(2)]
    mine = lax.all_gather(own, "seq", axis=0, axis_index_groups=groups)
    theirs = move(mine, flip_core)
    both = jnp.stack([jnp.where(c == 0, mine, theirs), jnp.where(c == 0, theirs, mine)], axis=1)
    both = jnp.moveaxis(both.reshape(seq_count, 4, rows, width), 1, 0)
    both = both.reshape(4, 4, seq_count * rows // 4, width)
    both = jnp.take(both, g ^ jnp.arange(4), axis=1).reshape(4, seq_count * rows, width)
    return [jnp.concatenate([both[0], both[1]], axis=1)], [jnp.concatenate([both[2], both[3]], axis=1)]


def run_copies(pairs, sems):
    copies = [pltpu.make_async_copy(a, b, sems.at[i]) for i, (a, b) in enumerate(pairs)]
    for copy in copies:
        copy.start()
    for copy in copies:
        copy.wait()


def weight_copies(pieces, whole, first):
    if len(pieces) == 1:
        return [(pieces[0], whole)]
    z, y, x, c = place()
    g = 2 * x + y
    rows, width = pieces[0].shape[0] // 4, pieces[0].shape[1]
    pairs = []
    for side in range(2):
        side_c = c if side == 0 else 1 - c
        for step, ref in zip((0, 3, 1, 2), pieces[4 * side : 4 * side + 4]):
            start = pl.multiple_of((((z + step) % 4 ^ g) * 2 + side_c) * rows, 64)
            for j in range(2):
                pairs.append(
                    (
                        ref.at[pl.ds((first + j) * rows, rows)],
                        whole.at[pl.ds(start, rows), pl.ds(j * width, width)],
                    )
                )
    return pairs


def norm_kernel(token_count, *refs):
    token_refs, normed, inv_out, rows_in, sems = refs[:4], *refs[4:]
    width = token_refs[0].shape[1]
    run_copies(
        [(ref.at[pl.ds(0, token_count + EXTRA)], rows_in.at[k]) for k, ref in enumerate(token_refs)],
        sems,
    )
    total = None
    for k in range(4):
        rows = rows_in[k, 0:token_count, :].astype(F32)
        part = jnp.sum(rows * rows, axis=1, keepdims=True)
        total = part if total is None else total + part
    inv_rms = lax.rsqrt(total / (4 * width) + epsilon)
    inv_out[...] = inv_rms
    for k in range(4):
        rows = rows_in[k, 0:token_count, :].astype(F32)
        gain = rows_in[k, token_count : token_count + 1, :].astype(F32)
        normed[:, k * width : (k + 1) * width] = (rows * inv_rms * gain).astype(LOW)


def table_kernel(token_count, *refs):
    token_refs, outer_refs = refs[:4], refs[4:8]
    pieces, (whole, tables, shared, encs, sems) = refs[8:-5], refs[-5:]
    width = token_refs[0].shape[1]
    pairs = weight_copies(pieces, whole, 0)
    for k in range(4):
        block = pl.ds(k * width, width)
        for i, (ref, start) in enumerate(
            ((outer_refs[k], 0), (token_refs[k], 2 * token_count + EXTRA), (outer_refs[k], OWN_ROWS))
        ):
            pairs.append((ref.at[pl.ds(start, OWN_ROWS)], encs.at[pl.ds(i * OWN_ROWS, OWN_ROWS), block]))
    run_copies(pairs, sems)
    tables[...] = jnp.dot(encs[...], whole[...], preferred_element_type=F32).astype(LOW)
    shared[0:OWN_ROWS, :] = tables[OWN_ROWS : 2 * OWN_ROWS, :]
    z, y, x, c = place()
    start = pl.multiple_of(jnp.where(c == 1, 0, 2 * OWN_ROWS), OWN_ROWS)
    shared[OWN_ROWS : 2 * OWN_ROWS, :] = tables[pl.ds(start, OWN_ROWS), :]


def query_kernel(token_count, *refs):
    normed, token_refs = refs[0], refs[1:5]
    pieces, (whole, queries, d_attended, rows_in, grads, sems) = refs[5:-6], refs[-6:]
    width = token_refs[0].shape[1]
    pairs = weight_copies(pieces, whole, 2) + [(normed, rows_in)]
    for k, ref in enumerate(token_refs):
        pairs.append(
            (ref.at[pl.ds(token_count + EXTRA, token_count)], grads.at[:, pl.ds(k * width, width)])
        )
    run_copies(pairs, sems)
    queries[...] = jnp.dot(rows_in[...], whole[:, 0:width], preferred_element_type=F32).astype(LOW)
    d_attended[...] = jnp.dot(grads[...], whole[:, width:], preferred_element_type=F32).astype(LOW)


def attention_kernel(seq_count, *refs):
    chosen, tables, shared, queries, d_attended = refs[:5]
    attended, d_queries, d_own, d_outer, d_shared, window, d_window, sems = refs[5:]
    token_count, width = queries.shape
    run_copies(
        [
            (tables, window.at[pl.ds(0, 3 * OWN_ROWS)]),
            (shared, window.at[pl.ds(3 * OWN_ROWS, 2 * OWN_ROWS)]),
        ],
        sems,
    )
    d_window[...] = jnp.zeros_like(d_window)
    scale = HD ** (-0.5)
    z, y, x, c = place()
    t = 2 * z + c
    for s in range(token_count // STRETCH):
        starts = []
        for j in range(NBR):
            name = chosen[s * NBR + j]
            away = (name // OWN_DEV - t + 2 + seq_count) % seq_count
            odd = 3 + jnp.where(away == 1, 1 - c, c)
            index = jnp.where(away % 2 == 0, away // 2, odd)
            starts.append(pl.multiple_of(index * OWN_ROWS + (name % OWN_DEV) * RET, RET))
        tokens = slice(s * STRETCH, (s + 1) * STRETCH)
        for h in range(width // HD):
            left = slice(h * HD, (h + 1) * HD)
            right = slice(width + h * HD, width + (h + 1) * HD)
            keys = jnp.concatenate([window[pl.ds(a, RET), left] for a in starts], axis=0)
            values = jnp.concatenate([window[pl.ds(a, RET), right] for a in starts], axis=0)
            query = queries[tokens, left]
            d_att = d_attended[tokens, left]
            scores = lax.dot_general(query, keys, ACROSS, preferred_element_type=F32) * scale
            exponent = jnp.exp(scores - jnp.max(scores, axis=1, keepdims=True))
            weights = exponent / jnp.sum(exponent, axis=1, keepdims=True)
            weights_low = weights.astype(LOW)
            attended[tokens, left] = jnp.dot(
                weights_low, values, preferred_element_type=F32
            ).astype(LOW)
            d_weights = lax.dot_general(d_att, values, ACROSS, preferred_element_type=F32)
            inner = jnp.sum(d_weights * weights, axis=1, keepdims=True)
            d_scores = (weights * (d_weights - inner) * scale).astype(LOW)
            d_queries[tokens, left] = jnp.dot(d_scores, keys, preferred_element_type=F32).astype(LOW)
            d_keys = lax.dot_general(d_scores, query, DOWN, preferred_element_type=F32)
            d_values = lax.dot_general(weights_low, d_att, DOWN, preferred_element_type=F32)
            for j, a in enumerate(starts):
                d_window[pl.ds(a, RET), left] += d_keys[j * RET : (j + 1) * RET, :]
                d_window[pl.ds(a, RET), right] += d_values[j * RET : (j + 1) * RET, :]
    d_own[...] = d_window[OWN_ROWS : 2 * OWN_ROWS, :]
    d_outer[0:OWN_ROWS, :] = d_window[0:OWN_ROWS, :].astype(LOW)
    d_outer[OWN_ROWS : 2 * OWN_ROWS, :] = d_window[2 * OWN_ROWS : 3 * OWN_ROWS, :].astype(LOW)
    d_shared[...] = d_window[3 * OWN_ROWS : 5 * OWN_ROWS, :].astype(LOW)


def as_row(column):
    return jnp.transpose(jnp.broadcast_to(column, (column.shape[0], 128)))[0:1, :]


def product_kernel(*refs):
    attended, d_queries, inv_rms, whole_in = refs[:4]
    token_refs, outs, (whole, rows_in, sems) = refs[4:8], refs[8:12], refs[12:]
    token_count, width = attended.shape
    pairs = [(whole_in, whole)]
    for k, ref in enumerate(token_refs):
        pairs.append((ref.at[pl.ds(0, token_count + EXTRA)], rows_in.at[k]))
    run_copies(pairs, sems)
    total = None
    for k, out in enumerate(outs):
        block = slice(k * width, (k + 1) * width)
        out[0:token_count, :] = lax.dot_general(
            attended[...], whole[block, width:], ACROSS, preferred_element_type=F32
        ).astype(LOW)
        back = lax.dot_general(
            d_queries[...], whole[block, 0:width], ACROSS, preferred_element_type=F32
        ).astype(LOW)
        out[token_count : 2 * token_count, :] = back
        rows = rows_in[k, 0:token_count, :].astype(F32)
        gain = rows_in[k, token_count : token_count + 1, :].astype(F32)
        part = jnp.sum(rows * gain * back.astype(F32), axis=1, keepdims=True)
        total = part if total is None else total + part
    lines = []
    for column in (total, inv_rms[...]):
        line = as_row(column)
        high = line.astype(LOW).astype(F32)
        lines += [high, line - high]
    lines.append(jnp.zeros((EXTRA - 4, token_count), F32))
    extra = jnp.concatenate(lines, axis=0)
    extra = jnp.concatenate([extra, jnp.zeros((EXTRA, width - token_count), F32)], axis=1).astype(LOW)
    for out in outs:
        out[2 * token_count : 2 * token_count + EXTRA, :] = extra


def finish_kernel(hidden, gain, *refs):
    terms, (branch_out, grad_rows) = refs[:4], refs[4:]
    token_count, width = hidden.shape
    branch, normed_grad, extra = None, None, None
    for k, term in enumerate(terms):
        out = term[0:token_count, :].astype(F32)
        back = term[token_count : 2 * token_count, :].astype(F32)
        lines = term[2 * token_count : 2 * token_count + EXTRA, :].astype(F32)
        branch = out if k == 0 else branch + out
        normed_grad = back if k == 0 else normed_grad + back
        extra = lines if k == 0 else extra + lines
        if k == 0:
            inv_row = lines[2:3, 0:token_count] + lines[3:4, 0:token_count]
    branch_out[...] = branch.astype(LOW)
    stat_row = extra[0:1, 0:token_count] + extra[1:2, 0:token_count]

    def as_column(row):
        return jnp.transpose(jnp.broadcast_to(row, (128, token_count)))[:, 0:1]

    statistic = as_column(stat_row) / (4 * width)
    inv_rms = as_column(inv_row)
    rows = hidden[...].astype(F32)
    grad_rows[...] = (
        inv_rms * gain[...].astype(F32) * normed_grad - rows * inv_rms * inv_rms * inv_rms * statistic
    ).astype(LOW)


def encoding_kernel(own, from_core, up, down, whole, *outs):
    width = whole.shape[1] // 2
    own_low = own[...] + from_core[0:OWN_ROWS, :].astype(F32)
    own_low = (own_low + up[...].astype(F32) + down[...].astype(F32)).astype(LOW)
    for k, out in enumerate(outs):
        out[...] = lax.dot_general(
            own_low, whole[k * width : (k + 1) * width, :], ACROSS, preferred_element_type=F32
        ).astype(LOW)


def call(kernel, operands, specs, outs, scratch=(), copies=0):
    scratch = list(scratch)
    if copies:
        scratch.append(pltpu.SemaphoreType.DMA((copies,)))
    return pl.pallas_call(
        kernel,
        out_shape=[jax.ShapeDtypeStruct(shape, dtype) for shape, dtype in outs],
        in_specs=specs,
        out_specs=[VMEM] * len(outs),
        scratch_shapes=scratch,
        compiler_params=pltpu.CompilerParams(vmem_limit_bytes=40 * 1024 * 1024),
    )(*operands)


def shards(hidden_rows, norm_gain, encodings, w_query, w_key, w_value, w_out, neighbours, grad_out):
    seq_count = lax.axis_size("seq")
    z, y, x, c = place()
    g = 2 * x + y
    token_count, width = hidden_rows.shape
    full_width = 4 * width
    ids = neighbours.size
    wide = 2 * width

    own_enc = encodings.reshape(OWN_ROWS, width)
    weights = move(jnp.concatenate([w_key, w_value, w_query, w_out.T], axis=0), spread(0))
    enc_below, enc_above = move(own_enc, ring_up), move(own_enc, ring_down)
    extra = jnp.pad(norm_gain[None, :], ((0, EXTRA - 1), (0, 0)))
    extra = extra + jnp.pad(neighbours.reshape(1, ids).astype(LOW), ((1, EXTRA - 2), (0, width - ids)))
    packed = jnp.concatenate([hidden_rows, extra, grad_out, own_enc], axis=0)
    weights, enc_below, enc_above, packed = tie(weights, enc_below, enc_above, packed)
    tokens = [move(packed, spread(k)) for k in range(4)]
    outer = jnp.concatenate([enc_below, enc_above], axis=0)
    if seq_count == 8:
        below, above = move(weights, ring_up), move(weights, ring_down)
        outer, below, above, *tokens = tie(outer, below, above, *tokens)
        two_below = move(below, lambda z, y, x, c: (z + 1, y, x, c) if z in (1, 2) else None)
        two_above = move(above, lambda z, y, x, c: (z - 1, y, x, c) if z in (1, 2) else None)
        pieces = [weights, below, above, jnp.where(z <= 1, two_above, two_below)]
        pieces = pieces + [move(piece, flip_core) for piece in pieces]
        kv_pieces = qo_pieces = pieces
    else:
        kv_pieces, qo_pieces = any_weights(weights, c, g)
    outer = [move(outer, spread(k)) for k in range(4)]
    piece_count = len(kv_pieces)

    chosen = tokens[0][token_count + 1, :ids].astype(jnp.int32)
    normed, inv_rms = call(
        lambda *refs: norm_kernel(token_count, *refs),
        tokens,
        [ANY] * 4,
        [((token_count, full_width), LOW), ((token_count, 1), F32)],
        [pltpu.VMEM((4, token_count + EXTRA, width), LOW)],
        4,
    )
    whole_kv, tables, shared = call(
        lambda *refs: table_kernel(token_count, *refs),
        tokens + outer + kv_pieces,
        [ANY] * (8 + piece_count),
        [((full_width, wide), LOW), ((3 * OWN_ROWS, wide), LOW), ((2 * OWN_ROWS, wide), LOW)],
        [pltpu.VMEM((3 * OWN_ROWS, full_width), LOW)],
        12 + 2 * piece_count,
    )
    shared = move(shared, flip_core)
    whole_qo, queries, d_attended = call(
        lambda *refs: query_kernel(token_count, *refs),
        [normed] + tokens + qo_pieces,
        [ANY] * (5 + piece_count),
        [((full_width, wide), LOW), ((token_count, width), LOW), ((token_count, width), LOW)],
        [pltpu.VMEM((token_count, full_width), LOW), pltpu.VMEM((token_count, full_width), LOW)],
        5 + 2 * piece_count,
    )
    attended, d_queries, d_own, d_outer, d_shared = call(
        lambda *refs: attention_kernel(seq_count, *refs),
        [chosen, tables, shared, queries, d_attended],
        [SMEM, ANY, ANY, VMEM, VMEM],
        [
            ((token_count, width), LOW),
            ((token_count, width), LOW),
            ((OWN_ROWS, wide), F32),
            ((2 * OWN_ROWS, wide), LOW),
            ((2 * OWN_ROWS, wide), LOW),
        ],
        [pltpu.VMEM((5 * OWN_ROWS, wide), LOW), pltpu.VMEM((5 * OWN_ROWS, wide), F32)],
        2,
    )
    from_core = move(d_shared, flip_core)
    shared_grad = from_core[OWN_ROWS:].astype(F32)
    to_below = (d_outer[:OWN_ROWS] + jnp.where(c == 1, shared_grad, 0.0)).astype(LOW)
    to_above = (d_outer[OWN_ROWS:] + jnp.where(c == 0, shared_grad, 0.0)).astype(LOW)
    terms = call(
        product_kernel,
        [attended, d_queries, inv_rms, whole_qo] + tokens,
        [VMEM, VMEM, VMEM] + [ANY] * 5,
        [((2 * token_count + EXTRA, width), LOW)] * 4,
        [
            pltpu.VMEM((full_width, wide), LOW),
            pltpu.VMEM((4, token_count + EXTRA, width), LOW),
        ],
        5,
    )
    to_below, to_above, *terms = tie(to_below, to_above, *terms)
    up, down = move(to_above, ring_up), move(to_below, ring_down)
    terms = [move(term, gather_back(k)) for k, term in enumerate(terms)]
    branch_out, grad_rows = call(
        finish_kernel,
        [hidden_rows, norm_gain[None, :]] + terms,
        [VMEM] * 6,
        [((token_count, width), LOW), ((token_count, width), LOW)],
    )
    enc_terms = call(
        encoding_kernel,
        [d_own, from_core, up, down, whole_kv],
        [VMEM] * 5,
        [((OWN_ROWS, width), LOW)] * 4,
    )
    enc_terms = [move(term, gather_back(k)).astype(F32) for k, term in enumerate(enc_terms)]
    grad_encodings = (enc_terms[0] + enc_terms[1] + enc_terms[2] + enc_terms[3]).astype(LOW)
    return (branch_out, grad_rows, grad_encodings.reshape(encodings.shape))


def solution(mesh):
    placed = (
        P("seq", "mp"),
        P("mp"),
        P("seq", None, "mp"),
        P("seq", "mp"),
        P("seq", "mp"),
        P("seq", "mp"),
        P("mp", "seq"),
        P("seq", None),
        P("seq", "mp"),
    )
    return jax.shard_map(
        shards,
        mesh=mesh,
        in_specs=placed,
        out_specs=(P("seq", "mp"), P("seq", "mp"), P("seq", None, "mp")),
        check_vma=False,
    )
```

```python
import jax
import jax.numpy as jnp
from jax import lax
from jax.experimental import pallas as pl
from jax.experimental.pallas import tpu as pltpu
from jax.sharding import PartitionSpec as P

HD = 128
STRETCH = 64
NBR = 2
RET = 128
OWN_DEV = 2
OWN_ROWS = OWN_DEV * RET
EXTRA = 16
LOW = jnp.bfloat16
F32 = jnp.float32
epsilon = 1e-05
ANY = pl.BlockSpec(memory_space=pl.ANY)
VMEM = pl.BlockSpec(memory_space=pltpu.VMEM)
SMEM = pl.BlockSpec(memory_space=pltpu.SMEM)
ACROSS = (((1,), (1,)), ((), ()))
DOWN = (((0,), (0,)), ((), ()))


def move(value, step):
    seq_count, mp_count = lax.axis_size("seq"), lax.axis_size("mp")
    z_count = seq_count // 2
    pairs = []
    for d in range(seq_count):
        for m in range(mp_count):
            target = step(d // 2, d % 2, m // 2, m % 2)
            if target is not None:
                z, y, x, c = target
                pairs.append((d * mp_count + m, ((z % z_count) * 2 + y) * mp_count + 2 * x + c))
    return lax.ppermute(value, ("seq", "mp"), pairs)


def spread(k):
    return lambda z, y, x, c: (z, c ^ (k % 2), x ^ (k // 2), y)


def gather_back(k):
    return lambda z, y, x, c: (z, c, x ^ (k // 2), y ^ (k % 2))


def flip_core(z, y, x, c):
    return (z, y, x, 1 - c)


def ring_up(z, y, x, c):
    return (z + 1, y, x, c)


def ring_down(z, y, x, c):
    return (z - 1, y, x, c)


def place():
    d, m = lax.axis_index("seq"), lax.axis_index("mp")
    return d // 2, d % 2, m // 2, m % 2


def tie(*values):
    return lax.optimization_barrier(values)


def any_weights(own, c, g):
    seq_count = lax.axis_size("seq")
    z_count = seq_count // 2
    rows, width = own.shape[0] // 4, own.shape[1]
    groups = [[2 * i + j for i in range(z_count)] for j in range(2)]
    mine = lax.all_gather(own, "seq", axis=0, axis_index_groups=groups)
    theirs = move(mine, flip_core)
    both = jnp.stack([jnp.where(c == 0, mine, theirs), jnp.where(c == 0, theirs, mine)], axis=1)
    both = jnp.moveaxis(both.reshape(seq_count, 4, rows, width), 1, 0)
    both = both.reshape(4, 4, seq_count * rows // 4, width)
    both = jnp.take(both, g ^ jnp.arange(4), axis=1).reshape(4, seq_count * rows, width)
    return [jnp.concatenate([both[0], both[1]], axis=1)], [jnp.concatenate([both[2], both[3]], axis=1)]


def run_copies(pairs, sems):
    copies = [pltpu.make_async_copy(a, b, sems.at[i]) for i, (a, b) in enumerate(pairs)]
    for copy in copies:
        copy.start()
    for copy in copies:
        copy.wait()


def weight_copies(pieces, whole, first):
    if len(pieces) == 1:
        return [(pieces[0], whole)]
    z, y, x, c = place()
    g = 2 * x + y
    rows, width = pieces[0].shape[0] // 4, pieces[0].shape[1]
    pairs = []
    for side in range(2):
        side_c = c if side == 0 else 1 - c
        for step, ref in zip((0, 3, 1, 2), pieces[4 * side : 4 * side + 4]):
            start = pl.multiple_of((((z + step) % 4 ^ g) * 2 + side_c) * rows, 64)
            for j in range(2):
                pairs.append(
                    (
                        ref.at[pl.ds((first + j) * rows, rows)],
                        whole.at[pl.ds(start, rows), pl.ds(j * width, width)],
                    )
                )
    return pairs


def norm_kernel(token_count, *refs):
    token_refs, normed, inv_out, rows_in, sems = refs[:4], *refs[4:]
    width = token_refs[0].shape[1]
    run_copies(
        [(ref.at[pl.ds(0, token_count + EXTRA)], rows_in.at[k]) for k, ref in enumerate(token_refs)],
        sems,
    )
    total = None
    for k in range(4):
        rows = rows_in[k, 0:token_count, :].astype(F32)
        part = jnp.sum(rows * rows, axis=1, keepdims=True)
        total = part if total is None else total + part
    inv_rms = lax.rsqrt(total / (4 * width) + epsilon)
    inv_out[...] = inv_rms
    for k in range(4):
        rows = rows_in[k, 0:token_count, :].astype(F32)
        gain = rows_in[k, token_count : token_count + 1, :].astype(F32)
        normed[:, k * width : (k + 1) * width] = (rows * inv_rms * gain).astype(LOW)


def table_kernel(token_count, *refs):
    token_refs, outer_refs = refs[:4], refs[4:8]
    pieces, (whole, tables, shared, encs, sems) = refs[8:-5], refs[-5:]
    width = token_refs[0].shape[1]
    pairs = weight_copies(pieces, whole, 0)
    for k in range(4):
        block = pl.ds(k * width, width)
        for i, (ref, start) in enumerate(
            ((outer_refs[k], 0), (token_refs[k], 2 * token_count + EXTRA), (outer_refs[k], OWN_ROWS))
        ):
            pairs.append((ref.at[pl.ds(start, OWN_ROWS)], encs.at[pl.ds(i * OWN_ROWS, OWN_ROWS), block]))
    run_copies(pairs, sems)
    tables[...] = jnp.dot(encs[...], whole[...], preferred_element_type=F32).astype(LOW)
    shared[0:OWN_ROWS, :] = tables[OWN_ROWS : 2 * OWN_ROWS, :]
    z, y, x, c = place()
    start = pl.multiple_of(jnp.where(c == 1, 0, 2 * OWN_ROWS), OWN_ROWS)
    shared[OWN_ROWS : 2 * OWN_ROWS, :] = tables[pl.ds(start, OWN_ROWS), :]


def query_kernel(token_count, *refs):
    normed, token_refs = refs[0], refs[1:5]
    pieces, (whole, queries, d_attended, rows_in, grads, sems) = refs[5:-6], refs[-6:]
    width = token_refs[0].shape[1]
    pairs = weight_copies(pieces, whole, 2) + [(normed, rows_in)]
    for k, ref in enumerate(token_refs):
        pairs.append(
            (ref.at[pl.ds(token_count + EXTRA, token_count)], grads.at[:, pl.ds(k * width, width)])
        )
    run_copies(pairs, sems)
    queries[...] = jnp.dot(rows_in[...], whole[:, 0:width], preferred_element_type=F32).astype(LOW)
    d_attended[...] = jnp.dot(grads[...], whole[:, width:], preferred_element_type=F32).astype(LOW)


def attention_kernel(seq_count, *refs):
    chosen, tables, shared, queries, d_attended = refs[:5]
    attended, d_queries, d_own, d_outer, d_shared, window, d_window, sems = refs[5:]
    token_count, width = queries.shape
    run_copies(
        [
            (tables, window.at[pl.ds(0, 3 * OWN_ROWS)]),
            (shared, window.at[pl.ds(3 * OWN_ROWS, 2 * OWN_ROWS)]),
        ],
        sems,
    )
    d_window[...] = jnp.zeros_like(d_window)
    scale = HD ** (-0.5)
    z, y, x, c = place()
    t = 2 * z + c
    for s in range(token_count // STRETCH):
        starts = []
        for j in range(NBR):
            name = chosen[s * NBR + j]
            away = (name // OWN_DEV - t + 2 + seq_count) % seq_count
            odd = 3 + jnp.where(away == 1, 1 - c, c)
            index = jnp.where(away % 2 == 0, away // 2, odd)
            starts.append(pl.multiple_of(index * OWN_ROWS + (name % OWN_DEV) * RET, RET))
        tokens = slice(s * STRETCH, (s + 1) * STRETCH)
        for h in range(width // HD):
            left = slice(h * HD, (h + 1) * HD)
            right = slice(width + h * HD, width + (h + 1) * HD)
            keys = jnp.concatenate([window[pl.ds(a, RET), left] for a in starts], axis=0)
            values = jnp.concatenate([window[pl.ds(a, RET), right] for a in starts], axis=0)
            query = queries[tokens, left]
            d_att = d_attended[tokens, left]
            scores = lax.dot_general(query, keys, ACROSS, preferred_element_type=F32) * scale
            exponent = jnp.exp(scores - jnp.max(scores, axis=1, keepdims=True))
            weights = exponent / jnp.sum(exponent, axis=1, keepdims=True)
            weights_low = weights.astype(LOW)
            attended[tokens, left] = jnp.dot(
                weights_low, values, preferred_element_type=F32
            ).astype(LOW)
            d_weights = lax.dot_general(d_att, values, ACROSS, preferred_element_type=F32)
            inner = jnp.sum(d_weights * weights, axis=1, keepdims=True)
            d_scores = (weights * (d_weights - inner) * scale).astype(LOW)
            d_queries[tokens, left] = jnp.dot(d_scores, keys, preferred_element_type=F32).astype(LOW)
            d_keys = lax.dot_general(d_scores, query, DOWN, preferred_element_type=F32)
            d_values = lax.dot_general(weights_low, d_att, DOWN, preferred_element_type=F32)
            for j, a in enumerate(starts):
                d_window[pl.ds(a, RET), left] += d_keys[j * RET : (j + 1) * RET, :]
                d_window[pl.ds(a, RET), right] += d_values[j * RET : (j + 1) * RET, :]
    d_own[...] = d_window[OWN_ROWS : 2 * OWN_ROWS, :]
    d_outer[0:OWN_ROWS, :] = d_window[0:OWN_ROWS, :].astype(LOW)
    d_outer[OWN_ROWS : 2 * OWN_ROWS, :] = d_window[2 * OWN_ROWS : 3 * OWN_ROWS, :].astype(LOW)
    d_shared[...] = d_window[3 * OWN_ROWS : 5 * OWN_ROWS, :].astype(LOW)


def as_row(column):
    return jnp.transpose(jnp.broadcast_to(column, (column.shape[0], 128)))[0:1, :]


def product_kernel(*refs):
    attended, d_queries, inv_rms, whole_in = refs[:4]
    token_refs, outs, (whole, rows_in, sems) = refs[4:8], refs[8:12], refs[12:]
    token_count, width = attended.shape
    pairs = [(whole_in, whole)]
    for k, ref in enumerate(token_refs):
        pairs.append((ref.at[pl.ds(0, token_count + EXTRA)], rows_in.at[k]))
    run_copies(pairs, sems)
    total = None
    for k, out in enumerate(outs):
        block = slice(k * width, (k + 1) * width)
        out[0:token_count, :] = lax.dot_general(
            attended[...], whole[block, width:], ACROSS, preferred_element_type=F32
        ).astype(LOW)
        back = lax.dot_general(
            d_queries[...], whole[block, 0:width], ACROSS, preferred_element_type=F32
        ).astype(LOW)
        out[token_count : 2 * token_count, :] = back
        rows = rows_in[k, 0:token_count, :].astype(F32)
        gain = rows_in[k, token_count : token_count + 1, :].astype(F32)
        part = jnp.sum(rows * gain * back.astype(F32), axis=1, keepdims=True)
        total = part if total is None else total + part
    lines = []
    for column in (total, inv_rms[...]):
        line = as_row(column)
        high = line.astype(LOW).astype(F32)
        lines += [high, line - high]
    lines.append(jnp.zeros((EXTRA - 4, token_count), F32))
    extra = jnp.concatenate(lines, axis=0)
    extra = jnp.concatenate([extra, jnp.zeros((EXTRA, width - token_count), F32)], axis=1).astype(LOW)
    for out in outs:
        out[2 * token_count : 2 * token_count + EXTRA, :] = extra


def finish_kernel(hidden, gain, *refs):
    terms, (branch_out, grad_rows) = refs[:4], refs[4:]
    token_count, width = hidden.shape
    branch, normed_grad, extra = None, None, None
    for k, term in enumerate(terms):
        out = term[0:token_count, :].astype(F32)
        back = term[token_count : 2 * token_count, :].astype(F32)
        lines = term[2 * token_count : 2 * token_count + EXTRA, :].astype(F32)
        branch = out if k == 0 else branch + out
        normed_grad = back if k == 0 else normed_grad + back
        extra = lines if k == 0 else extra + lines
        if k == 0:
            inv_row = lines[2:3, 0:token_count] + lines[3:4, 0:token_count]
    branch_out[...] = branch.astype(LOW)
    stat_row = extra[0:1, 0:token_count] + extra[1:2, 0:token_count]

    def as_column(row):
        return jnp.transpose(jnp.broadcast_to(row, (128, token_count)))[:, 0:1]

    statistic = as_column(stat_row) / (4 * width)
    inv_rms = as_column(inv_row)
    rows = hidden[...].astype(F32)
    grad_rows[...] = (
        inv_rms * gain[...].astype(F32) * normed_grad - rows * inv_rms * inv_rms * inv_rms * statistic
    ).astype(LOW)


def encoding_kernel(own, from_core, up, down, whole, *outs):
    width = whole.shape[1] // 2
    own_low = own[...] + from_core[0:OWN_ROWS, :].astype(F32)
    own_low = (own_low + up[...].astype(F32) + down[...].astype(F32)).astype(LOW)
    for k, out in enumerate(outs):
        out[...] = lax.dot_general(
            own_low, whole[k * width : (k + 1) * width, :], ACROSS, preferred_element_type=F32
        ).astype(LOW)


def call(kernel, operands, specs, outs, scratch=(), copies=0):
    scratch = list(scratch)
    if copies:
        scratch.append(pltpu.SemaphoreType.DMA((copies,)))
    return pl.pallas_call(
        kernel,
        out_shape=[jax.ShapeDtypeStruct(shape, dtype) for shape, dtype in outs],
        in_specs=specs,
        out_specs=[VMEM] * len(outs),
        scratch_shapes=scratch,
        compiler_params=pltpu.CompilerParams(vmem_limit_bytes=16 * 1024 * 1024),
    )(*operands)


def shards(hidden_rows, norm_gain, encodings, w_query, w_key, w_value, w_out, neighbours, grad_out):
    seq_count = lax.axis_size("seq")
    z, y, x, c = place()
    g = 2 * x + y
    token_count, width = hidden_rows.shape
    full_width = 4 * width
    ids = neighbours.size
    wide = 2 * width

    own_enc = encodings.reshape(OWN_ROWS, width)
    weights = move(jnp.concatenate([w_key, w_value, w_query, w_out.T], axis=0), spread(0))
    enc_below, enc_above = move(own_enc, ring_up), move(own_enc, ring_down)
    extra = jnp.pad(norm_gain[None, :], ((0, EXTRA - 1), (0, 0)))
    extra = extra + jnp.pad(neighbours.reshape(1, ids).astype(LOW), ((1, EXTRA - 2), (0, width - ids)))
    packed = jnp.concatenate([hidden_rows, extra, grad_out, own_enc], axis=0)
    weights, enc_below, enc_above, packed = tie(weights, enc_below, enc_above, packed)
    outer = jnp.concatenate([enc_below, enc_above], axis=0)
    tokens, outers = [None] * 4, [None] * 4
    if seq_count == 8:
        below, above = move(weights, ring_up), move(weights, ring_down)
        own_other = move(weights, flip_core)
        tokens[2], tokens[3] = move(packed, spread(2)), move(packed, spread(3))
        packed, own_other = tie(packed, own_other)
        tokens[0] = move(packed, spread(0))
        packed, tokens[0] = tie(packed, tokens[0])
        tokens[1] = move(packed, spread(1))
        outer, below, above, *tokens = tie(outer, below, above, *tokens)
        two = move(jnp.where(z % 2 == 0, below, above), lambda z, y, x, c: (z ^ 1, y, x, c))
        below_other, above_other = move(below, flip_core), move(above, flip_core)
        outers[2], outers[3] = move(outer, spread(2)), move(outer, spread(3))
        outer, below_other, above_other = tie(outer, below_other, above_other)
        outers[0], outers[1] = move(outer, spread(0)), move(outer, spread(1))
        two_other = move(two, flip_core)
        kv_pieces = [weights, below, above, two, own_other, below_other, above_other, two_other]
        qo_pieces = kv_pieces
    else:
        kv_pieces, qo_pieces = any_weights(weights, c, g)
        tokens = [move(packed, spread(k)) for k in range(4)]
        outers = [move(outer, spread(k)) for k in range(4)]
    piece_count = len(kv_pieces)

    chosen = tokens[0][token_count + 1, :ids].astype(jnp.int32)
    normed, inv_rms = call(
        lambda *refs: norm_kernel(token_count, *refs),
        tokens,
        [ANY] * 4,
        [((token_count, full_width), LOW), ((token_count, 1), F32)],
        [pltpu.VMEM((4, token_count + EXTRA, width), LOW)],
        4,
    )
    whole_kv, tables, shared = call(
        lambda *refs: table_kernel(token_count, *refs),
        tokens + outers + kv_pieces,
        [ANY] * (8 + piece_count),
        [((full_width, wide), LOW), ((3 * OWN_ROWS, wide), LOW), ((2 * OWN_ROWS, wide), LOW)],
        [pltpu.VMEM((3 * OWN_ROWS, full_width), LOW)],
        12 + 2 * piece_count,
    )
    shared = move(shared, flip_core)
    whole_qo, queries, d_attended = call(
        lambda *refs: query_kernel(token_count, *refs),
        [normed] + tokens + qo_pieces,
        [ANY] * (5 + piece_count),
        [((full_width, wide), LOW), ((token_count, width), LOW), ((token_count, width), LOW)],
        [pltpu.VMEM((token_count, full_width), LOW), pltpu.VMEM((token_count, full_width), LOW)],
        5 + 2 * piece_count,
    )
    attended, d_queries, d_own, d_outer, d_shared = call(
        lambda *refs: attention_kernel(seq_count, *refs),
        [chosen, tables, shared, queries, d_attended],
        [SMEM, ANY, ANY, VMEM, VMEM],
        [
            ((token_count, width), LOW),
            ((token_count, width), LOW),
            ((OWN_ROWS, wide), F32),
            ((2 * OWN_ROWS, wide), LOW),
            ((2 * OWN_ROWS, wide), LOW),
        ],
        [pltpu.VMEM((5 * OWN_ROWS, wide), LOW), pltpu.VMEM((5 * OWN_ROWS, wide), F32)],
        2,
    )
    from_core = move(d_shared, flip_core)
    shared_grad = from_core[OWN_ROWS:].astype(F32)
    to_below = (d_outer[:OWN_ROWS] + jnp.where(c == 1, shared_grad, 0.0)).astype(LOW)
    to_above = (d_outer[OWN_ROWS:] + jnp.where(c == 0, shared_grad, 0.0)).astype(LOW)
    terms = call(
        product_kernel,
        [attended, d_queries, inv_rms, whole_qo] + tokens,
        [VMEM, VMEM, VMEM] + [ANY] * 5,
        [((2 * token_count + EXTRA, width), LOW)] * 4,
        [
            pltpu.VMEM((full_width, wide), LOW),
            pltpu.VMEM((4, token_count + EXTRA, width), LOW),
        ],
        5,
    )
    to_below, to_above, *terms = tie(to_below, to_above, *terms)
    up, down = move(to_above, ring_up), move(to_below, ring_down)
    terms[1], up = tie(terms[1], up)
    terms = [move(term, gather_back(k)) for k, term in enumerate(terms)]
    branch_out, grad_rows = call(
        finish_kernel,
        [hidden_rows, norm_gain[None, :]] + terms,
        [VMEM] * 6,
        [((token_count, width), LOW), ((token_count, width), LOW)],
    )
    enc_terms = call(
        encoding_kernel,
        [d_own, from_core, up, down, whole_kv],
        [VMEM] * 5,
        [((OWN_ROWS, width), LOW)] * 4,
    )
    enc_terms = [move(term, gather_back(k)).astype(F32) for k, term in enumerate(enc_terms)]
    grad_encodings = (enc_terms[0] + enc_terms[1] + enc_terms[2] + enc_terms[3]).astype(LOW)
    return (branch_out, grad_rows, grad_encodings.reshape(encodings.shape))


def solution(mesh):
    placed = (
        P("seq", "mp"),
        P("mp"),
        P("seq", None, "mp"),
        P("seq", "mp"),
        P("seq", "mp"),
        P("seq", "mp"),
        P("mp", "seq"),
        P("seq", None),
        P("seq", "mp"),
    )
    return jax.shard_map(
        shards,
        mesh=mesh,
        in_specs=placed,
        out_specs=(P("seq", "mp"), P("seq", "mp"), P("seq", None, "mp")),
        check_vma=False,
    )
```

```python
import jax
import jax.numpy as jnp
from jax import lax
from jax.experimental import pallas as pl
from jax.experimental.pallas import tpu as pltpu
from jax.sharding import PartitionSpec as P

HD = 128
STRETCH = 64
NBR = 2
RET = 128
OWN_DEV = 2
OWN_ROWS = OWN_DEV * RET
EXTRA = 16
LOW = jnp.bfloat16
F32 = jnp.float32
epsilon = 1e-05
ANY = pl.BlockSpec(memory_space=pl.ANY)
VMEM = pl.BlockSpec(memory_space=pltpu.VMEM)
SMEM = pl.BlockSpec(memory_space=pltpu.SMEM)
ACROSS = (((1,), (1,)), ((), ()))
DOWN = (((0,), (0,)), ((), ()))


def move(value, step):
    seq_count, mp_count = lax.axis_size("seq"), lax.axis_size("mp")
    z_count = seq_count // 2
    pairs = []
    for d in range(seq_count):
        for m in range(mp_count):
            target = step(d // 2, d % 2, m // 2, m % 2)
            if target is not None:
                z, y, x, c = target
                pairs.append((d * mp_count + m, ((z % z_count) * 2 + y) * mp_count + 2 * x + c))
    return lax.ppermute(value, ("seq", "mp"), pairs)


def spread(k):
    return lambda z, y, x, c: (z, c ^ (k % 2), x ^ (k // 2), y)


def gather_back(k):
    return lambda z, y, x, c: (z, c, x ^ (k // 2), y ^ (k % 2))


def flip_core(z, y, x, c):
    return (z, y, x, 1 - c)


def ring_up(z, y, x, c):
    return (z + 1, y, x, c)


def ring_down(z, y, x, c):
    return (z - 1, y, x, c)


def place():
    d, m = lax.axis_index("seq"), lax.axis_index("mp")
    return d // 2, d % 2, m // 2, m % 2


def tie(*values):
    return lax.optimization_barrier(values)


def any_weights(own, c, g):
    seq_count = lax.axis_size("seq")
    z_count = seq_count // 2
    rows, width = own.shape[0] // 4, own.shape[1]
    groups = [[2 * i + j for i in range(z_count)] for j in range(2)]
    mine = lax.all_gather(own, "seq", axis=0, axis_index_groups=groups)
    theirs = move(mine, flip_core)
    both = jnp.stack([jnp.where(c == 0, mine, theirs), jnp.where(c == 0, theirs, mine)], axis=1)
    both = jnp.moveaxis(both.reshape(seq_count, 4, rows, width), 1, 0)
    both = both.reshape(4, 4, seq_count * rows // 4, width)
    both = jnp.take(both, g ^ jnp.arange(4), axis=1).reshape(4, seq_count * rows, width)
    return [jnp.concatenate([both[0], both[1]], axis=1)], [jnp.concatenate([both[2], both[3]], axis=1)]


def run_copies(pairs, sems):
    copies = [pltpu.make_async_copy(a, b, sems.at[i]) for i, (a, b) in enumerate(pairs)]
    for copy in copies:
        copy.start()
    for copy in copies:
        copy.wait()


def weight_copies(pieces, whole, first):
    if len(pieces) == 1:
        return [(pieces[0], whole)]
    z, y, x, c = place()
    g = 2 * x + y
    rows, width = pieces[0].shape[0] // 4, pieces[0].shape[1]
    pairs = []
    for side in range(2):
        side_c = c if side == 0 else 1 - c
        for step, ref in zip((0, 3, 1, 2), pieces[4 * side : 4 * side + 4]):
            start = pl.multiple_of((((z + step) % 4 ^ g) * 2 + side_c) * rows, 64)
            for j in range(2):
                pairs.append(
                    (
                        ref.at[pl.ds((first + j) * rows, rows)],
                        whole.at[pl.ds(start, rows), pl.ds(j * width, width)],
                    )
                )
    return pairs


def norm_kernel(token_count, *refs):
    token_refs, normed, inv_out, rows_in, sems = refs[:4], *refs[4:]
    width = token_refs[0].shape[1]
    run_copies(
        [(ref.at[pl.ds(0, token_count + EXTRA)], rows_in.at[k]) for k, ref in enumerate(token_refs)],
        sems,
    )
    total = None
    for k in range(4):
        rows = rows_in[k, 0:token_count, :].astype(F32)
        part = jnp.sum(rows * rows, axis=1, keepdims=True)
        total = part if total is None else total + part
    inv_rms = lax.rsqrt(total / (4 * width) + epsilon)
    inv_out[...] = inv_rms
    for k in range(4):
        rows = rows_in[k, 0:token_count, :].astype(F32)
        gain = rows_in[k, token_count : token_count + 1, :].astype(F32)
        normed[:, k * width : (k + 1) * width] = (rows * inv_rms * gain).astype(LOW)


def table_kernel(token_count, *refs):
    token_refs, outer_refs = refs[:4], refs[4:8]
    pieces, (tables, shared, whole, encs, sems) = refs[8:-5], refs[-5:]
    width = token_refs[0].shape[1]
    pairs = weight_copies(pieces, whole, 0)
    for k in range(4):
        block = pl.ds(k * width, width)
        for i, (ref, start) in enumerate(
            ((outer_refs[k], 0), (token_refs[k], 2 * token_count + EXTRA), (outer_refs[k], OWN_ROWS))
        ):
            pairs.append((ref.at[pl.ds(start, OWN_ROWS)], encs.at[pl.ds(i * OWN_ROWS, OWN_ROWS), block]))
    run_copies(pairs, sems)
    tables[...] = jnp.dot(encs[...], whole[...], preferred_element_type=F32).astype(LOW)
    shared[0:OWN_ROWS, :] = tables[OWN_ROWS : 2 * OWN_ROWS, :]
    z, y, x, c = place()
    start = pl.multiple_of(jnp.where(c == 1, 0, 2 * OWN_ROWS), OWN_ROWS)
    shared[OWN_ROWS : 2 * OWN_ROWS, :] = tables[pl.ds(start, OWN_ROWS), :]


def query_kernel(token_count, *refs):
    normed, token_refs = refs[0], refs[1:5]
    pieces, (queries, d_attended, whole, rows_in, grads, sems) = refs[5:-6], refs[-6:]
    width = token_refs[0].shape[1]
    pairs = weight_copies(pieces, whole, 2) + [(normed, rows_in)]
    for k, ref in enumerate(token_refs):
        pairs.append(
            (ref.at[pl.ds(token_count + EXTRA, token_count)], grads.at[:, pl.ds(k * width, width)])
        )
    run_copies(pairs, sems)
    queries[...] = jnp.dot(rows_in[...], whole[:, 0:width], preferred_element_type=F32).astype(LOW)
    d_attended[...] = jnp.dot(grads[...], whole[:, width:], preferred_element_type=F32).astype(LOW)


def attention_kernel(seq_count, *refs):
    chosen, tables, shared, queries, d_attended = refs[:5]
    attended, d_queries, d_own, d_outer, d_shared, window, d_window, sems = refs[5:]
    token_count, width = queries.shape
    run_copies(
        [
            (tables, window.at[pl.ds(0, 3 * OWN_ROWS)]),
            (shared, window.at[pl.ds(3 * OWN_ROWS, 2 * OWN_ROWS)]),
        ],
        sems,
    )
    d_window[...] = jnp.zeros_like(d_window)
    scale = HD ** (-0.5)
    z, y, x, c = place()
    t = 2 * z + c
    for s in range(token_count // STRETCH):
        starts = []
        for j in range(NBR):
            name = chosen[s * NBR + j]
            away = (name // OWN_DEV - t + 2 + seq_count) % seq_count
            odd = 3 + jnp.where(away == 1, 1 - c, c)
            index = jnp.where(away % 2 == 0, away // 2, odd)
            starts.append(pl.multiple_of(index * OWN_ROWS + (name % OWN_DEV) * RET, RET))
        tokens = slice(s * STRETCH, (s + 1) * STRETCH)
        for h in range(width // HD):
            left = slice(h * HD, (h + 1) * HD)
            right = slice(width + h * HD, width + (h + 1) * HD)
            keys = jnp.concatenate([window[pl.ds(a, RET), left] for a in starts], axis=0)
            values = jnp.concatenate([window[pl.ds(a, RET), right] for a in starts], axis=0)
            query = queries[tokens, left]
            d_att = d_attended[tokens, left]
            scores = lax.dot_general(query, keys, ACROSS, preferred_element_type=F32) * scale
            exponent = jnp.exp(scores - jnp.max(scores, axis=1, keepdims=True))
            weights = exponent / jnp.sum(exponent, axis=1, keepdims=True)
            weights_low = weights.astype(LOW)
            attended[tokens, left] = jnp.dot(
                weights_low, values, preferred_element_type=F32
            ).astype(LOW)
            d_weights = lax.dot_general(d_att, values, ACROSS, preferred_element_type=F32)
            inner = jnp.sum(d_weights * weights, axis=1, keepdims=True)
            d_scores = (weights * (d_weights - inner) * scale).astype(LOW)
            d_queries[tokens, left] = jnp.dot(d_scores, keys, preferred_element_type=F32).astype(LOW)
            d_keys = lax.dot_general(d_scores, query, DOWN, preferred_element_type=F32)
            d_values = lax.dot_general(weights_low, d_att, DOWN, preferred_element_type=F32)
            for j, a in enumerate(starts):
                d_window[pl.ds(a, RET), left] += d_keys[j * RET : (j + 1) * RET, :]
                d_window[pl.ds(a, RET), right] += d_values[j * RET : (j + 1) * RET, :]
    d_own[...] = d_window[OWN_ROWS : 2 * OWN_ROWS, :]
    d_outer[0:OWN_ROWS, :] = d_window[0:OWN_ROWS, :].astype(LOW)
    d_outer[OWN_ROWS : 2 * OWN_ROWS, :] = d_window[2 * OWN_ROWS : 3 * OWN_ROWS, :].astype(LOW)
    d_shared[...] = d_window[3 * OWN_ROWS : 5 * OWN_ROWS, :].astype(LOW)


def as_row(column):
    return jnp.transpose(jnp.broadcast_to(column, (column.shape[0], 128)))[0:1, :]


def product_kernel(*refs):
    attended, d_queries, inv_rms = refs[:3]
    token_refs, pieces, outs, (whole, rows_in, sems) = refs[3:7], refs[7:-7], refs[-7:-3], refs[-3:]
    token_count, width = attended.shape
    pairs = weight_copies(pieces, whole, 2)
    for k, ref in enumerate(token_refs):
        pairs.append((ref.at[pl.ds(0, token_count + EXTRA)], rows_in.at[k]))
    run_copies(pairs, sems)
    total = None
    for k, out in enumerate(outs):
        block = slice(k * width, (k + 1) * width)
        out[0:token_count, :] = lax.dot_general(
            attended[...], whole[block, width:], ACROSS, preferred_element_type=F32
        ).astype(LOW)
        back = lax.dot_general(
            d_queries[...], whole[block, 0:width], ACROSS, preferred_element_type=F32
        ).astype(LOW)
        out[token_count : 2 * token_count, :] = back
        rows = rows_in[k, 0:token_count, :].astype(F32)
        gain = rows_in[k, token_count : token_count + 1, :].astype(F32)
        part = jnp.sum(rows * gain * back.astype(F32), axis=1, keepdims=True)
        total = part if total is None else total + part
    lines = []
    for column in (total, inv_rms[...]):
        line = as_row(column)
        high = line.astype(LOW).astype(F32)
        lines += [high, line - high]
    lines.append(jnp.zeros((EXTRA - 4, token_count), F32))
    extra = jnp.concatenate(lines, axis=0)
    extra = jnp.concatenate([extra, jnp.zeros((EXTRA, width - token_count), F32)], axis=1).astype(LOW)
    for out in outs:
        out[2 * token_count : 2 * token_count + EXTRA, :] = extra


def finish_kernel(hidden, gain, *refs):
    terms, (branch_out, grad_rows) = refs[:4], refs[4:]
    token_count, width = hidden.shape
    branch, normed_grad, extra = None, None, None
    for k, term in enumerate(terms):
        out = term[0:token_count, :].astype(F32)
        back = term[token_count : 2 * token_count, :].astype(F32)
        lines = term[2 * token_count : 2 * token_count + EXTRA, :].astype(F32)
        branch = out if k == 0 else branch + out
        normed_grad = back if k == 0 else normed_grad + back
        extra = lines if k == 0 else extra + lines
        if k == 0:
            inv_row = lines[2:3, 0:token_count] + lines[3:4, 0:token_count]
    branch_out[...] = branch.astype(LOW)
    stat_row = extra[0:1, 0:token_count] + extra[1:2, 0:token_count]

    def as_column(row):
        return jnp.transpose(jnp.broadcast_to(row, (128, token_count)))[:, 0:1]

    statistic = as_column(stat_row) / (4 * width)
    inv_rms = as_column(inv_row)
    rows = hidden[...].astype(F32)
    grad_rows[...] = (
        inv_rms * gain[...].astype(F32) * normed_grad - rows * inv_rms * inv_rms * inv_rms * statistic
    ).astype(LOW)


def encoding_kernel(own, from_core, up, down, *refs):
    pieces, outs, (whole, sems) = refs[:-6], refs[-6:-2], refs[-2:]
    width = whole.shape[1] // 2
    run_copies(weight_copies(pieces, whole, 0), sems)
    own_low = own[...] + from_core[0:OWN_ROWS, :].astype(F32)
    own_low = (own_low + up[...].astype(F32) + down[...].astype(F32)).astype(LOW)
    for k, out in enumerate(outs):
        out[...] = lax.dot_general(
            own_low, whole[k * width : (k + 1) * width, :], ACROSS, preferred_element_type=F32
        ).astype(LOW)


def call(kernel, operands, specs, outs, scratch=(), copies=0):
    scratch = list(scratch)
    if copies:
        scratch.append(pltpu.SemaphoreType.DMA((copies,)))
    return pl.pallas_call(
        kernel,
        out_shape=[jax.ShapeDtypeStruct(shape, dtype) for shape, dtype in outs],
        in_specs=specs,
        out_specs=[VMEM] * len(outs),
        scratch_shapes=scratch,
        compiler_params=pltpu.CompilerParams(vmem_limit_bytes=16 * 1024 * 1024),
    )(*operands)


def shards(hidden_rows, norm_gain, encodings, w_query, w_key, w_value, w_out, neighbours, grad_out):
    seq_count = lax.axis_size("seq")
    z, y, x, c = place()
    g = 2 * x + y
    token_count, width = hidden_rows.shape
    full_width = 4 * width
    ids = neighbours.size
    wide = 2 * width

    own_enc = encodings.reshape(OWN_ROWS, width)
    weights = move(jnp.concatenate([w_key, w_value, w_query, w_out.T], axis=0), spread(0))
    enc_below, enc_above = move(own_enc, ring_up), move(own_enc, ring_down)
    extra = jnp.pad(norm_gain[None, :], ((0, EXTRA - 1), (0, 0)))
    extra = extra + jnp.pad(neighbours.reshape(1, ids).astype(LOW), ((1, EXTRA - 2), (0, width - ids)))
    packed = jnp.concatenate([hidden_rows, extra, grad_out, own_enc], axis=0)
    weights, enc_below, enc_above, packed = tie(weights, enc_below, enc_above, packed)
    tokens = [move(packed, spread(k)) for k in range(4)]
    outer = jnp.concatenate([enc_below, enc_above], axis=0)
    if seq_count == 8:
        below, above = move(weights, ring_up), move(weights, ring_down)
        outer, below, above, *tokens = tie(outer, below, above, *tokens)
        two = move(jnp.where(z % 2 == 0, below, above), lambda z, y, x, c: (z ^ 1, y, x, c))
        outers = [move(outer, spread(k)) for k in range(4)]
        two, *outers = tie(two, *outers)
        pieces = [weights, below, above, two]
        kv_pieces = qo_pieces = pieces + [move(piece, flip_core) for piece in pieces]
    else:
        kv_pieces, qo_pieces = any_weights(weights, c, g)
        outers = [move(outer, spread(k)) for k in range(4)]
    piece_count = len(kv_pieces)

    chosen = tokens[0][token_count + 1, :ids].astype(jnp.int32)
    normed, inv_rms = call(
        lambda *refs: norm_kernel(token_count, *refs),
        tokens,
        [ANY] * 4,
        [((token_count, full_width), LOW), ((token_count, 1), F32)],
        [pltpu.VMEM((4, token_count + EXTRA, width), LOW)],
        4,
    )
    tables, shared = call(
        lambda *refs: table_kernel(token_count, *refs),
        tokens + outers + kv_pieces,
        [ANY] * (8 + piece_count),
        [((3 * OWN_ROWS, wide), LOW), ((2 * OWN_ROWS, wide), LOW)],
        [pltpu.VMEM((full_width, wide), LOW), pltpu.VMEM((3 * OWN_ROWS, full_width), LOW)],
        12 + 2 * piece_count,
    )
    shared = move(shared, flip_core)
    queries, d_attended = call(
        lambda *refs: query_kernel(token_count, *refs),
        [normed] + tokens + qo_pieces,
        [ANY] * (5 + piece_count),
        [((token_count, width), LOW), ((token_count, width), LOW)],
        [pltpu.VMEM((full_width, wide), LOW)] + [pltpu.VMEM((token_count, full_width), LOW)] * 2,
        5 + 2 * piece_count,
    )
    attended, d_queries, d_own, d_outer, d_shared = call(
        lambda *refs: attention_kernel(seq_count, *refs),
        [chosen, tables, shared, queries, d_attended],
        [SMEM, ANY, ANY, VMEM, VMEM],
        [
            ((token_count, width), LOW),
            ((token_count, width), LOW),
            ((OWN_ROWS, wide), F32),
            ((2 * OWN_ROWS, wide), LOW),
            ((2 * OWN_ROWS, wide), LOW),
        ],
        [pltpu.VMEM((5 * OWN_ROWS, wide), LOW), pltpu.VMEM((5 * OWN_ROWS, wide), F32)],
        2,
    )
    from_core = move(d_shared, flip_core)
    shared_grad = from_core[OWN_ROWS:].astype(F32)
    to_below = (d_outer[:OWN_ROWS] + jnp.where(c == 1, shared_grad, 0.0)).astype(LOW)
    to_above = (d_outer[OWN_ROWS:] + jnp.where(c == 0, shared_grad, 0.0)).astype(LOW)
    terms = call(
        product_kernel,
        [attended, d_queries, inv_rms] + tokens + qo_pieces,
        [VMEM, VMEM, VMEM] + [ANY] * (4 + piece_count),
        [((2 * token_count + EXTRA, width), LOW)] * 4,
        [
            pltpu.VMEM((full_width, wide), LOW),
            pltpu.VMEM((4, token_count + EXTRA, width), LOW),
        ],
        4 + 2 * piece_count,
    )
    to_below, to_above, *terms = tie(to_below, to_above, *terms)
    up, down = move(to_above, ring_up), move(to_below, ring_down)
    terms = [move(term, gather_back(k)) for k, term in enumerate(terms)]
    branch_out, grad_rows = call(
        finish_kernel,
        [hidden_rows, norm_gain[None, :]] + terms,
        [VMEM] * 6,
        [((token_count, width), LOW), ((token_count, width), LOW)],
    )
    enc_terms = call(
        encoding_kernel,
        [d_own, from_core, up, down] + kv_pieces,
        [VMEM] * 4 + [ANY] * piece_count,
        [((OWN_ROWS, width), LOW)] * 4,
        [pltpu.VMEM((full_width, wide), LOW)],
        2 * piece_count,
    )
    enc_terms = [move(term, gather_back(k)).astype(F32) for k, term in enumerate(enc_terms)]
    grad_encodings = (enc_terms[0] + enc_terms[1] + enc_terms[2] + enc_terms[3]).astype(LOW)
    return (branch_out, grad_rows, grad_encodings.reshape(encodings.shape))


def solution(mesh):
    placed = (
        P("seq", "mp"),
        P("mp"),
        P("seq", None, "mp"),
        P("seq", "mp"),
        P("seq", "mp"),
        P("seq", "mp"),
        P("mp", "seq"),
        P("seq", None),
        P("seq", "mp"),
    )
    return jax.shard_map(
        shards,
        mesh=mesh,
        in_specs=placed,
        out_specs=(P("seq", "mp"), P("seq", "mp"), P("seq", None, "mp")),
        check_vma=False,
    )
```

```python
import jax
import jax.numpy as jnp
from jax import lax
from jax.experimental import pallas as pl
from jax.experimental.pallas import tpu as pltpu
from jax.sharding import PartitionSpec as P

HD = 128
STRETCH = 64
NBR = 2
RET = 128
OWN_DEV = 2
OWN_ROWS = OWN_DEV * RET
EXTRA = 16
LOW = jnp.bfloat16
F32 = jnp.float32
epsilon = 1e-05
ANY = pl.BlockSpec(memory_space=pl.ANY)
VMEM = pl.BlockSpec(memory_space=pltpu.VMEM)
SMEM = pl.BlockSpec(memory_space=pltpu.SMEM)
ACROSS = (((1,), (1,)), ((), ()))
DOWN = (((0,), (0,)), ((), ()))


def move(value, step):
    seq_count, mp_count = lax.axis_size("seq"), lax.axis_size("mp")
    z_count = seq_count // 2
    pairs = []
    for d in range(seq_count):
        for m in range(mp_count):
            target = step(d // 2, d % 2, m // 2, m % 2)
            if target is not None:
                z, y, x, c = target
                pairs.append((d * mp_count + m, ((z % z_count) * 2 + y) * mp_count + 2 * x + c))
    return lax.ppermute(value, ("seq", "mp"), pairs)


def spread(k):
    return lambda z, y, x, c: (z, c ^ (k % 2), x ^ (k // 2), y)


def gather_back(k):
    return lambda z, y, x, c: (z, c, x ^ (k // 2), y ^ (k % 2))


def flip_core(z, y, x, c):
    return (z, y, x, 1 - c)


def ring_up(z, y, x, c):
    return (z + 1, y, x, c)


def ring_down(z, y, x, c):
    return (z - 1, y, x, c)


def place():
    d, m = lax.axis_index("seq"), lax.axis_index("mp")
    return d // 2, d % 2, m // 2, m % 2


def tie(*values):
    return lax.optimization_barrier(values)


def any_weights(own, c, g):
    seq_count = lax.axis_size("seq")
    z_count = seq_count // 2
    rows, width = own.shape[0] // 4, own.shape[1]
    groups = [[2 * i + j for i in range(z_count)] for j in range(2)]
    mine = lax.all_gather(own, "seq", axis=0, axis_index_groups=groups)
    theirs = move(mine, flip_core)
    both = jnp.stack([jnp.where(c == 0, mine, theirs), jnp.where(c == 0, theirs, mine)], axis=1)
    both = jnp.moveaxis(both.reshape(seq_count, 4, rows, width), 1, 0)
    both = both.reshape(4, 4, seq_count * rows // 4, width)
    both = jnp.take(both, g ^ jnp.arange(4), axis=1).reshape(4, seq_count * rows, width)
    return [jnp.concatenate([both[0], both[1]], axis=1)], [jnp.concatenate([both[2], both[3]], axis=1)]


def run_copies(pairs, sems):
    copies = [pltpu.make_async_copy(a, b, sems.at[i]) for i, (a, b) in enumerate(pairs)]
    for copy in copies:
        copy.start()
    for copy in copies:
        copy.wait()


def weight_copies(pieces, whole, first):
    if len(pieces) == 1:
        return [(pieces[0], whole)]
    z, y, x, c = place()
    g = 2 * x + y
    rows, width = pieces[0].shape[0] // 4, pieces[0].shape[1]
    pairs = []
    for side in range(2):
        side_c = c if side == 0 else 1 - c
        for step, ref in zip((0, 3, 1, 2), pieces[4 * side : 4 * side + 4]):
            start = pl.multiple_of((((z + step) % 4 ^ g) * 2 + side_c) * rows, 64)
            for j in range(2):
                pairs.append(
                    (
                        ref.at[pl.ds((first + j) * rows, rows)],
                        whole.at[pl.ds(start, rows), pl.ds(j * width, width)],
                    )
                )
    return pairs


def norm_kernel(token_count, *refs):
    token_refs, normed, inv_out, rows_in, sems = refs[:4], *refs[4:]
    width = token_refs[0].shape[1]
    run_copies(
        [(ref.at[pl.ds(0, token_count + EXTRA)], rows_in.at[k]) for k, ref in enumerate(token_refs)],
        sems,
    )
    total = None
    for k in range(4):
        rows = rows_in[k, 0:token_count, :].astype(F32)
        part = jnp.sum(rows * rows, axis=1, keepdims=True)
        total = part if total is None else total + part
    inv_rms = lax.rsqrt(total / (4 * width) + epsilon)
    inv_out[...] = inv_rms
    for k in range(4):
        rows = rows_in[k, 0:token_count, :].astype(F32)
        gain = rows_in[k, token_count : token_count + 1, :].astype(F32)
        normed[:, k * width : (k + 1) * width] = (rows * inv_rms * gain).astype(LOW)


def table_kernel(token_count, *refs):
    token_refs, outer_refs = refs[:4], refs[4:8]
    pieces, (tables, shared, whole, encs, sems) = refs[8:-5], refs[-5:]
    width = token_refs[0].shape[1]
    pairs = weight_copies(pieces, whole, 0)
    for k in range(4):
        block = pl.ds(k * width, width)
        for i, (ref, start) in enumerate(
            ((outer_refs[k], 0), (token_refs[k], 2 * token_count + EXTRA), (outer_refs[k], OWN_ROWS))
        ):
            pairs.append((ref.at[pl.ds(start, OWN_ROWS)], encs.at[pl.ds(i * OWN_ROWS, OWN_ROWS), block]))
    run_copies(pairs, sems)
    tables[...] = jnp.dot(encs[...], whole[...], preferred_element_type=F32).astype(LOW)
    shared[0:OWN_ROWS, :] = tables[OWN_ROWS : 2 * OWN_ROWS, :]
    z, y, x, c = place()
    start = pl.multiple_of(jnp.where(c == 1, 0, 2 * OWN_ROWS), OWN_ROWS)
    shared[OWN_ROWS : 2 * OWN_ROWS, :] = tables[pl.ds(start, OWN_ROWS), :]


def query_kernel(token_count, *refs):
    normed, token_refs = refs[0], refs[1:5]
    pieces, (queries, d_attended, whole, rows_in, grads, sems) = refs[5:-6], refs[-6:]
    width = token_refs[0].shape[1]
    pairs = weight_copies(pieces, whole, 2) + [(normed, rows_in)]
    for k, ref in enumerate(token_refs):
        pairs.append(
            (ref.at[pl.ds(token_count + EXTRA, token_count)], grads.at[:, pl.ds(k * width, width)])
        )
    run_copies(pairs, sems)
    queries[...] = jnp.dot(rows_in[...], whole[:, 0:width], preferred_element_type=F32).astype(LOW)
    d_attended[...] = jnp.dot(grads[...], whole[:, width:], preferred_element_type=F32).astype(LOW)


def attention_kernel(seq_count, *refs):
    chosen, tables, shared, queries, d_attended = refs[:5]
    attended, d_queries, d_own, d_outer, d_shared, window, d_window, sems = refs[5:]
    token_count, width = queries.shape
    run_copies(
        [
            (tables, window.at[pl.ds(0, 3 * OWN_ROWS)]),
            (shared, window.at[pl.ds(3 * OWN_ROWS, 2 * OWN_ROWS)]),
        ],
        sems,
    )
    d_window[...] = jnp.zeros_like(d_window)
    scale = HD ** (-0.5)
    z, y, x, c = place()
    t = 2 * z + c
    for s in range(token_count // STRETCH):
        starts = []
        for j in range(NBR):
            name = chosen[s * NBR + j]
            away = (name // OWN_DEV - t + 2 + seq_count) % seq_count
            odd = 3 + jnp.where(away == 1, 1 - c, c)
            index = jnp.where(away % 2 == 0, away // 2, odd)
            starts.append(pl.multiple_of(index * OWN_ROWS + (name % OWN_DEV) * RET, RET))
        tokens = slice(s * STRETCH, (s + 1) * STRETCH)
        for h in range(width // HD):
            left = slice(h * HD, (h + 1) * HD)
            right = slice(width + h * HD, width + (h + 1) * HD)
            keys = jnp.concatenate([window[pl.ds(a, RET), left] for a in starts], axis=0)
            values = jnp.concatenate([window[pl.ds(a, RET), right] for a in starts], axis=0)
            query = queries[tokens, left]
            d_att = d_attended[tokens, left]
            scores = lax.dot_general(query, keys, ACROSS, preferred_element_type=F32) * scale
            exponent = jnp.exp(scores - jnp.max(scores, axis=1, keepdims=True))
            weights = exponent / jnp.sum(exponent, axis=1, keepdims=True)
            weights_low = weights.astype(LOW)
            attended[tokens, left] = jnp.dot(
                weights_low, values, preferred_element_type=F32
            ).astype(LOW)
            d_weights = lax.dot_general(d_att, values, ACROSS, preferred_element_type=F32)
            inner = jnp.sum(d_weights * weights, axis=1, keepdims=True)
            d_scores = (weights * (d_weights - inner) * scale).astype(LOW)
            d_queries[tokens, left] = jnp.dot(d_scores, keys, preferred_element_type=F32).astype(LOW)
            d_keys = lax.dot_general(d_scores, query, DOWN, preferred_element_type=F32)
            d_values = lax.dot_general(weights_low, d_att, DOWN, preferred_element_type=F32)
            for j, a in enumerate(starts):
                d_window[pl.ds(a, RET), left] += d_keys[j * RET : (j + 1) * RET, :]
                d_window[pl.ds(a, RET), right] += d_values[j * RET : (j + 1) * RET, :]
    d_own[...] = d_window[OWN_ROWS : 2 * OWN_ROWS, :]
    d_outer[0:OWN_ROWS, :] = d_window[0:OWN_ROWS, :].astype(LOW)
    d_outer[OWN_ROWS : 2 * OWN_ROWS, :] = d_window[2 * OWN_ROWS : 3 * OWN_ROWS, :].astype(LOW)
    d_shared[...] = d_window[3 * OWN_ROWS : 5 * OWN_ROWS, :].astype(LOW)


def as_row(column):
    return jnp.transpose(jnp.broadcast_to(column, (column.shape[0], 128)))[0:1, :]


def product_kernel(*refs):
    attended, d_queries, inv_rms = refs[:3]
    token_refs, pieces, outs, (whole, rows_in, sems) = refs[3:7], refs[7:-7], refs[-7:-3], refs[-3:]
    token_count, width = attended.shape
    pairs = weight_copies(pieces, whole, 2)
    for k, ref in enumerate(token_refs):
        pairs.append((ref.at[pl.ds(0, token_count + EXTRA)], rows_in.at[k]))
    run_copies(pairs, sems)
    total = None
    for k, out in enumerate(outs):
        block = slice(k * width, (k + 1) * width)
        out[0:token_count, :] = lax.dot_general(
            attended[...], whole[block, width:], ACROSS, preferred_element_type=F32
        ).astype(LOW)
        back = lax.dot_general(
            d_queries[...], whole[block, 0:width], ACROSS, preferred_element_type=F32
        ).astype(LOW)
        out[token_count : 2 * token_count, :] = back
        rows = rows_in[k, 0:token_count, :].astype(F32)
        gain = rows_in[k, token_count : token_count + 1, :].astype(F32)
        part = jnp.sum(rows * gain * back.astype(F32), axis=1, keepdims=True)
        total = part if total is None else total + part
    lines = []
    for column in (total, inv_rms[...]):
        line = as_row(column)
        high = line.astype(LOW).astype(F32)
        lines += [high, line - high]
    lines.append(jnp.zeros((EXTRA - 4, token_count), F32))
    extra = jnp.concatenate(lines, axis=0)
    extra = jnp.concatenate([extra, jnp.zeros((EXTRA, width - token_count), F32)], axis=1).astype(LOW)
    for out in outs:
        out[2 * token_count : 2 * token_count + EXTRA, :] = extra


def finish_kernel(hidden, gain, *refs):
    terms, (branch_out, grad_rows) = refs[:4], refs[4:]
    token_count, width = hidden.shape
    branch, normed_grad, extra = None, None, None
    for k, term in enumerate(terms):
        out = term[0:token_count, :].astype(F32)
        back = term[token_count : 2 * token_count, :].astype(F32)
        lines = term[2 * token_count : 2 * token_count + EXTRA, :].astype(F32)
        branch = out if k == 0 else branch + out
        normed_grad = back if k == 0 else normed_grad + back
        extra = lines if k == 0 else extra + lines
        if k == 0:
            inv_row = lines[2:3, 0:token_count] + lines[3:4, 0:token_count]
    branch_out[...] = branch.astype(LOW)
    stat_row = extra[0:1, 0:token_count] + extra[1:2, 0:token_count]

    def as_column(row):
        return jnp.transpose(jnp.broadcast_to(row, (128, token_count)))[:, 0:1]

    statistic = as_column(stat_row) / (4 * width)
    inv_rms = as_column(inv_row)
    rows = hidden[...].astype(F32)
    grad_rows[...] = (
        inv_rms * gain[...].astype(F32) * normed_grad - rows * inv_rms * inv_rms * inv_rms * statistic
    ).astype(LOW)


def encoding_kernel(own, from_core, up, down, *refs):
    pieces, outs, (whole, sems) = refs[:-6], refs[-6:-2], refs[-2:]
    width = whole.shape[1] // 2
    run_copies(weight_copies(pieces, whole, 0), sems)
    own_low = own[...] + from_core[0:OWN_ROWS, :].astype(F32)
    own_low = (own_low + up[...].astype(F32) + down[...].astype(F32)).astype(LOW)
    for k, out in enumerate(outs):
        out[...] = lax.dot_general(
            own_low, whole[k * width : (k + 1) * width, :], ACROSS, preferred_element_type=F32
        ).astype(LOW)


def call(kernel, operands, specs, outs, scratch=(), copies=0):
    scratch = list(scratch)
    if copies:
        scratch.append(pltpu.SemaphoreType.DMA((copies,)))
    return pl.pallas_call(
        kernel,
        out_shape=[jax.ShapeDtypeStruct(shape, dtype) for shape, dtype in outs],
        in_specs=specs,
        out_specs=[VMEM] * len(outs),
        scratch_shapes=scratch,
        compiler_params=pltpu.CompilerParams(vmem_limit_bytes=16 * 1024 * 1024),
    )(*operands)


def shards(hidden_rows, norm_gain, encodings, w_query, w_key, w_value, w_out, neighbours, grad_out):
    seq_count = lax.axis_size("seq")
    z, y, x, c = place()
    g = 2 * x + y
    token_count, width = hidden_rows.shape
    full_width = 4 * width
    ids = neighbours.size
    wide = 2 * width

    own_enc = encodings.reshape(OWN_ROWS, width)
    weights = move(jnp.concatenate([w_key, w_value, w_query, w_out.T], axis=0), spread(0))
    enc_below, enc_above = move(own_enc, ring_up), move(own_enc, ring_down)
    extra = jnp.pad(norm_gain[None, :], ((0, EXTRA - 1), (0, 0)))
    extra = extra + jnp.pad(neighbours.reshape(1, ids).astype(LOW), ((1, EXTRA - 2), (0, width - ids)))
    packed = jnp.concatenate([hidden_rows, extra, grad_out, own_enc], axis=0)
    weights, enc_below, enc_above, packed = tie(weights, enc_below, enc_above, packed)
    tokens = [move(packed, spread(k)) for k in range(4)]
    outer = jnp.concatenate([enc_below, enc_above], axis=0)
    if seq_count == 8:
        below, above = move(weights, ring_up), move(weights, ring_down)
        outer, below, above, *tokens = tie(outer, below, above, *tokens)
        two = move(jnp.where(z % 2 == 0, below, above), lambda z, y, x, c: (z ^ 1, y, x, c))
        outers = [move(outer, spread(k)) for k in range(4)]
        two, *outers = tie(two, *outers)
        pieces = [weights, below, above, two]
        kv_pieces = qo_pieces = pieces + [move(piece, flip_core) for piece in pieces]
    else:
        kv_pieces, qo_pieces = any_weights(weights, c, g)
        outers = [move(outer, spread(k)) for k in range(4)]
    piece_count = len(kv_pieces)

    chosen = tokens[0][token_count + 1, :ids].astype(jnp.int32)
    normed, inv_rms = call(
        lambda *refs: norm_kernel(token_count, *refs),
        tokens,
        [ANY] * 4,
        [((token_count, full_width), LOW), ((token_count, 1), F32)],
        [pltpu.VMEM((4, token_count + EXTRA, width), LOW)],
        4,
    )
    tables, shared = call(
        lambda *refs: table_kernel(token_count, *refs),
        tokens + outers + kv_pieces,
        [ANY] * (8 + piece_count),
        [((3 * OWN_ROWS, wide), LOW), ((2 * OWN_ROWS, wide), LOW)],
        [pltpu.VMEM((full_width, wide), LOW), pltpu.VMEM((3 * OWN_ROWS, full_width), LOW)],
        12 + 2 * piece_count,
    )
    shared = move(shared, flip_core)
    queries, d_attended = call(
        lambda *refs: query_kernel(token_count, *refs),
        [normed] + tokens + qo_pieces,
        [ANY] * (5 + piece_count),
        [((token_count, width), LOW), ((token_count, width), LOW)],
        [pltpu.VMEM((full_width, wide), LOW)] + [pltpu.VMEM((token_count, full_width), LOW)] * 2,
        5 + 2 * piece_count,
    )
    attended, d_queries, d_own, d_outer, d_shared = call(
        lambda *refs: attention_kernel(seq_count, *refs),
        [chosen, tables, shared, queries, d_attended],
        [SMEM, ANY, ANY, VMEM, VMEM],
        [
            ((token_count, width), LOW),
            ((token_count, width), LOW),
            ((OWN_ROWS, wide), F32),
            ((2 * OWN_ROWS, wide), LOW),
            ((2 * OWN_ROWS, wide), LOW),
        ],
        [pltpu.VMEM((5 * OWN_ROWS, wide), LOW), pltpu.VMEM((5 * OWN_ROWS, wide), F32)],
        2,
    )
    from_core = move(d_shared, flip_core)
    shared_grad = from_core[OWN_ROWS:].astype(F32)
    to_below = (d_outer[:OWN_ROWS] + jnp.where(c == 1, shared_grad, 0.0)).astype(LOW)
    to_above = (d_outer[OWN_ROWS:] + jnp.where(c == 0, shared_grad, 0.0)).astype(LOW)
    terms = call(
        product_kernel,
        [attended, d_queries, inv_rms] + [pltpu.with_memory_space_constraint(o, pltpu.HBM) for o in tokens + qo_pieces],
        [VMEM, VMEM, VMEM] + [ANY] * (4 + piece_count),
        [((2 * token_count + EXTRA, width), LOW)] * 4,
        [
            pltpu.VMEM((full_width, wide), LOW),
            pltpu.VMEM((4, token_count + EXTRA, width), LOW),
        ],
        4 + 2 * piece_count,
    )
    to_below, to_above, *terms = tie(to_below, to_above, *terms)
    up, down = move(to_above, ring_up), move(to_below, ring_down)
    terms = [move(term, gather_back(k)) for k, term in enumerate(terms)]
    branch_out, grad_rows = call(
        finish_kernel,
        [hidden_rows, norm_gain[None, :]] + terms,
        [VMEM] * 6,
        [((token_count, width), LOW), ((token_count, width), LOW)],
    )
    enc_terms = call(
        encoding_kernel,
        [d_own, from_core, up, down] + [pltpu.with_memory_space_constraint(o, pltpu.HBM) for o in kv_pieces],
        [VMEM] * 4 + [ANY] * piece_count,
        [((OWN_ROWS, width), LOW)] * 4,
        [pltpu.VMEM((full_width, wide), LOW)],
        2 * piece_count,
    )
    enc_terms = [move(term, gather_back(k)).astype(F32) for k, term in enumerate(enc_terms)]
    grad_encodings = (enc_terms[0] + enc_terms[1] + enc_terms[2] + enc_terms[3]).astype(LOW)
    return (branch_out, grad_rows, grad_encodings.reshape(encodings.shape))


def solution(mesh):
    placed = (
        P("seq", "mp"),
        P("mp"),
        P("seq", None, "mp"),
        P("seq", "mp"),
        P("seq", "mp"),
        P("seq", "mp"),
        P("mp", "seq"),
        P("seq", None),
        P("seq", "mp"),
    )
    return jax.shard_map(
        shards,
        mesh=mesh,
        in_specs=placed,
        out_specs=(P("seq", "mp"), P("seq", "mp"), P("seq", None, "mp")),
        check_vma=False,
    )
```

```python
import jax
import jax.numpy as jnp
from jax import lax
from jax.experimental import pallas as pl
from jax.experimental.pallas import tpu as pltpu
from jax.sharding import PartitionSpec as P

HD = 128
STRETCH = 64
NBR = 2
RET = 128
OWN_DEV = 2
OWN_ROWS = OWN_DEV * RET
EXTRA = 16
LOW = jnp.bfloat16
F32 = jnp.float32
epsilon = 1e-05
ANY = pl.BlockSpec(memory_space=pl.ANY)
VMEM = pl.BlockSpec(memory_space=pltpu.VMEM)
SMEM = pl.BlockSpec(memory_space=pltpu.SMEM)
ACROSS = (((1,), (1,)), ((), ()))
DOWN = (((0,), (0,)), ((), ()))


def move(value, step):
    seq_count, mp_count = lax.axis_size("seq"), lax.axis_size("mp")
    z_count = seq_count // 2
    pairs = []
    for d in range(seq_count):
        for m in range(mp_count):
            target = step(d // 2, d % 2, m // 2, m % 2)
            if target is not None:
                z, y, x, c = target
                pairs.append((d * mp_count + m, ((z % z_count) * 2 + y) * mp_count + 2 * x + c))
    return lax.ppermute(value, ("seq", "mp"), pairs)


def spread(k):
    return lambda z, y, x, c: (z, c ^ (k % 2), x ^ (k // 2), y)


def gather_back(k):
    return lambda z, y, x, c: (z, c, x ^ (k // 2), y ^ (k % 2))


def flip_core(z, y, x, c):
    return (z, y, x, 1 - c)


def ring_up(z, y, x, c):
    return (z + 1, y, x, c)


def ring_down(z, y, x, c):
    return (z - 1, y, x, c)


def place():
    d, m = lax.axis_index("seq"), lax.axis_index("mp")
    return d // 2, d % 2, m // 2, m % 2


def in_hbm(value):
    return pltpu.with_memory_space_constraint(value, pltpu.HBM)


def tie(*values):
    return lax.optimization_barrier(values)


def any_weights(own, c, g):
    seq_count = lax.axis_size("seq")
    z_count = seq_count // 2
    rows, width = own.shape[0] // 4, own.shape[1]
    groups = [[2 * i + j for i in range(z_count)] for j in range(2)]
    mine = lax.all_gather(own, "seq", axis=0, axis_index_groups=groups)
    theirs = move(mine, flip_core)
    both = jnp.stack([jnp.where(c == 0, mine, theirs), jnp.where(c == 0, theirs, mine)], axis=1)
    both = jnp.moveaxis(both.reshape(seq_count, 4, rows, width), 1, 0)
    both = both.reshape(4, 4, seq_count * rows // 4, width)
    both = jnp.take(both, g ^ jnp.arange(4), axis=1).reshape(4, seq_count * rows, width)
    return [jnp.concatenate([both[0], both[1]], axis=1)], [jnp.concatenate([both[2], both[3]], axis=1)]


def run_copies(pairs, sems):
    copies = [pltpu.make_async_copy(a, b, sems.at[i]) for i, (a, b) in enumerate(pairs)]
    for copy in copies:
        copy.start()
    for copy in copies:
        copy.wait()


def weight_copies(pieces, whole, first):
    if len(pieces) == 1:
        return [(pieces[0], whole)]
    z, y, x, c = place()
    g = 2 * x + y
    rows, width = pieces[0].shape[0] // 4, pieces[0].shape[1]
    pairs = []
    for side in range(2):
        side_c = c if side == 0 else 1 - c
        for step, ref in zip((0, 3, 1, 2), pieces[4 * side : 4 * side + 4]):
            start = pl.multiple_of((((z + step) % 4 ^ g) * 2 + side_c) * rows, 64)
            for j in range(2):
                pairs.append(
                    (
                        ref.at[pl.ds((first + j) * rows, rows)],
                        whole.at[pl.ds(start, rows), pl.ds(j * width, width)],
                    )
                )
    return pairs


def block(refs, k, start, rows):
    if len(refs) == 4:
        return refs[k].at[pl.ds(start, rows)]
    ref = refs[k // 2]
    return ref.at[pl.ds((k % 2) * (ref.shape[0] // 2) + start, rows)]


def whole_kernel(*refs):
    pieces, (whole, sems) = refs[:-2], refs[-2:]
    run_copies(weight_copies(pieces, whole, 0), sems)


def norm_kernel(token_count, *refs):
    tokens, (normed, inv_out, rows_in, sems) = refs[:4], refs[4:]
    width = tokens[0].shape[1]
    run_copies(
        [(block(tokens, k, 0, token_count + EXTRA), rows_in.at[k]) for k in range(4)],
        sems,
    )
    total = None
    for k in range(4):
        rows = rows_in[k, 0:token_count, :].astype(F32)
        part = jnp.sum(rows * rows, axis=1, keepdims=True)
        total = part if total is None else total + part
    inv_rms = lax.rsqrt(total / (4 * width) + epsilon)
    inv_out[...] = inv_rms
    for k in range(4):
        rows = rows_in[k, 0:token_count, :].astype(F32)
        gain = rows_in[k, token_count : token_count + 1, :].astype(F32)
        normed[:, k * width : (k + 1) * width] = (rows * inv_rms * gain).astype(LOW)


def table_kernel(token_count, *refs):
    tokens, outers = refs[:4], refs[4:6]
    pieces, (tables, shared, whole, encs, sems) = refs[6:-5], refs[-5:]
    width = tokens[0].shape[1]
    pairs = weight_copies(pieces, whole, 0)
    sources = ((outers, 0), (tokens, 2 * token_count + EXTRA), (outers, OWN_ROWS))
    for i, (pair, start) in enumerate(sources):
        for k in range(4):
            target = encs.at[pl.ds(i * OWN_ROWS, OWN_ROWS), pl.ds(k * width, width)]
            pairs.append((block(pair, k, start, OWN_ROWS), target))
    run_copies(pairs, sems)
    tables[...] = jnp.dot(encs[...], whole[...], preferred_element_type=F32).astype(LOW)
    shared[0:OWN_ROWS, :] = tables[OWN_ROWS : 2 * OWN_ROWS, :]
    z, y, x, c = place()
    start = pl.multiple_of(jnp.where(c == 1, 0, 2 * OWN_ROWS), OWN_ROWS)
    shared[OWN_ROWS : 2 * OWN_ROWS, :] = tables[pl.ds(start, OWN_ROWS), :]


def query_kernel(token_count, *refs):
    normed, tokens = refs[0], refs[1:5]
    pieces, (queries, d_attended, whole, rows_in, grads, sems) = refs[5:-6], refs[-6:]
    width = tokens[0].shape[1]
    pairs = weight_copies(pieces, whole, 2) + [(normed, rows_in)]
    for k in range(4):
        source = block(tokens, k, token_count + EXTRA, token_count)
        pairs.append((source, grads.at[:, pl.ds(k * width, width)]))
    run_copies(pairs, sems)
    queries[...] = jnp.dot(rows_in[...], whole[:, 0:width], preferred_element_type=F32).astype(LOW)
    d_attended[...] = jnp.dot(grads[...], whole[:, width:], preferred_element_type=F32).astype(LOW)


def attention_kernel(seq_count, *refs):
    chosen, tables, shared, queries, d_attended = refs[:5]
    attended, d_queries, d_own, d_outer, d_shared, window, d_window, sems = refs[5:]
    token_count, width = queries.shape
    run_copies(
        [
            (tables, window.at[pl.ds(0, 3 * OWN_ROWS)]),
            (shared, window.at[pl.ds(3 * OWN_ROWS, 2 * OWN_ROWS)]),
        ],
        sems,
    )
    d_window[...] = jnp.zeros_like(d_window)
    scale = HD ** (-0.5)
    z, y, x, c = place()
    t = 2 * z + c
    for s in range(token_count // STRETCH):
        starts = []
        for j in range(NBR):
            name = chosen[s * NBR + j]
            away = (name // OWN_DEV - t + 2 + seq_count) % seq_count
            odd = 3 + jnp.where(away == 1, 1 - c, c)
            index = jnp.where(away % 2 == 0, away // 2, odd)
            starts.append(pl.multiple_of(index * OWN_ROWS + (name % OWN_DEV) * RET, RET))
        tokens = slice(s * STRETCH, (s + 1) * STRETCH)
        for h in range(width // HD):
            left = slice(h * HD, (h + 1) * HD)
            right = slice(width + h * HD, width + (h + 1) * HD)
            keys = jnp.concatenate([window[pl.ds(a, RET), left] for a in starts], axis=0)
            values = jnp.concatenate([window[pl.ds(a, RET), right] for a in starts], axis=0)
            query = queries[tokens, left]
            d_att = d_attended[tokens, left]
            scores = lax.dot_general(query, keys, ACROSS, preferred_element_type=F32) * scale
            exponent = jnp.exp(scores - jnp.max(scores, axis=1, keepdims=True))
            weights = exponent / jnp.sum(exponent, axis=1, keepdims=True)
            weights_low = weights.astype(LOW)
            attended[tokens, left] = jnp.dot(
                weights_low, values, preferred_element_type=F32
            ).astype(LOW)
            d_weights = lax.dot_general(d_att, values, ACROSS, preferred_element_type=F32)
            inner = jnp.sum(d_weights * weights, axis=1, keepdims=True)
            d_scores = (weights * (d_weights - inner) * scale).astype(LOW)
            d_queries[tokens, left] = jnp.dot(d_scores, keys, preferred_element_type=F32).astype(LOW)
            d_keys = lax.dot_general(d_scores, query, DOWN, preferred_element_type=F32)
            d_values = lax.dot_general(weights_low, d_att, DOWN, preferred_element_type=F32)
            for j, a in enumerate(starts):
                d_window[pl.ds(a, RET), left] += d_keys[j * RET : (j + 1) * RET, :]
                d_window[pl.ds(a, RET), right] += d_values[j * RET : (j + 1) * RET, :]
    d_own[...] = d_window[OWN_ROWS : 2 * OWN_ROWS, :]
    d_outer[0:OWN_ROWS, :] = d_window[0:OWN_ROWS, :].astype(LOW)
    d_outer[OWN_ROWS : 2 * OWN_ROWS, :] = d_window[2 * OWN_ROWS : 3 * OWN_ROWS, :].astype(LOW)
    d_shared[...] = d_window[3 * OWN_ROWS : 5 * OWN_ROWS, :].astype(LOW)


def as_row(column):
    return jnp.transpose(jnp.broadcast_to(column, (column.shape[0], 128)))[0:1, :]


def product_kernel(*refs):
    attended, d_queries, inv_rms, tokens = refs[0], refs[1], refs[2], refs[3:7]
    pieces, outs, (whole, rows_in, sems) = refs[7:-7], refs[-7:-3], refs[-3:]
    token_count, width = attended.shape
    term_rows = 2 * token_count + EXTRA
    pairs = weight_copies(pieces, whole, 2)
    for k in range(4):
        pairs.append((block(tokens, k, 0, token_count + EXTRA), rows_in.at[k]))
    run_copies(pairs, sems)
    total = None
    for k in range(4):
        columns = slice(k * width, (k + 1) * width)
        outs[k][0:token_count, :] = lax.dot_general(
            attended[...], whole[columns, width:], ACROSS, preferred_element_type=F32
        ).astype(LOW)
        back = lax.dot_general(
            d_queries[...], whole[columns, 0:width], ACROSS, preferred_element_type=F32
        ).astype(LOW)
        outs[k][token_count : 2 * token_count, :] = back
        rows = rows_in[k, 0:token_count, :].astype(F32)
        gain = rows_in[k, token_count : token_count + 1, :].astype(F32)
        part = jnp.sum(rows * gain * back.astype(F32), axis=1, keepdims=True)
        total = part if total is None else total + part
    lines = []
    for column in (total, inv_rms[...]):
        line = as_row(column)
        high = line.astype(LOW).astype(F32)
        lines += [high, line - high]
    lines.append(jnp.zeros((EXTRA - 4, token_count), F32))
    extra = jnp.concatenate(lines, axis=0)
    extra = jnp.concatenate([extra, jnp.zeros((EXTRA, width - token_count), F32)], axis=1).astype(LOW)
    for out in outs:
        out[term_rows - EXTRA : term_rows, :] = extra


def finish_kernel(hidden, gain, *refs):
    terms, (branch_out, grad_rows) = refs[:4], refs[4:]
    token_count, width = hidden.shape
    branch, normed_grad, extra = None, None, None
    for k, term in enumerate(terms):
        out = term[0:token_count, :].astype(F32)
        back = term[token_count : 2 * token_count, :].astype(F32)
        lines = term[2 * token_count : 2 * token_count + EXTRA, :].astype(F32)
        branch = out if k == 0 else branch + out
        normed_grad = back if k == 0 else normed_grad + back
        extra = lines if k == 0 else extra + lines
        if k == 0:
            inv_row = lines[2:3, 0:token_count] + lines[3:4, 0:token_count]
    branch_out[...] = branch.astype(LOW)
    stat_row = extra[0:1, 0:token_count] + extra[1:2, 0:token_count]

    def as_column(row):
        return jnp.transpose(jnp.broadcast_to(row, (128, token_count)))[:, 0:1]

    statistic = as_column(stat_row) / (4 * width)
    inv_rms = as_column(inv_row)
    rows = hidden[...].astype(F32)
    grad_rows[...] = (
        inv_rms * gain[...].astype(F32)[None, :] * normed_grad - rows * inv_rms * inv_rms * inv_rms * statistic
    ).astype(LOW)


def encoding_kernel(own, from_core, up, down, whole, *outs):
    width = whole.shape[1] // 2
    own_low = own[...] + from_core[0:OWN_ROWS, :].astype(F32)
    own_low = (own_low + up[...].astype(F32) + down[...].astype(F32)).astype(LOW)
    for k, out in enumerate(outs):
        out[...] = lax.dot_general(
            own_low, whole[k * width : (k + 1) * width, :], ACROSS, preferred_element_type=F32
        ).astype(LOW)


def call(kernel, operands, specs, outs, scratch=(), copies=0, out_specs=None):
    scratch = list(scratch)
    if copies:
        scratch.append(pltpu.SemaphoreType.DMA((copies,)))
    return pl.pallas_call(
        kernel,
        out_shape=[jax.ShapeDtypeStruct(shape, dtype) for shape, dtype in outs],
        in_specs=specs,
        out_specs=out_specs or [VMEM] * len(outs),
        scratch_shapes=scratch,
        compiler_params=pltpu.CompilerParams(vmem_limit_bytes=16 * 1024 * 1024),
    )(*operands)


def shards(hidden_rows, norm_gain, encodings, w_query, w_key, w_value, w_out, neighbours, grad_out):
    seq_count = lax.axis_size("seq")
    z, y, x, c = place()
    g = 2 * x + y
    token_count, width = hidden_rows.shape
    full_width = 4 * width
    ids = neighbours.size
    wide = 2 * width

    own_enc = encodings.reshape(OWN_ROWS, width)
    weights = move(jnp.concatenate([w_key, w_value, w_query, w_out.T], axis=0), spread(0))
    enc_below, enc_above = move(own_enc, ring_up), move(own_enc, ring_down)
    id_row = jnp.pad(neighbours.reshape(1, ids).astype(LOW), ((1, EXTRA - 2), (0, width - ids)))
    extra = jnp.pad(norm_gain[None, :], ((0, EXTRA - 1), (0, 0))) + id_row
    packed = jnp.concatenate([hidden_rows, extra, grad_out, own_enc], axis=0)
    weights, enc_below, enc_above, packed = tie(weights, enc_below, enc_above, packed)
    tokens = [move(packed, spread(k)) for k in range(4)]
    outer = jnp.concatenate(
        [enc_below, enc_above, move(enc_below, flip_core), move(enc_above, flip_core)], axis=0
    )
    if seq_count == 8:
        below, above = move(weights, ring_up), move(weights, ring_down)
        below, above, *tokens = tie(below, above, *tokens)
    outers = [move(outer, spread(0)), move(outer, spread(2))]
    normed, inv_rms = call(
        lambda *refs: norm_kernel(token_count, *refs),
        tokens,
        [ANY] * 4,
        [((token_count, full_width), LOW), ((token_count, 1), F32)],
        [pltpu.VMEM((4, token_count + EXTRA, width), LOW)],
        4,
    )
    if seq_count == 8:
        two = move(jnp.where(z % 2 == 0, below, above), lambda z, y, x, c: (z ^ 1, y, x, c))
        pieces = [weights, below, above, two]
        others = [move(piece, flip_core) for piece in pieces[:3]]
        two, normed, *outers = tie(two, normed, *outers)
        kv_pieces = qo_pieces = pieces[:3] + [two] + others + [move(two, flip_core)]
    else:
        kv_pieces, qo_pieces = any_weights(weights, c, g)
    piece_count = len(kv_pieces)

    chosen = tokens[0][token_count + 1, :ids].astype(jnp.int32)
    tables, shared = call(
        lambda *refs: table_kernel(token_count, *refs),
        tokens + outers + kv_pieces,
        [ANY] * (6 + piece_count),
        [((3 * OWN_ROWS, wide), LOW), ((2 * OWN_ROWS, wide), LOW)],
        [pltpu.VMEM((full_width, wide), LOW), pltpu.VMEM((3 * OWN_ROWS, full_width), LOW)],
        12 + 2 * piece_count,
    )
    shared = move(shared, flip_core)
    queries, d_attended = call(
        lambda *refs: query_kernel(token_count, *refs),
        [normed] + tokens + qo_pieces,
        [ANY] * (5 + piece_count),
        [((token_count, width), LOW), ((token_count, width), LOW)],
        [pltpu.VMEM((full_width, wide), LOW)] + [pltpu.VMEM((token_count, full_width), LOW)] * 2,
        5 + 2 * piece_count,
    )
    attended, d_queries, d_own, d_outer, d_shared = call(
        lambda *refs: attention_kernel(seq_count, *refs),
        [chosen, tables, shared, queries, d_attended],
        [SMEM, ANY, ANY, VMEM, VMEM],
        [
            ((token_count, width), LOW),
            ((token_count, width), LOW),
            ((OWN_ROWS, wide), F32),
            ((2 * OWN_ROWS, wide), LOW),
            ((2 * OWN_ROWS, wide), LOW),
        ],
        [pltpu.VMEM((5 * OWN_ROWS, wide), LOW), pltpu.VMEM((5 * OWN_ROWS, wide), F32)],
        2,
    )
    from_core = move(d_shared, flip_core)
    shared_grad = from_core[OWN_ROWS:].astype(F32)
    to_below = (d_outer[:OWN_ROWS] + jnp.where(c == 1, shared_grad, 0.0)).astype(LOW)
    to_above = (d_outer[OWN_ROWS:] + jnp.where(c == 0, shared_grad, 0.0)).astype(LOW)
    terms = call(
        product_kernel,
        [attended, d_queries, inv_rms] + [in_hbm(o) for o in tokens + qo_pieces],
        [VMEM, VMEM, VMEM] + [ANY] * (4 + piece_count),
        [((2 * token_count + EXTRA, width), LOW)] * 4,
        [
            pltpu.VMEM((full_width, wide), LOW),
            pltpu.VMEM((4, token_count + EXTRA, width), LOW),
        ],
        4 + 2 * piece_count,
    )
    to_below, to_above, *terms = tie(to_below, to_above, *terms)
    up, down = move(to_above, ring_up), move(to_below, ring_down)
    terms = [move(term, gather_back(k)) for k, term in enumerate(terms)]
    branch_out, grad_rows = call(
        finish_kernel,
        [hidden_rows, norm_gain] + terms,
        [VMEM] * 6,
        [((token_count, width), LOW), ((token_count, width), LOW)],
    )
    (whole,) = call(
        whole_kernel,
        [in_hbm(piece) for piece in kv_pieces],
        [ANY] * piece_count,
        [((full_width, wide), LOW)],
        copies=2 * piece_count,
    )
    enc_terms = call(
        encoding_kernel,
        [d_own, from_core, up, down, whole],
        [VMEM] * 5,
        [((OWN_ROWS, width), LOW)] * 4,
    )
    enc_terms = [move(term, gather_back(k)) for k, term in enumerate(enc_terms)]
    enc_terms = [term.astype(F32) for term in enc_terms]
    grad_encodings = (enc_terms[0] + enc_terms[1] + enc_terms[2] + enc_terms[3]).astype(LOW)
    return (branch_out, grad_rows, grad_encodings.reshape(encodings.shape))


def solution(mesh):
    placed = (
        P("seq", "mp"),
        P("mp"),
        P("seq", None, "mp"),
        P("seq", "mp"),
        P("seq", "mp"),
        P("seq", "mp"),
        P("mp", "seq"),
        P("seq", None),
        P("seq", "mp"),
    )
    return jax.shard_map(
        shards,
        mesh=mesh,
        in_specs=placed,
        out_specs=(P("seq", "mp"), P("seq", "mp"), P("seq", None, "mp")),
        check_vma=False,
    )
```

```python
import jax
import jax.numpy as jnp
from jax import lax
from jax.experimental import pallas as pl
from jax.experimental.pallas import tpu as pltpu
from jax.sharding import PartitionSpec as P

HD = 128
STRETCH = 64
NBR = 2
RET = 128
OWN_DEV = 2
OWN_ROWS = OWN_DEV * RET
EXTRA = 16
LOW = jnp.bfloat16
F32 = jnp.float32
epsilon = 1e-05
ANY = pl.BlockSpec(memory_space=pl.ANY)
VMEM = pl.BlockSpec(memory_space=pltpu.VMEM)
SMEM = pl.BlockSpec(memory_space=pltpu.SMEM)
ACROSS = (((1,), (1,)), ((), ()))
DOWN = (((0,), (0,)), ((), ()))


def move(value, step):
    seq_count, mp_count = lax.axis_size("seq"), lax.axis_size("mp")
    z_count = seq_count // 2
    pairs = []
    for d in range(seq_count):
        for m in range(mp_count):
            target = step(d // 2, d % 2, m // 2, m % 2)
            if target is not None:
                z, y, x, c = target
                pairs.append((d * mp_count + m, ((z % z_count) * 2 + y) * mp_count + 2 * x + c))
    return lax.ppermute(value, ("seq", "mp"), pairs)


def spread(k):
    return lambda z, y, x, c: (z, c ^ (k % 2), x ^ (k // 2), y)


def gather_back(k):
    return lambda z, y, x, c: (z, c, x ^ (k // 2), y ^ (k % 2))


def flip_core(z, y, x, c):
    return (z, y, x, 1 - c)


def ring_up(z, y, x, c):
    return (z + 1, y, x, c)


def ring_down(z, y, x, c):
    return (z - 1, y, x, c)


def place():
    d, m = lax.axis_index("seq"), lax.axis_index("mp")
    return d // 2, d % 2, m // 2, m % 2


def in_hbm(value):
    return pltpu.with_memory_space_constraint(value, pltpu.HBM)


def tie(*values):
    return lax.optimization_barrier(values)


def any_weights(own, c, g):
    seq_count = lax.axis_size("seq")
    z_count = seq_count // 2
    rows, width = own.shape[0] // 4, own.shape[1]
    groups = [[2 * i + j for i in range(z_count)] for j in range(2)]
    mine = lax.all_gather(own, "seq", axis=0, axis_index_groups=groups)
    theirs = move(mine, flip_core)
    both = jnp.stack([jnp.where(c == 0, mine, theirs), jnp.where(c == 0, theirs, mine)], axis=1)
    both = jnp.moveaxis(both.reshape(seq_count, 4, rows, width), 1, 0)
    both = both.reshape(4, 4, seq_count * rows // 4, width)
    both = jnp.take(both, g ^ jnp.arange(4), axis=1).reshape(4, seq_count * rows, width)
    return [jnp.concatenate([both[0], both[1]], axis=1)], [jnp.concatenate([both[2], both[3]], axis=1)]


def run_copies(pairs, sems):
    copies = [pltpu.make_async_copy(a, b, sems.at[i]) for i, (a, b) in enumerate(pairs)]
    for copy in copies:
        copy.start()
    for copy in copies:
        copy.wait()


def weight_copies(pieces, whole, first):
    if len(pieces) == 1:
        return [(pieces[0], whole)]
    z, y, x, c = place()
    g = 2 * x + y
    rows, width = pieces[0].shape[0] // 4, pieces[0].shape[1]
    pairs = []
    for side in range(2):
        side_c = c if side == 0 else 1 - c
        for step, ref in zip((0, 3, 1, 2), pieces[4 * side : 4 * side + 4]):
            start = pl.multiple_of((((z + step) % 4 ^ g) * 2 + side_c) * rows, 64)
            for j in range(2):
                pairs.append(
                    (
                        ref.at[pl.ds((first + j) * rows, rows)],
                        whole.at[pl.ds(start, rows), pl.ds(j * width, width)],
                    )
                )
    return pairs


def block(refs, k, start, rows):
    if len(refs) == 4:
        return refs[k].at[pl.ds(start, rows)]
    ref = refs[k // 2]
    return ref.at[pl.ds((k % 2) * (ref.shape[0] // 2) + start, rows)]


def whole_kernel(*refs):
    pieces, (whole, sems) = refs[:-2], refs[-2:]
    run_copies(weight_copies(pieces, whole, 0), sems)


def norm_kernel(token_count, *refs):
    tokens, (normed, inv_out, rows_in, sems) = refs[:4], refs[4:]
    width = tokens[0].shape[1]
    run_copies(
        [(block(tokens, k, 0, token_count + EXTRA), rows_in.at[k]) for k in range(4)],
        sems,
    )
    total = None
    for k in range(4):
        rows = rows_in[k, 0:token_count, :].astype(F32)
        part = jnp.sum(rows * rows, axis=1, keepdims=True)
        total = part if total is None else total + part
    inv_rms = lax.rsqrt(total / (4 * width) + epsilon)
    inv_out[...] = inv_rms
    for k in range(4):
        rows = rows_in[k, 0:token_count, :].astype(F32)
        gain = rows_in[k, token_count : token_count + 1, :].astype(F32)
        normed[:, k * width : (k + 1) * width] = (rows * inv_rms * gain).astype(LOW)


def table_kernel(token_count, *refs):
    tokens, outers = refs[:4], refs[4:6]
    pieces, (tables, shared, whole, encs, sems) = refs[6:-5], refs[-5:]
    width = tokens[0].shape[1]
    pairs = weight_copies(pieces, whole, 0)
    sources = ((outers, 0), (tokens, 2 * token_count + EXTRA), (outers, OWN_ROWS))
    for i, (pair, start) in enumerate(sources):
        for k in range(4):
            target = encs.at[pl.ds(i * OWN_ROWS, OWN_ROWS), pl.ds(k * width, width)]
            pairs.append((block(pair, k, start, OWN_ROWS), target))
    run_copies(pairs, sems)
    tables[...] = jnp.dot(encs[...], whole[...], preferred_element_type=F32).astype(LOW)
    shared[0:OWN_ROWS, :] = tables[OWN_ROWS : 2 * OWN_ROWS, :]
    z, y, x, c = place()
    start = pl.multiple_of(jnp.where(c == 1, 0, 2 * OWN_ROWS), OWN_ROWS)
    shared[OWN_ROWS : 2 * OWN_ROWS, :] = tables[pl.ds(start, OWN_ROWS), :]


def query_kernel(token_count, *refs):
    normed, tokens = refs[0], refs[1:5]
    pieces, (queries, d_attended, whole, rows_in, grads, sems) = refs[5:-6], refs[-6:]
    width = tokens[0].shape[1]
    pairs = weight_copies(pieces, whole, 2) + [(normed, rows_in)]
    for k in range(4):
        source = block(tokens, k, token_count + EXTRA, token_count)
        pairs.append((source, grads.at[:, pl.ds(k * width, width)]))
    run_copies(pairs, sems)
    queries[...] = jnp.dot(rows_in[...], whole[:, 0:width], preferred_element_type=F32).astype(LOW)
    d_attended[...] = jnp.dot(grads[...], whole[:, width:], preferred_element_type=F32).astype(LOW)


def attention_kernel(seq_count, *refs):
    chosen, tables, shared, queries, d_attended = refs[:5]
    attended, d_queries, d_own, d_outer, d_shared, window, d_window, logits, slopes, weights, d_scores, sems = refs[5:]
    token_count, width = queries.shape
    sources = [
        (tables, window.at[pl.ds(0, 3 * OWN_ROWS)]),
        (shared, window.at[pl.ds(3 * OWN_ROWS, 2 * OWN_ROWS)]),
    ]
    copies = [pltpu.make_async_copy(a, b, sems.at[i]) for i, (a, b) in enumerate(sources)]
    for copy in copies:
        copy.start()
    d_window[...] = jnp.zeros_like(d_window)
    scale = HD ** (-0.5)
    z, y, x, c = place()
    t = 2 * z + c
    items = []
    for s in range(token_count // STRETCH):
        starts = []
        for j in range(NBR):
            name = chosen[s * NBR + j]
            away = (name // OWN_DEV - t + 2 + seq_count) % seq_count
            odd = 3 + jnp.where(away == 1, 1 - c, c)
            index = jnp.where(away % 2 == 0, away // 2, odd)
            starts.append(pl.multiple_of(index * OWN_ROWS + (name % OWN_DEV) * RET, RET))
        for h in range(width // HD):
            rows = slice(len(items) * STRETCH, (len(items) + 1) * STRETCH)
            tokens = slice(s * STRETCH, (s + 1) * STRETCH)
            items.append((rows, tokens, slice(h * HD, (h + 1) * HD), slice(width + h * HD, width + (h + 1) * HD), starts))

    def picked(starts, columns):
        return jnp.concatenate([window[pl.ds(a, RET), columns] for a in starts], axis=0)

    for copy in copies:
        copy.wait()
    for rows, tokens, left, right, starts in items:
        logits[rows, :] = lax.dot_general(
            queries[tokens, left], picked(starts, left), ACROSS, preferred_element_type=F32
        )
        slopes[rows, :] = lax.dot_general(
            d_attended[tokens, left], picked(starts, right), ACROSS, preferred_element_type=F32
        )
    scores = logits[...] * scale
    exponent = jnp.exp(scores - jnp.max(scores, axis=1, keepdims=True))
    soft = exponent / jnp.sum(exponent, axis=1, keepdims=True)
    d_weights = slopes[...]
    inner = jnp.sum(d_weights * soft, axis=1, keepdims=True)
    weights[...] = soft.astype(LOW)
    d_scores[...] = (soft * (d_weights - inner) * scale).astype(LOW)
    for rows, tokens, left, right, starts in items:
        attended[tokens, left] = jnp.dot(
            weights[rows, :], picked(starts, right), preferred_element_type=F32
        ).astype(LOW)
        d_queries[tokens, left] = jnp.dot(
            d_scores[rows, :], picked(starts, left), preferred_element_type=F32
        ).astype(LOW)
    for rows, tokens, left, right, starts in items:
        d_keys = lax.dot_general(
            d_scores[rows, :], queries[tokens, left], DOWN, preferred_element_type=F32
        )
        d_values = lax.dot_general(
            weights[rows, :], d_attended[tokens, left], DOWN, preferred_element_type=F32
        )
        for j, a in enumerate(starts):
            d_window[pl.ds(a, RET), left] += d_keys[j * RET : (j + 1) * RET, :]
            d_window[pl.ds(a, RET), right] += d_values[j * RET : (j + 1) * RET, :]
    d_own[...] = d_window[OWN_ROWS : 2 * OWN_ROWS, :]
    d_outer[0:OWN_ROWS, :] = d_window[0:OWN_ROWS, :].astype(LOW)
    d_outer[OWN_ROWS : 2 * OWN_ROWS, :] = d_window[2 * OWN_ROWS : 3 * OWN_ROWS, :].astype(LOW)
    d_shared[...] = d_window[3 * OWN_ROWS : 5 * OWN_ROWS, :].astype(LOW)


def as_row(column):
    return jnp.transpose(jnp.broadcast_to(column, (column.shape[0], 128)))[0:1, :]


def product_kernel(*refs):
    attended, d_queries, inv_rms, tokens = refs[0], refs[1], refs[2], refs[3:7]
    pieces, outs, (whole, rows_in, sems) = refs[7:-7], refs[-7:-3], refs[-3:]
    token_count, width = attended.shape
    term_rows = 2 * token_count + EXTRA
    pairs = weight_copies(pieces, whole, 2)
    for k in range(4):
        pairs.append((block(tokens, k, 0, token_count + EXTRA), rows_in.at[k]))
    run_copies(pairs, sems)
    total = None
    for k in range(4):
        columns = slice(k * width, (k + 1) * width)
        outs[k][0:token_count, :] = lax.dot_general(
            attended[...], whole[columns, width:], ACROSS, preferred_element_type=F32
        ).astype(LOW)
        back = lax.dot_general(
            d_queries[...], whole[columns, 0:width], ACROSS, preferred_element_type=F32
        ).astype(LOW)
        outs[k][token_count : 2 * token_count, :] = back
        rows = rows_in[k, 0:token_count, :].astype(F32)
        gain = rows_in[k, token_count : token_count + 1, :].astype(F32)
        part = jnp.sum(rows * gain * back.astype(F32), axis=1, keepdims=True)
        total = part if total is None else total + part
    lines = []
    for column in (total, inv_rms[...]):
        line = as_row(column)
        high = line.astype(LOW).astype(F32)
        lines += [high, line - high]
    lines.append(jnp.zeros((EXTRA - 4, token_count), F32))
    extra = jnp.concatenate(lines, axis=0)
    extra = jnp.concatenate([extra, jnp.zeros((EXTRA, width - token_count), F32)], axis=1).astype(LOW)
    for out in outs:
        out[term_rows - EXTRA : term_rows, :] = extra


def finish_kernel(hidden, gain, *refs):
    terms, (branch_out, grad_rows) = refs[:4], refs[4:]
    token_count, width = hidden.shape
    branch, normed_grad, extra = None, None, None
    for k, term in enumerate(terms):
        out = term[0:token_count, :].astype(F32)
        back = term[token_count : 2 * token_count, :].astype(F32)
        lines = term[2 * token_count : 2 * token_count + EXTRA, :].astype(F32)
        branch = out if k == 0 else branch + out
        normed_grad = back if k == 0 else normed_grad + back
        extra = lines if k == 0 else extra + lines
        if k == 0:
            inv_row = lines[2:3, 0:token_count] + lines[3:4, 0:token_count]
    branch_out[...] = branch.astype(LOW)
    stat_row = extra[0:1, 0:token_count] + extra[1:2, 0:token_count]

    def as_column(row):
        return jnp.transpose(jnp.broadcast_to(row, (128, token_count)))[:, 0:1]

    statistic = as_column(stat_row) / (4 * width)
    inv_rms = as_column(inv_row)
    rows = hidden[...].astype(F32)
    grad_rows[...] = (
        inv_rms * gain[...].astype(F32)[None, :] * normed_grad - rows * inv_rms * inv_rms * inv_rms * statistic
    ).astype(LOW)


def encoding_kernel(own, from_core, up, down, whole, *outs):
    width = whole.shape[1] // 2
    own_low = own[...] + from_core[0:OWN_ROWS, :].astype(F32)
    own_low = (own_low + up[...].astype(F32) + down[...].astype(F32)).astype(LOW)
    for k, out in enumerate(outs):
        out[...] = lax.dot_general(
            own_low, whole[k * width : (k + 1) * width, :], ACROSS, preferred_element_type=F32
        ).astype(LOW)


def call(kernel, operands, specs, outs, scratch=(), copies=0, out_specs=None):
    scratch = list(scratch)
    if copies:
        scratch.append(pltpu.SemaphoreType.DMA((copies,)))
    return pl.pallas_call(
        kernel,
        out_shape=[jax.ShapeDtypeStruct(shape, dtype) for shape, dtype in outs],
        in_specs=specs,
        out_specs=out_specs or [VMEM] * len(outs),
        scratch_shapes=scratch,
        compiler_params=pltpu.CompilerParams(vmem_limit_bytes=16 * 1024 * 1024),
    )(*operands)


def shards(hidden_rows, norm_gain, encodings, w_query, w_key, w_value, w_out, neighbours, grad_out):
    seq_count = lax.axis_size("seq")
    z, y, x, c = place()
    g = 2 * x + y
    token_count, width = hidden_rows.shape
    full_width = 4 * width
    ids = neighbours.size
    wide = 2 * width

    own_enc = encodings.reshape(OWN_ROWS, width)
    weights = move(jnp.concatenate([w_key, w_value, w_query, w_out.T], axis=0), spread(0))
    enc_below, enc_above = move(own_enc, ring_up), move(own_enc, ring_down)
    id_row = jnp.pad(neighbours.reshape(1, ids).astype(LOW), ((1, EXTRA - 2), (0, width - ids)))
    extra = jnp.pad(norm_gain[None, :], ((0, EXTRA - 1), (0, 0))) + id_row
    packed = jnp.concatenate([hidden_rows, extra, grad_out, own_enc], axis=0)
    weights, enc_below, enc_above, packed = tie(weights, enc_below, enc_above, packed)
    tokens = [move(packed, spread(k)) for k in range(4)]
    outer = jnp.concatenate(
        [enc_below, enc_above, move(enc_below, flip_core), move(enc_above, flip_core)], axis=0
    )
    if seq_count == 8:
        below, above = move(weights, ring_up), move(weights, ring_down)
        below, above, *tokens = tie(below, above, *tokens)
    outers = [move(outer, spread(0)), move(outer, spread(2))]
    normed, inv_rms = call(
        lambda *refs: norm_kernel(token_count, *refs),
        tokens,
        [ANY] * 4,
        [((token_count, full_width), LOW), ((token_count, 1), F32)],
        [pltpu.VMEM((4, token_count + EXTRA, width), LOW)],
        4,
    )
    if seq_count == 8:
        two = move(jnp.where(z % 2 == 0, below, above), lambda z, y, x, c: (z ^ 1, y, x, c))
        pieces = [weights, below, above, two]
        others = [move(piece, flip_core) for piece in pieces[:3]]
        two, normed, *outers = tie(two, normed, *outers)
        kv_pieces = qo_pieces = pieces[:3] + [two] + others + [move(two, flip_core)]
    else:
        kv_pieces, qo_pieces = any_weights(weights, c, g)
    piece_count = len(kv_pieces)

    chosen = tokens[0][token_count + 1, :ids].astype(jnp.int32)
    tables, shared = call(
        lambda *refs: table_kernel(token_count, *refs),
        tokens + outers + kv_pieces,
        [ANY] * (6 + piece_count),
        [((3 * OWN_ROWS, wide), LOW), ((2 * OWN_ROWS, wide), LOW)],
        [pltpu.VMEM((full_width, wide), LOW), pltpu.VMEM((3 * OWN_ROWS, full_width), LOW)],
        12 + 2 * piece_count,
    )
    shared = move(shared, flip_core)
    queries, d_attended = call(
        lambda *refs: query_kernel(token_count, *refs),
        [normed] + tokens + qo_pieces,
        [ANY] * (5 + piece_count),
        [((token_count, width), LOW), ((token_count, width), LOW)],
        [pltpu.VMEM((full_width, wide), LOW)] + [pltpu.VMEM((token_count, full_width), LOW)] * 2,
        5 + 2 * piece_count,
    )
    attended, d_queries, d_own, d_outer, d_shared = call(
        lambda *refs: attention_kernel(seq_count, *refs),
        [chosen, tables, shared, queries, d_attended],
        [SMEM, ANY, ANY, VMEM, VMEM],
        [
            ((token_count, width), LOW),
            ((token_count, width), LOW),
            ((OWN_ROWS, wide), F32),
            ((2 * OWN_ROWS, wide), LOW),
            ((2 * OWN_ROWS, wide), LOW),
        ],
        [pltpu.VMEM((5 * OWN_ROWS, wide), LOW), pltpu.VMEM((5 * OWN_ROWS, wide), F32)]
        + [pltpu.VMEM((token_count * width // HD, NBR * RET), dtype) for dtype in (F32, F32, LOW, LOW)],
        2,
    )
    from_core = move(d_shared, flip_core)
    shared_grad = from_core[OWN_ROWS:].astype(F32)
    to_below = (d_outer[:OWN_ROWS] + jnp.where(c == 1, shared_grad, 0.0)).astype(LOW)
    to_above = (d_outer[OWN_ROWS:] + jnp.where(c == 0, shared_grad, 0.0)).astype(LOW)
    terms = call(
        product_kernel,
        [attended, d_queries, inv_rms] + [in_hbm(o) for o in tokens + qo_pieces],
        [VMEM, VMEM, VMEM] + [ANY] * (4 + piece_count),
        [((2 * token_count + EXTRA, width), LOW)] * 4,
        [
            pltpu.VMEM((full_width, wide), LOW),
            pltpu.VMEM((4, token_count + EXTRA, width), LOW),
        ],
        4 + 2 * piece_count,
    )
    to_below, to_above, *terms = tie(to_below, to_above, *terms)
    up, down = move(to_above, ring_up), move(to_below, ring_down)
    terms = [move(term, gather_back(k)) for k, term in enumerate(terms)]
    branch_out, grad_rows = call(
        finish_kernel,
        [hidden_rows, norm_gain] + terms,
        [VMEM] * 6,
        [((token_count, width), LOW), ((token_count, width), LOW)],
    )
    (whole,) = call(
        whole_kernel,
        [in_hbm(piece) for piece in kv_pieces],
        [ANY] * piece_count,
        [((full_width, wide), LOW)],
        copies=2 * piece_count,
    )
    enc_terms = call(
        encoding_kernel,
        [d_own, from_core, up, down, whole],
        [VMEM] * 5,
        [((OWN_ROWS, width), LOW)] * 4,
    )
    enc_terms = [move(term, gather_back(k)) for k, term in enumerate(enc_terms)]
    enc_terms = [term.astype(F32) for term in enc_terms]
    grad_encodings = (enc_terms[0] + enc_terms[1] + enc_terms[2] + enc_terms[3]).astype(LOW)
    return (branch_out, grad_rows, grad_encodings.reshape(encodings.shape))


def solution(mesh):
    placed = (
        P("seq", "mp"),
        P("mp"),
        P("seq", None, "mp"),
        P("seq", "mp"),
        P("seq", "mp"),
        P("seq", "mp"),
        P("mp", "seq"),
        P("seq", None),
        P("seq", "mp"),
    )
    return jax.shard_map(
        shards,
        mesh=mesh,
        in_specs=placed,
        out_specs=(P("seq", "mp"), P("seq", "mp"), P("seq", None, "mp")),
        check_vma=False,
    )
```

```python
import jax
import jax.numpy as jnp
from jax import lax
from jax.experimental import pallas as pl
from jax.experimental.pallas import tpu as pltpu
from jax.sharding import PartitionSpec as P

HD = 128
STRETCH = 64
NBR = 2
RET = 128
OWN_DEV = 2
OWN_ROWS = OWN_DEV * RET
EXTRA = 16
LOW = jnp.bfloat16
F32 = jnp.float32
epsilon = 1e-05
ANY = pl.BlockSpec(memory_space=pl.ANY)
VMEM = pl.BlockSpec(memory_space=pltpu.VMEM)
SMEM = pl.BlockSpec(memory_space=pltpu.SMEM)
ACROSS = (((1,), (1,)), ((), ()))
DOWN = (((0,), (0,)), ((), ()))


def move(value, step):
    seq_count, mp_count = lax.axis_size("seq"), lax.axis_size("mp")
    z_count = seq_count // 2
    pairs = []
    for d in range(seq_count):
        for m in range(mp_count):
            target = step(d // 2, d % 2, m // 2, m % 2)
            if target is not None:
                z, y, x, c = target
                pairs.append((d * mp_count + m, ((z % z_count) * 2 + y) * mp_count + 2 * x + c))
    return lax.ppermute(value, ("seq", "mp"), pairs)


def spread(k):
    return lambda z, y, x, c: (z, c ^ (k % 2), x ^ (k // 2), y)


def gather_back(k):
    return lambda z, y, x, c: (z, c, x ^ (k // 2), y ^ (k % 2))


def flip_core(z, y, x, c):
    return (z, y, x, 1 - c)


def ring_up(z, y, x, c):
    return (z + 1, y, x, c)


def ring_down(z, y, x, c):
    return (z - 1, y, x, c)


def place():
    d, m = lax.axis_index("seq"), lax.axis_index("mp")
    return d // 2, d % 2, m // 2, m % 2


def in_hbm(value):
    return pltpu.with_memory_space_constraint(value, pltpu.HBM)


def tie(*values):
    return lax.optimization_barrier(values)


def any_weights(own, c, g):
    seq_count = lax.axis_size("seq")
    z_count = seq_count // 2
    rows, width = own.shape[0] // 4, own.shape[1]
    groups = [[2 * i + j for i in range(z_count)] for j in range(2)]
    mine = lax.all_gather(own, "seq", axis=0, axis_index_groups=groups)
    theirs = move(mine, flip_core)
    both = jnp.stack([jnp.where(c == 0, mine, theirs), jnp.where(c == 0, theirs, mine)], axis=1)
    both = jnp.moveaxis(both.reshape(seq_count, 4, rows, width), 1, 0)
    both = both.reshape(4, 4, seq_count * rows // 4, width)
    both = jnp.take(both, g ^ jnp.arange(4), axis=1).reshape(4, seq_count * rows, width)
    return [jnp.concatenate([both[0], both[1]], axis=1)], [jnp.concatenate([both[2], both[3]], axis=1)]


def run_copies(pairs, sems):
    copies = [pltpu.make_async_copy(a, b, sems.at[i]) for i, (a, b) in enumerate(pairs)]
    for copy in copies:
        copy.start()
    for copy in copies:
        copy.wait()


def weight_copies(pieces, whole, first):
    if len(pieces) == 1:
        return [(pieces[0], whole)]
    z, y, x, c = place()
    g = 2 * x + y
    rows, width = pieces[0].shape[0] // 4, pieces[0].shape[1]
    pairs = []
    for side in range(2):
        side_c = c if side == 0 else 1 - c
        for step, ref in zip((0, 3, 1, 2), pieces[4 * side : 4 * side + 4]):
            start = pl.multiple_of((((z + step) % 4 ^ g) * 2 + side_c) * rows, 64)
            for j in range(2):
                pairs.append(
                    (
                        ref.at[pl.ds((first + j) * rows, rows)],
                        whole.at[pl.ds(start, rows), pl.ds(j * width, width)],
                    )
                )
    return pairs


def block(refs, k, start, rows):
    ref = refs[k // 2]
    return ref.at[pl.ds((k % 2) * (ref.shape[0] // 2) + start, rows)]


def join_kernel(*refs):
    parts, (out, sems) = refs[:-2], refs[-2:]
    pairs, start = [], 0
    for part in parts:
        pairs.append((part, out.at[pl.ds(start, part.shape[0])]))
        start += part.shape[0]
    run_copies(pairs, sems)


def whole_kernel(*refs):
    pieces, (whole, sems) = refs[:-2], refs[-2:]
    run_copies(weight_copies(pieces, whole, 0), sems)


def norm_kernel(token_count, *refs):
    tokens, (normed, inv_out, rows_in, sems) = refs[:2], refs[2:]
    width = tokens[0].shape[1]
    run_copies(
        [(block(tokens, k, 0, token_count + EXTRA), rows_in.at[k]) for k in range(4)],
        sems,
    )
    total = None
    for k in range(4):
        rows = rows_in[k, 0:token_count, :].astype(F32)
        part = jnp.sum(rows * rows, axis=1, keepdims=True)
        total = part if total is None else total + part
    inv_rms = lax.rsqrt(total / (4 * width) + epsilon)
    inv_out[...] = inv_rms
    for k in range(4):
        rows = rows_in[k, 0:token_count, :].astype(F32)
        gain = rows_in[k, token_count : token_count + 1, :].astype(F32)
        normed[:, k * width : (k + 1) * width] = (rows * inv_rms * gain).astype(LOW)


def table_kernel(token_count, *refs):
    tokens, outers = refs[:2], refs[2:4]
    pieces, (tables, shared, whole, encs, sems) = refs[4:-5], refs[-5:]
    width = tokens[0].shape[1]
    pairs = weight_copies(pieces, whole, 0)
    sources = ((outers, 0), (tokens, 2 * token_count + EXTRA), (outers, OWN_ROWS))
    for i, (pair, start) in enumerate(sources):
        for k in range(4):
            target = encs.at[pl.ds(i * OWN_ROWS, OWN_ROWS), pl.ds(k * width, width)]
            pairs.append((block(pair, k, start, OWN_ROWS), target))
    run_copies(pairs, sems)
    tables[...] = jnp.dot(encs[...], whole[...], preferred_element_type=F32).astype(LOW)
    shared[0:OWN_ROWS, :] = tables[OWN_ROWS : 2 * OWN_ROWS, :]
    z, y, x, c = place()
    start = pl.multiple_of(jnp.where(c == 1, 0, 2 * OWN_ROWS), OWN_ROWS)
    shared[OWN_ROWS : 2 * OWN_ROWS, :] = tables[pl.ds(start, OWN_ROWS), :]


def query_kernel(token_count, *refs):
    normed, tokens = refs[0], refs[1:3]
    pieces, (queries, d_attended, whole, rows_in, grads, sems) = refs[3:-6], refs[-6:]
    width = tokens[0].shape[1]
    pairs = weight_copies(pieces, whole, 2) + [(normed, rows_in)]
    for k in range(4):
        source = block(tokens, k, token_count + EXTRA, token_count)
        pairs.append((source, grads.at[:, pl.ds(k * width, width)]))
    run_copies(pairs, sems)
    queries[...] = jnp.dot(rows_in[...], whole[:, 0:width], preferred_element_type=F32).astype(LOW)
    d_attended[...] = jnp.dot(grads[...], whole[:, width:], preferred_element_type=F32).astype(LOW)


def attention_kernel(seq_count, *refs):
    chosen, tables, shared, queries, d_attended = refs[:5]
    attended, d_queries, d_own, d_outer, d_shared, window, d_window, logits, slopes, weights, d_scores, sems = refs[5:]
    token_count, width = queries.shape
    sources = [
        (tables, window.at[pl.ds(0, 3 * OWN_ROWS)]),
        (shared, window.at[pl.ds(3 * OWN_ROWS, 2 * OWN_ROWS)]),
    ]
    copies = [pltpu.make_async_copy(a, b, sems.at[i]) for i, (a, b) in enumerate(sources)]
    for copy in copies:
        copy.start()
    d_window[...] = jnp.zeros_like(d_window)
    scale = HD ** (-0.5)
    z, y, x, c = place()
    t = 2 * z + c
    items = []
    for s in range(token_count // STRETCH):
        starts = []
        for j in range(NBR):
            name = chosen[s * NBR + j]
            away = (name // OWN_DEV - t + 2 + seq_count) % seq_count
            odd = 3 + jnp.where(away == 1, 1 - c, c)
            index = jnp.where(away % 2 == 0, away // 2, odd)
            starts.append(pl.multiple_of(index * OWN_ROWS + (name % OWN_DEV) * RET, RET))
        for h in range(width // HD):
            rows = slice(len(items) * STRETCH, (len(items) + 1) * STRETCH)
            tokens = slice(s * STRETCH, (s + 1) * STRETCH)
            items.append((rows, tokens, slice(h * HD, (h + 1) * HD), slice(width + h * HD, width + (h + 1) * HD), starts))

    def picked(starts, columns):
        return jnp.concatenate([window[pl.ds(a, RET), columns] for a in starts], axis=0)

    for copy in copies:
        copy.wait()
    for rows, tokens, left, right, starts in items:
        logits[rows, :] = lax.dot_general(
            queries[tokens, left], picked(starts, left), ACROSS, preferred_element_type=F32
        )
        slopes[rows, :] = lax.dot_general(
            d_attended[tokens, left], picked(starts, right), ACROSS, preferred_element_type=F32
        )
    scores = logits[...] * scale
    exponent = jnp.exp(scores - jnp.max(scores, axis=1, keepdims=True))
    soft = exponent / jnp.sum(exponent, axis=1, keepdims=True)
    d_weights = slopes[...]
    inner = jnp.sum(d_weights * soft, axis=1, keepdims=True)
    weights[...] = soft.astype(LOW)
    d_scores[...] = (soft * (d_weights - inner) * scale).astype(LOW)
    for rows, tokens, left, right, starts in items:
        attended[tokens, left] = jnp.dot(
            weights[rows, :], picked(starts, right), preferred_element_type=F32
        ).astype(LOW)
        d_queries[tokens, left] = jnp.dot(
            d_scores[rows, :], picked(starts, left), preferred_element_type=F32
        ).astype(LOW)
    for rows, tokens, left, right, starts in items:
        d_keys = lax.dot_general(
            d_scores[rows, :], queries[tokens, left], DOWN, preferred_element_type=F32
        )
        d_values = lax.dot_general(
            weights[rows, :], d_attended[tokens, left], DOWN, preferred_element_type=F32
        )
        for j, a in enumerate(starts):
            d_window[pl.ds(a, RET), left] += d_keys[j * RET : (j + 1) * RET, :]
            d_window[pl.ds(a, RET), right] += d_values[j * RET : (j + 1) * RET, :]
    d_own[...] = d_window[OWN_ROWS : 2 * OWN_ROWS, :]
    d_outer[0:OWN_ROWS, :] = d_window[0:OWN_ROWS, :].astype(LOW)
    d_outer[OWN_ROWS : 2 * OWN_ROWS, :] = d_window[2 * OWN_ROWS : 3 * OWN_ROWS, :].astype(LOW)
    d_shared[...] = d_window[3 * OWN_ROWS : 5 * OWN_ROWS, :].astype(LOW)


def as_row(column):
    return jnp.transpose(jnp.broadcast_to(column, (column.shape[0], 128)))[0:1, :]


def product_kernel(*refs):
    attended, d_queries, inv_rms, tokens = refs[0], refs[1], refs[2], refs[3:5]
    pieces, outs, (whole, rows_in, sems) = refs[5:-7], refs[-7:-3], refs[-3:]
    token_count, width = attended.shape
    term_rows = 2 * token_count + EXTRA
    pairs = weight_copies(pieces, whole, 2)
    for k in range(4):
        pairs.append((block(tokens, k, 0, token_count + EXTRA), rows_in.at[k]))
    run_copies(pairs, sems)
    total = None
    for k in range(4):
        columns = slice(k * width, (k + 1) * width)
        outs[k][0:token_count, :] = lax.dot_general(
            attended[...], whole[columns, width:], ACROSS, preferred_element_type=F32
        ).astype(LOW)
        back = lax.dot_general(
            d_queries[...], whole[columns, 0:width], ACROSS, preferred_element_type=F32
        ).astype(LOW)
        outs[k][token_count : 2 * token_count, :] = back
        rows = rows_in[k, 0:token_count, :].astype(F32)
        gain = rows_in[k, token_count : token_count + 1, :].astype(F32)
        part = jnp.sum(rows * gain * back.astype(F32), axis=1, keepdims=True)
        total = part if total is None else total + part
    lines = []
    for column in (total, inv_rms[...]):
        line = as_row(column)
        high = line.astype(LOW).astype(F32)
        lines += [high, line - high]
    lines.append(jnp.zeros((EXTRA - 4, token_count), F32))
    extra = jnp.concatenate(lines, axis=0)
    extra = jnp.concatenate([extra, jnp.zeros((EXTRA, width - token_count), F32)], axis=1).astype(LOW)
    for out in outs:
        out[term_rows - EXTRA : term_rows, :] = extra


def finish_kernel(hidden, gain, *refs):
    terms, (branch_out, grad_rows) = refs[:4], refs[4:]
    token_count, width = hidden.shape
    branch, normed_grad, extra = None, None, None
    for k, term in enumerate(terms):
        out = term[0:token_count, :].astype(F32)
        back = term[token_count : 2 * token_count, :].astype(F32)
        lines = term[2 * token_count : 2 * token_count + EXTRA, :].astype(F32)
        branch = out if k == 0 else branch + out
        normed_grad = back if k == 0 else normed_grad + back
        extra = lines if k == 0 else extra + lines
        if k == 0:
            inv_row = lines[2:3, 0:token_count] + lines[3:4, 0:token_count]
    branch_out[...] = branch.astype(LOW)
    stat_row = extra[0:1, 0:token_count] + extra[1:2, 0:token_count]

    def as_column(row):
        return jnp.transpose(jnp.broadcast_to(row, (128, token_count)))[:, 0:1]

    statistic = as_column(stat_row) / (4 * width)
    inv_rms = as_column(inv_row)
    rows = hidden[...].astype(F32)
    grad_rows[...] = (
        inv_rms * gain[...].astype(F32)[None, :] * normed_grad - rows * inv_rms * inv_rms * inv_rms * statistic
    ).astype(LOW)


def encoding_kernel(own, from_core, up, down, whole, *outs):
    width = whole.shape[1] // 2
    own_low = own[...] + from_core[0:OWN_ROWS, :].astype(F32)
    own_low = (own_low + up[...].astype(F32) + down[...].astype(F32)).astype(LOW)
    for k, out in enumerate(outs):
        out[...] = lax.dot_general(
            own_low, whole[k * width : (k + 1) * width, :], ACROSS, preferred_element_type=F32
        ).astype(LOW)


def call(kernel, operands, specs, outs, scratch=(), copies=0, out_specs=None):
    scratch = list(scratch)
    if copies:
        scratch.append(pltpu.SemaphoreType.DMA((copies,)))
    return pl.pallas_call(
        kernel,
        out_shape=[jax.ShapeDtypeStruct(shape, dtype) for shape, dtype in outs],
        in_specs=specs,
        out_specs=out_specs or [VMEM] * len(outs),
        scratch_shapes=scratch,
        compiler_params=pltpu.CompilerParams(vmem_limit_bytes=16 * 1024 * 1024),
    )(*operands)


def join(parts):
    rows = sum(part.shape[0] for part in parts)
    return call(
        join_kernel,
        parts,
        [ANY] * len(parts),
        [((rows, parts[0].shape[1]), LOW)],
        copies=len(parts),
        out_specs=[ANY],
    )[0]


def shards(hidden_rows, norm_gain, encodings, w_query, w_key, w_value, w_out, neighbours, grad_out):
    seq_count = lax.axis_size("seq")
    z, y, x, c = place()
    g = 2 * x + y
    token_count, width = hidden_rows.shape
    full_width = 4 * width
    ids = neighbours.size
    wide = 2 * width

    own_enc = encodings.reshape(OWN_ROWS, width)
    weights = move(jnp.concatenate([w_key, w_value, w_query, w_out.T], axis=0), spread(0))
    enc_below, enc_above = move(own_enc, ring_up), move(own_enc, ring_down)
    id_row = jnp.pad(neighbours.reshape(1, ids).astype(LOW), ((1, EXTRA - 2), (0, width - ids)))
    extra = jnp.pad(norm_gain[None, :], ((0, EXTRA - 1), (0, 0))) + id_row
    parts = [jnp.concatenate([hidden_rows, extra], axis=0), jnp.concatenate([grad_out, own_enc], axis=0)]
    packed = join(parts + [move(part, flip_core) for part in parts])
    weights, enc_below, enc_above = tie(weights, enc_below, enc_above)
    below_other = move(enc_below, flip_core)
    packed, below_other = tie(packed, below_other)
    tokens = [move(packed, spread(0)), move(packed, spread(2))]
    outer = jnp.concatenate([enc_below, enc_above, below_other, move(enc_above, flip_core)], axis=0)
    if seq_count == 8:
        below, above = move(weights, ring_up), move(weights, ring_down)
        below, above, *tokens = tie(below, above, *tokens)
    outers = [move(outer, spread(0)), move(outer, spread(2))]
    normed, inv_rms = call(
        lambda *refs: norm_kernel(token_count, *refs),
        tokens,
        [ANY] * 2,
        [((token_count, full_width), LOW), ((token_count, 1), F32)],
        [pltpu.VMEM((4, token_count + EXTRA, width), LOW)],
        4,
    )
    if seq_count == 8:
        two = move(jnp.where(z % 2 == 0, below, above), lambda z, y, x, c: (z ^ 1, y, x, c))
        pieces = [weights, below, above, two]
        others = [move(piece, flip_core) for piece in pieces[:3]]
        two, normed, *outers = tie(two, normed, *outers)
        kv_pieces = qo_pieces = pieces[:3] + [two] + others + [move(two, flip_core)]
    else:
        kv_pieces, qo_pieces = any_weights(weights, c, g)
    piece_count = len(kv_pieces)

    chosen = tokens[0][token_count + 1, :ids].astype(jnp.int32)
    tables, shared = call(
        lambda *refs: table_kernel(token_count, *refs),
        tokens + outers + kv_pieces,
        [ANY] * (4 + piece_count),
        [((3 * OWN_ROWS, wide), LOW), ((2 * OWN_ROWS, wide), LOW)],
        [pltpu.VMEM((full_width, wide), LOW), pltpu.VMEM((3 * OWN_ROWS, full_width), LOW)],
        12 + 2 * piece_count,
    )
    shared = move(shared, flip_core)
    queries, d_attended = call(
        lambda *refs: query_kernel(token_count, *refs),
        [normed] + tokens + qo_pieces,
        [ANY] * (3 + piece_count),
        [((token_count, width), LOW), ((token_count, width), LOW)],
        [pltpu.VMEM((full_width, wide), LOW)] + [pltpu.VMEM((token_count, full_width), LOW)] * 2,
        5 + 2 * piece_count,
    )
    attended, d_queries, d_own, d_outer, d_shared = call(
        lambda *refs: attention_kernel(seq_count, *refs),
        [chosen, tables, shared, queries, d_attended],
        [SMEM, ANY, ANY, VMEM, VMEM],
        [
            ((token_count, width), LOW),
            ((token_count, width), LOW),
            ((OWN_ROWS, wide), F32),
            ((2 * OWN_ROWS, wide), LOW),
            ((2 * OWN_ROWS, wide), LOW),
        ],
        [pltpu.VMEM((5 * OWN_ROWS, wide), LOW), pltpu.VMEM((5 * OWN_ROWS, wide), F32)]
        + [pltpu.VMEM((token_count * width // HD, NBR * RET), dtype) for dtype in (F32, F32, LOW, LOW)],
        2,
    )
    from_core = move(d_shared, flip_core)
    shared_grad = from_core[OWN_ROWS:].astype(F32)
    to_below = (d_outer[:OWN_ROWS] + jnp.where(c == 1, shared_grad, 0.0)).astype(LOW)
    to_above = (d_outer[OWN_ROWS:] + jnp.where(c == 0, shared_grad, 0.0)).astype(LOW)
    terms = call(
        product_kernel,
        [attended, d_queries, inv_rms] + [in_hbm(o) for o in tokens + qo_pieces],
        [VMEM, VMEM, VMEM] + [ANY] * (2 + piece_count),
        [((2 * token_count + EXTRA, width), LOW)] * 4,
        [
            pltpu.VMEM((full_width, wide), LOW),
            pltpu.VMEM((4, token_count + EXTRA, width), LOW),
        ],
        4 + 2 * piece_count,
    )
    to_below, to_above, *terms = tie(to_below, to_above, *terms)
    up, down = move(to_above, ring_up), move(to_below, ring_down)
    terms = [move(term, gather_back(k)) for k, term in enumerate(terms)]
    branch_out, grad_rows = call(
        finish_kernel,
        [hidden_rows, norm_gain] + terms,
        [VMEM] * 6,
        [((token_count, width), LOW), ((token_count, width), LOW)],
    )
    (whole,) = call(
        whole_kernel,
        [in_hbm(piece) for piece in kv_pieces],
        [ANY] * piece_count,
        [((full_width, wide), LOW)],
        copies=2 * piece_count,
    )
    enc_terms = call(
        encoding_kernel,
        [d_own, from_core, up, down, whole],
        [VMEM] * 5,
        [((OWN_ROWS, width), LOW)] * 4,
    )
    enc_terms = [move(term, gather_back(k)) for k, term in enumerate(enc_terms)]
    enc_terms = [term.astype(F32) for term in enc_terms]
    grad_encodings = (enc_terms[0] + enc_terms[1] + enc_terms[2] + enc_terms[3]).astype(LOW)
    return (branch_out, grad_rows, grad_encodings.reshape(encodings.shape))


def solution(mesh):
    placed = (
        P("seq", "mp"),
        P("mp"),
        P("seq", None, "mp"),
        P("seq", "mp"),
        P("seq", "mp"),
        P("seq", "mp"),
        P("mp", "seq"),
        P("seq", None),
        P("seq", "mp"),
    )
    return jax.shard_map(
        shards,
        mesh=mesh,
        in_specs=placed,
        out_specs=(P("seq", "mp"), P("seq", "mp"), P("seq", None, "mp")),
        check_vma=False,
    )
```

```python
import jax
import jax.numpy as jnp
from jax import lax
from jax.experimental import pallas as pl
from jax.experimental.pallas import tpu as pltpu
from jax.sharding import PartitionSpec as P

HD = 128
STRETCH = 64
NBR = 2
RET = 128
OWN_DEV = 2
OWN_ROWS = OWN_DEV * RET
EXTRA = 16
LOW = jnp.bfloat16
F32 = jnp.float32
epsilon = 1e-05
ANY = pl.BlockSpec(memory_space=pl.ANY)
VMEM = pl.BlockSpec(memory_space=pltpu.VMEM)
SMEM = pl.BlockSpec(memory_space=pltpu.SMEM)
ACROSS = (((1,), (1,)), ((), ()))
DOWN = (((0,), (0,)), ((), ()))


def move(value, step):
    seq_count, mp_count = lax.axis_size("seq"), lax.axis_size("mp")
    z_count = seq_count // 2
    pairs = []
    for d in range(seq_count):
        for m in range(mp_count):
            target = step(d // 2, d % 2, m // 2, m % 2)
            if target is not None:
                z, y, x, c = target
                pairs.append((d * mp_count + m, ((z % z_count) * 2 + y) * mp_count + 2 * x + c))
    return lax.ppermute(value, ("seq", "mp"), pairs)


def spread(k):
    return lambda z, y, x, c: (z, c ^ (k % 2), x ^ (k // 2), y)


def gather_back(k):
    return lambda z, y, x, c: (z, c, x ^ (k // 2), y ^ (k % 2))


def flip_core(z, y, x, c):
    return (z, y, x, 1 - c)


def ring_up(z, y, x, c):
    return (z + 1, y, x, c)


def ring_down(z, y, x, c):
    return (z - 1, y, x, c)


def place():
    d, m = lax.axis_index("seq"), lax.axis_index("mp")
    return d // 2, d % 2, m // 2, m % 2


def in_hbm(value):
    return pltpu.with_memory_space_constraint(value, pltpu.HBM)


def tie(*values):
    return lax.optimization_barrier(values)


def any_weights(own, c, g):
    seq_count = lax.axis_size("seq")
    z_count = seq_count // 2
    rows, width = own.shape[0] // 4, own.shape[1]
    groups = [[2 * i + j for i in range(z_count)] for j in range(2)]
    mine = lax.all_gather(own, "seq", axis=0, axis_index_groups=groups)
    theirs = move(mine, flip_core)
    both = jnp.stack([jnp.where(c == 0, mine, theirs), jnp.where(c == 0, theirs, mine)], axis=1)
    both = jnp.moveaxis(both.reshape(seq_count, 4, rows, width), 1, 0)
    both = both.reshape(4, 4, seq_count * rows // 4, width)
    both = jnp.take(both, g ^ jnp.arange(4), axis=1).reshape(4, seq_count * rows, width)
    return [jnp.concatenate([both[0], both[1]], axis=1)], [jnp.concatenate([both[2], both[3]], axis=1)]


def run_copies(pairs, sems):
    copies = [pltpu.make_async_copy(a, b, sems.at[i]) for i, (a, b) in enumerate(pairs)]
    for copy in copies:
        copy.start()
    for copy in copies:
        copy.wait()


def weight_copies(pieces, whole, first):
    if len(pieces) == 1:
        return [(pieces[0], whole)]
    z, y, x, c = place()
    g = 2 * x + y
    rows, width = pieces[0].shape[0] // 4, pieces[0].shape[1]
    pairs = []
    for side in range(2):
        side_c = c if side == 0 else 1 - c
        for step, ref in zip((0, 3, 1, 2), pieces[4 * side : 4 * side + 4]):
            start = pl.multiple_of((((z + step) % 4 ^ g) * 2 + side_c) * rows, 64)
            for j in range(2):
                pairs.append(
                    (
                        ref.at[pl.ds((first + j) * rows, rows)],
                        whole.at[pl.ds(start, rows), pl.ds(j * width, width)],
                    )
                )
    return pairs


def block(refs, k, start, rows):
    ref = refs[k // 2]
    return ref.at[pl.ds((k % 2) * (ref.shape[0] // 2) + start, rows)]


def join_kernel(*refs):
    parts, (out, sems) = refs[:-2], refs[-2:]
    pairs, start = [], 0
    for part in parts:
        pairs.append((part, out.at[pl.ds(start, part.shape[0])]))
        start += part.shape[0]
    run_copies(pairs, sems)


def whole_kernel(*refs):
    pieces, (whole, sems) = refs[:-2], refs[-2:]
    run_copies(weight_copies(pieces, whole, 0), sems)


def norm_kernel(token_count, *refs):
    tokens, (normed, inv_out, rows_in, sems) = refs[:2], refs[2:]
    width = tokens[0].shape[1]
    run_copies(
        [(block(tokens, k, 0, token_count + EXTRA), rows_in.at[k]) for k in range(4)],
        sems,
    )
    total = None
    for k in range(4):
        rows = rows_in[k, 0:token_count, :].astype(F32)
        part = jnp.sum(rows * rows, axis=1, keepdims=True)
        total = part if total is None else total + part
    inv_rms = lax.rsqrt(total / (4 * width) + epsilon)
    inv_out[...] = inv_rms
    for k in range(4):
        rows = rows_in[k, 0:token_count, :].astype(F32)
        gain = rows_in[k, token_count : token_count + 1, :].astype(F32)
        normed[:, k * width : (k + 1) * width] = (rows * inv_rms * gain).astype(LOW)


def table_kernel(token_count, *refs):
    tokens, outers = refs[:2], refs[2:4]
    pieces, (tables, shared, whole, encs, sems) = refs[4:-5], refs[-5:]
    width = tokens[0].shape[1]
    pairs = weight_copies(pieces, whole, 0)
    for k in range(4):
        columns = pl.ds(k * width, width)
        pairs.append((block(outers, k, 0, 2 * OWN_ROWS), encs.at[pl.ds(0, 2 * OWN_ROWS), columns]))
        own = block(tokens, k, 2 * token_count + EXTRA, OWN_ROWS)
        pairs.append((own, encs.at[pl.ds(2 * OWN_ROWS, OWN_ROWS), columns]))
    run_copies(pairs, sems)
    tables[...] = jnp.dot(encs[...], whole[...], preferred_element_type=F32).astype(LOW)
    shared[0:OWN_ROWS, :] = tables[2 * OWN_ROWS : 3 * OWN_ROWS, :]
    z, y, x, c = place()
    start = pl.multiple_of(jnp.where(c == 1, 0, OWN_ROWS), OWN_ROWS)
    shared[OWN_ROWS : 2 * OWN_ROWS, :] = tables[pl.ds(start, OWN_ROWS), :]


def query_kernel(token_count, *refs):
    normed, tokens = refs[0], refs[1:3]
    pieces, (queries, d_attended, whole, rows_in, grads, sems) = refs[3:-6], refs[-6:]
    width = tokens[0].shape[1]
    pairs = weight_copies(pieces, whole, 2) + [(normed, rows_in)]
    for k in range(4):
        source = block(tokens, k, token_count + EXTRA, token_count)
        pairs.append((source, grads.at[:, pl.ds(k * width, width)]))
    run_copies(pairs, sems)
    queries[...] = jnp.dot(rows_in[...], whole[:, 0:width], preferred_element_type=F32).astype(LOW)
    d_attended[...] = jnp.dot(grads[...], whole[:, width:], preferred_element_type=F32).astype(LOW)


def attention_kernel(seq_count, *refs):
    chosen, tables, shared, queries, d_attended = refs[:5]
    attended, d_queries, d_own, d_outer, d_shared, d_window, logits, slopes, weights, d_scores = refs[5:]
    token_count, width = queries.shape
    d_window[...] = jnp.zeros_like(d_window)
    scale = HD ** (-0.5)
    z, y, x, c = place()
    t = 2 * z + c
    items = []
    for s in range(token_count // STRETCH):
        starts = []
        for j in range(NBR):
            name = chosen[s * NBR + j]
            away = (name // OWN_DEV - t + 2 + seq_count) % seq_count
            here = away % 2 == 0
            local = (name % OWN_DEV) * RET
            place_here = jnp.where(away == 4, 1, away)
            in_tables = pl.multiple_of(jnp.where(here, place_here, 0) * OWN_ROWS + local, RET)
            other = jnp.where(away == 1, 1 - c, c)
            in_shared = pl.multiple_of(jnp.where(here, 0, other) * OWN_ROWS + local, RET)
            row = pl.multiple_of(jnp.where(here, place_here, 3 + other) * OWN_ROWS + local, RET)
            starts.append((here, in_tables, in_shared, row))
        for h in range(width // HD):
            rows = slice(len(items) * STRETCH, (len(items) + 1) * STRETCH)
            tokens = slice(s * STRETCH, (s + 1) * STRETCH)
            items.append((rows, tokens, slice(h * HD, (h + 1) * HD), slice(width + h * HD, width + (h + 1) * HD), starts))

    def picked(starts, columns):
        return jnp.concatenate(
            [
                jnp.where(here, tables[pl.ds(a, RET), columns], shared[pl.ds(b, RET), columns])
                for here, a, b, _ in starts
            ],
            axis=0,
        )

    for rows, tokens, left, right, starts in items:
        logits[rows, :] = lax.dot_general(
            queries[tokens, left], picked(starts, left), ACROSS, preferred_element_type=F32
        )
        slopes[rows, :] = lax.dot_general(
            d_attended[tokens, left], picked(starts, right), ACROSS, preferred_element_type=F32
        )
    scores = logits[...] * scale
    exponent = jnp.exp(scores - jnp.max(scores, axis=1, keepdims=True))
    soft = exponent / jnp.sum(exponent, axis=1, keepdims=True)
    d_weights = slopes[...]
    inner = jnp.sum(d_weights * soft, axis=1, keepdims=True)
    weights[...] = soft.astype(LOW)
    d_scores[...] = (soft * (d_weights - inner) * scale).astype(LOW)
    for rows, tokens, left, right, starts in items:
        d_keys = lax.dot_general(
            d_scores[rows, :], queries[tokens, left], DOWN, preferred_element_type=F32
        )
        d_values = lax.dot_general(
            weights[rows, :], d_attended[tokens, left], DOWN, preferred_element_type=F32
        )
        for j, (_, _, _, a) in enumerate(starts):
            d_window[pl.ds(a, RET), left] += d_keys[j * RET : (j + 1) * RET, :]
            d_window[pl.ds(a, RET), right] += d_values[j * RET : (j + 1) * RET, :]
    for rows, tokens, left, right, starts in items:
        attended[tokens, left] = jnp.dot(
            weights[rows, :], picked(starts, right), preferred_element_type=F32
        ).astype(LOW)
        d_queries[tokens, left] = jnp.dot(
            d_scores[rows, :], picked(starts, left), preferred_element_type=F32
        ).astype(LOW)
    d_own[...] = d_window[2 * OWN_ROWS : 3 * OWN_ROWS, :]
    d_outer[...] = d_window[0 : 2 * OWN_ROWS, :].astype(LOW)
    d_shared[...] = d_window[3 * OWN_ROWS : 5 * OWN_ROWS, :].astype(LOW)


def as_row(column):
    return jnp.transpose(jnp.broadcast_to(column, (column.shape[0], 128)))[0:1, :]


def product_kernel(*refs):
    attended, d_queries, inv_rms, tokens = refs[0], refs[1], refs[2], refs[3:5]
    pieces, outs, (whole, rows_in, sems) = refs[5:-7], refs[-7:-3], refs[-3:]
    token_count, width = attended.shape
    term_rows = 2 * token_count + EXTRA
    pairs = weight_copies(pieces, whole, 2)
    for k in range(4):
        pairs.append((block(tokens, k, 0, token_count + EXTRA), rows_in.at[k]))
    run_copies(pairs, sems)
    total = None
    for k in range(4):
        columns = slice(k * width, (k + 1) * width)
        outs[k][0:token_count, :] = lax.dot_general(
            attended[...], whole[columns, width:], ACROSS, preferred_element_type=F32
        ).astype(LOW)
        back = lax.dot_general(
            d_queries[...], whole[columns, 0:width], ACROSS, preferred_element_type=F32
        ).astype(LOW)
        outs[k][token_count : 2 * token_count, :] = back
        rows = rows_in[k, 0:token_count, :].astype(F32)
        gain = rows_in[k, token_count : token_count + 1, :].astype(F32)
        part = jnp.sum(rows * gain * back.astype(F32), axis=1, keepdims=True)
        total = part if total is None else total + part
    lines = []
    for column in (total, inv_rms[...]):
        line = as_row(column)
        high = line.astype(LOW).astype(F32)
        lines += [high, line - high]
    lines.append(jnp.zeros((EXTRA - 4, token_count), F32))
    extra = jnp.concatenate(lines, axis=0)
    extra = jnp.concatenate([extra, jnp.zeros((EXTRA, width - token_count), F32)], axis=1).astype(LOW)
    for out in outs:
        out[term_rows - EXTRA : term_rows, :] = extra


def finish_kernel(hidden, gain, *refs):
    terms, (branch_out, grad_rows) = refs[:4], refs[4:]
    token_count, width = hidden.shape
    branch, normed_grad, extra = None, None, None
    for k, term in enumerate(terms):
        out = term[0:token_count, :].astype(F32)
        back = term[token_count : 2 * token_count, :].astype(F32)
        lines = term[2 * token_count : 2 * token_count + EXTRA, :].astype(F32)
        branch = out if k == 0 else branch + out
        normed_grad = back if k == 0 else normed_grad + back
        extra = lines if k == 0 else extra + lines
        if k == 0:
            inv_row = lines[2:3, 0:token_count] + lines[3:4, 0:token_count]
    branch_out[...] = branch.astype(LOW)
    stat_row = extra[0:1, 0:token_count] + extra[1:2, 0:token_count]

    def as_column(row):
        return jnp.transpose(jnp.broadcast_to(row, (128, token_count)))[:, 0:1]

    statistic = as_column(stat_row) / (4 * width)
    inv_rms = as_column(inv_row)
    rows = hidden[...].astype(F32)
    grad_rows[...] = (
        inv_rms * gain[...].astype(F32)[None, :] * normed_grad - rows * inv_rms * inv_rms * inv_rms * statistic
    ).astype(LOW)


def encoding_kernel(own, from_core, up, down, whole, *outs):
    width = whole.shape[1] // 2
    own_low = own[...] + from_core[0:OWN_ROWS, :].astype(F32)
    own_low = (own_low + up[...].astype(F32) + down[...].astype(F32)).astype(LOW)
    for k, out in enumerate(outs):
        out[...] = lax.dot_general(
            own_low, whole[k * width : (k + 1) * width, :], ACROSS, preferred_element_type=F32
        ).astype(LOW)


def call(kernel, operands, specs, outs, scratch=(), copies=0, out_specs=None):
    scratch = list(scratch)
    if copies:
        scratch.append(pltpu.SemaphoreType.DMA((copies,)))
    return pl.pallas_call(
        kernel,
        out_shape=[jax.ShapeDtypeStruct(shape, dtype) for shape, dtype in outs],
        in_specs=specs,
        out_specs=out_specs or [VMEM] * len(outs),
        scratch_shapes=scratch,
        compiler_params=pltpu.CompilerParams(vmem_limit_bytes=16 * 1024 * 1024),
    )(*operands)


def join(parts):
    rows = sum(part.shape[0] for part in parts)
    return call(
        join_kernel,
        parts,
        [ANY] * len(parts),
        [((rows, parts[0].shape[1]), LOW)],
        copies=len(parts),
        out_specs=[ANY],
    )[0]


def shards(hidden_rows, norm_gain, encodings, w_query, w_key, w_value, w_out, neighbours, grad_out):
    seq_count = lax.axis_size("seq")
    z, y, x, c = place()
    g = 2 * x + y
    token_count, width = hidden_rows.shape
    full_width = 4 * width
    ids = neighbours.size
    wide = 2 * width

    own_enc = encodings.reshape(OWN_ROWS, width)
    weights = move(jnp.concatenate([w_key, w_value, w_query, w_out.T], axis=0), spread(0))
    enc_below, enc_above = move(own_enc, ring_up), move(own_enc, ring_down)
    id_row = jnp.pad(neighbours.reshape(1, ids).astype(LOW), ((1, EXTRA - 2), (0, width - ids)))
    extra = jnp.pad(norm_gain[None, :], ((0, EXTRA - 1), (0, 0))) + id_row
    parts = [jnp.concatenate([hidden_rows, extra], axis=0), jnp.concatenate([grad_out, own_enc], axis=0)]
    packed = join(parts + [move(part, flip_core) for part in parts])
    weights, enc_below, enc_above = tie(weights, enc_below, enc_above)
    below_other = move(enc_below, flip_core)
    packed, below_other = tie(packed, below_other)
    tokens = [move(packed, spread(0)), move(packed, spread(2))]
    outer = jnp.concatenate([enc_below, enc_above, below_other, move(enc_above, flip_core)], axis=0)
    if seq_count == 8:
        below, above = move(weights, ring_up), move(weights, ring_down)
        below, above, *tokens = tie(below, above, *tokens)
    outers = [move(outer, spread(0)), move(outer, spread(2))]
    normed, inv_rms = call(
        lambda *refs: norm_kernel(token_count, *refs),
        tokens,
        [ANY] * 2,
        [((token_count, full_width), LOW), ((token_count, 1), F32)],
        [pltpu.VMEM((4, token_count + EXTRA, width), LOW)],
        4,
    )
    if seq_count == 8:
        two = move(jnp.where(z % 2 == 0, below, above), lambda z, y, x, c: (z ^ 1, y, x, c))
        pieces = [weights, below, above, two]
        others = [move(piece, flip_core) for piece in pieces[:3]]
        two, normed, *outers = tie(two, normed, *outers)
        kv_pieces = qo_pieces = pieces[:3] + [two] + others + [move(two, flip_core)]
    else:
        kv_pieces, qo_pieces = any_weights(weights, c, g)
    piece_count = len(kv_pieces)

    chosen = tokens[0][token_count + 1, :ids].astype(jnp.int32)
    tables, shared = call(
        lambda *refs: table_kernel(token_count, *refs),
        tokens + outers + kv_pieces,
        [ANY] * (4 + piece_count),
        [((3 * OWN_ROWS, wide), LOW), ((2 * OWN_ROWS, wide), LOW)],
        [pltpu.VMEM((full_width, wide), LOW), pltpu.VMEM((3 * OWN_ROWS, full_width), LOW)],
        8 + 2 * piece_count,
    )
    shared = move(shared, flip_core)
    queries, d_attended = call(
        lambda *refs: query_kernel(token_count, *refs),
        [normed] + tokens + qo_pieces,
        [ANY] * (3 + piece_count),
        [((token_count, width), LOW), ((token_count, width), LOW)],
        [pltpu.VMEM((full_width, wide), LOW)] + [pltpu.VMEM((token_count, full_width), LOW)] * 2,
        5 + 2 * piece_count,
    )
    attended, d_queries, d_own, d_outer, d_shared = call(
        lambda *refs: attention_kernel(seq_count, *refs),
        [chosen, tables, shared, queries, d_attended],
        [SMEM, VMEM, VMEM, VMEM, VMEM],
        [
            ((token_count, width), LOW),
            ((token_count, width), LOW),
            ((OWN_ROWS, wide), F32),
            ((2 * OWN_ROWS, wide), LOW),
            ((2 * OWN_ROWS, wide), LOW),
        ],
        [pltpu.VMEM((5 * OWN_ROWS, wide), F32)]
        + [pltpu.VMEM((token_count * width // HD, NBR * RET), dtype) for dtype in (F32, F32, LOW, LOW)],
    )
    from_core = move(d_shared, flip_core)
    shared_grad = from_core[OWN_ROWS:].astype(F32)
    to_below = (d_outer[:OWN_ROWS] + jnp.where(c == 1, shared_grad, 0.0)).astype(LOW)
    to_above = (d_outer[OWN_ROWS:] + jnp.where(c == 0, shared_grad, 0.0)).astype(LOW)
    terms = call(
        product_kernel,
        [attended, d_queries, inv_rms] + [in_hbm(o) for o in tokens + qo_pieces],
        [VMEM, VMEM, VMEM] + [ANY] * (2 + piece_count),
        [((2 * token_count + EXTRA, width), LOW)] * 4,
        [
            pltpu.VMEM((full_width, wide), LOW),
            pltpu.VMEM((4, token_count + EXTRA, width), LOW),
        ],
        4 + 2 * piece_count,
    )
    to_below, to_above, *terms = tie(to_below, to_above, *terms)
    up, down = move(to_above, ring_up), move(to_below, ring_down)
    terms = [move(term, gather_back(k)) for k, term in enumerate(terms)]
    branch_out, grad_rows = call(
        finish_kernel,
        [hidden_rows, norm_gain] + terms,
        [VMEM] * 6,
        [((token_count, width), LOW), ((token_count, width), LOW)],
    )
    (whole,) = call(
        whole_kernel,
        [in_hbm(piece) for piece in kv_pieces],
        [ANY] * piece_count,
        [((full_width, wide), LOW)],
        copies=2 * piece_count,
    )
    enc_terms = call(
        encoding_kernel,
        [d_own, from_core, up, down, whole],
        [VMEM] * 5,
        [((OWN_ROWS, width), LOW)] * 4,
    )
    enc_terms = [move(term, gather_back(k)) for k, term in enumerate(enc_terms)]
    enc_terms = [term.astype(F32) for term in enc_terms]
    grad_encodings = (enc_terms[0] + enc_terms[1] + enc_terms[2] + enc_terms[3]).astype(LOW)
    return (branch_out, grad_rows, grad_encodings.reshape(encodings.shape))


def solution(mesh):
    placed = (
        P("seq", "mp"),
        P("mp"),
        P("seq", None, "mp"),
        P("seq", "mp"),
        P("seq", "mp"),
        P("seq", "mp"),
        P("mp", "seq"),
        P("seq", None),
        P("seq", "mp"),
    )
    return jax.shard_map(
        shards,
        mesh=mesh,
        in_specs=placed,
        out_specs=(P("seq", "mp"), P("seq", "mp"), P("seq", None, "mp")),
        check_vma=False,
    )
```

```python
import jax
import jax.numpy as jnp
from jax import lax
from jax.experimental import pallas as pl
from jax.experimental.pallas import tpu as pltpu
from jax.sharding import PartitionSpec as P

HD = 128
STRETCH = 64
NBR = 2
RET = 128
OWN_DEV = 2
OWN_ROWS = OWN_DEV * RET
EXTRA = 16
LOW = jnp.bfloat16
F32 = jnp.float32
epsilon = 1e-05
ANY = pl.BlockSpec(memory_space=pl.ANY)
VMEM = pl.BlockSpec(memory_space=pltpu.VMEM)
SMEM = pl.BlockSpec(memory_space=pltpu.SMEM)
ACROSS = (((1,), (1,)), ((), ()))
DOWN = (((0,), (0,)), ((), ()))


def move(value, step):
    seq_count, mp_count = lax.axis_size("seq"), lax.axis_size("mp")
    z_count = seq_count // 2
    pairs = []
    for d in range(seq_count):
        for m in range(mp_count):
            target = step(d // 2, d % 2, m // 2, m % 2)
            if target is not None:
                z, y, x, c = target
                pairs.append((d * mp_count + m, ((z % z_count) * 2 + y) * mp_count + 2 * x + c))
    return lax.ppermute(value, ("seq", "mp"), pairs)


def spread(k):
    return lambda z, y, x, c: (z, c ^ (k % 2), x ^ (k // 2), y)


def gather_back(k):
    return lambda z, y, x, c: (z, c, x ^ (k // 2), y ^ (k % 2))


def flip_core(z, y, x, c):
    return (z, y, x, 1 - c)


def ring_up(z, y, x, c):
    return (z + 1, y, x, c)


def ring_down(z, y, x, c):
    return (z - 1, y, x, c)


def place():
    d, m = lax.axis_index("seq"), lax.axis_index("mp")
    return d // 2, d % 2, m // 2, m % 2


def in_hbm(value):
    return pltpu.with_memory_space_constraint(value, pltpu.HBM)


def tie(*values):
    return lax.optimization_barrier(values)


def any_weights(own, c, g):
    seq_count = lax.axis_size("seq")
    z_count = seq_count // 2
    rows, width = own.shape[0] // 4, own.shape[1]
    groups = [[2 * i + j for i in range(z_count)] for j in range(2)]
    mine = lax.all_gather(own, "seq", axis=0, axis_index_groups=groups)
    theirs = move(mine, flip_core)
    both = jnp.stack([jnp.where(c == 0, mine, theirs), jnp.where(c == 0, theirs, mine)], axis=1)
    both = jnp.moveaxis(both.reshape(seq_count, 4, rows, width), 1, 0)
    both = both.reshape(4, 4, seq_count * rows // 4, width)
    both = jnp.take(both, g ^ jnp.arange(4), axis=1).reshape(4, seq_count * rows, width)
    return [jnp.concatenate([both[0], both[1]], axis=1)], [jnp.concatenate([both[2], both[3]], axis=1)]


def run_copies(pairs, sems):
    copies = [pltpu.make_async_copy(a, b, sems.at[i]) for i, (a, b) in enumerate(pairs)]
    for copy in copies:
        copy.start()
    for copy in copies:
        copy.wait()


def weight_copies(pieces, whole, first):
    if len(pieces) == 1:
        return [(pieces[0], whole)]
    z, y, x, c = place()
    g = 2 * x + y
    rows, width = pieces[0].shape[0] // 4, pieces[0].shape[1]
    pairs = []
    for side in range(2):
        side_c = c if side == 0 else 1 - c
        for step, ref in zip((0, 3, 1, 2), pieces[4 * side : 4 * side + 4]):
            start = pl.multiple_of((((z + step) % 4 ^ g) * 2 + side_c) * rows, 64)
            for j in range(2):
                pairs.append(
                    (
                        ref.at[pl.ds((first + j) * rows, rows)],
                        whole.at[pl.ds(start, rows), pl.ds(j * width, width)],
                    )
                )
    return pairs


def block(refs, k, start, rows):
    ref = refs[k // 2]
    return ref.at[pl.ds((k % 2) * (ref.shape[0] // 2) + start, rows)]


def join_kernel(*refs):
    parts, (out, sems) = refs[:-2], refs[-2:]
    pairs, start = [], 0
    for part in parts:
        pairs.append((part, out.at[pl.ds(start, part.shape[0])]))
        start += part.shape[0]
    run_copies(pairs, sems)


def whole_kernel(*refs):
    pieces, (whole, sems) = refs[:-2], refs[-2:]
    run_copies(weight_copies(pieces, whole, 0), sems)


def norm_kernel(token_count, *refs):
    tokens, (normed, inv_out, rows_in, sems) = refs[:2], refs[2:]
    width = tokens[0].shape[1]
    run_copies(
        [(block(tokens, k, 0, token_count + EXTRA), rows_in.at[k]) for k in range(4)],
        sems,
    )
    total = None
    for k in range(4):
        rows = rows_in[k, 0:token_count, :].astype(F32)
        part = jnp.sum(rows * rows, axis=1, keepdims=True)
        total = part if total is None else total + part
    inv_rms = lax.rsqrt(total / (4 * width) + epsilon)
    inv_out[...] = inv_rms
    for k in range(4):
        rows = rows_in[k, 0:token_count, :].astype(F32)
        gain = rows_in[k, token_count : token_count + 1, :].astype(F32)
        normed[:, k * width : (k + 1) * width] = (rows * inv_rms * gain).astype(LOW)


def table_kernel(token_count, *refs):
    tokens, outers = refs[:2], refs[2:4]
    pieces, (tables, shared, whole, encs, sems) = refs[4:-5], refs[-5:]
    width = tokens[0].shape[1]
    pairs = weight_copies(pieces, whole, 0)
    for k in range(4):
        columns = pl.ds(k * width, width)
        pairs.append((block(outers, k, 0, 2 * OWN_ROWS), encs.at[pl.ds(0, 2 * OWN_ROWS), columns]))
        own = block(tokens, k, 2 * token_count + EXTRA, OWN_ROWS)
        pairs.append((own, encs.at[pl.ds(2 * OWN_ROWS, OWN_ROWS), columns]))
    run_copies(pairs, sems)
    tables[...] = jnp.dot(encs[...], whole[...], preferred_element_type=F32).astype(LOW)
    shared[0:OWN_ROWS, :] = tables[2 * OWN_ROWS : 3 * OWN_ROWS, :]
    z, y, x, c = place()
    start = pl.multiple_of(jnp.where(c == 1, 0, OWN_ROWS), OWN_ROWS)
    shared[OWN_ROWS : 2 * OWN_ROWS, :] = tables[pl.ds(start, OWN_ROWS), :]


def query_kernel(token_count, *refs):
    normed, tokens = refs[0], refs[1:3]
    pieces, (queries, d_attended, whole, rows_in, grads, sems) = refs[3:-6], refs[-6:]
    width = tokens[0].shape[1]
    pairs = weight_copies(pieces, whole, 2) + [(normed, rows_in)]
    for k in range(4):
        source = block(tokens, k, token_count + EXTRA, token_count)
        pairs.append((source, grads.at[:, pl.ds(k * width, width)]))
    run_copies(pairs, sems)
    queries[...] = jnp.dot(rows_in[...], whole[:, 0:width], preferred_element_type=F32).astype(LOW)
    d_attended[...] = jnp.dot(grads[...], whole[:, width:], preferred_element_type=F32).astype(LOW)


def attention_kernel(seq_count, *refs):
    chosen, tables, shared, queries, d_attended = refs[:5]
    attended, d_queries, d_own, d_outer, d_shared, d_window, logits, slopes, weights, d_scores = refs[5:]
    token_count, width = queries.shape
    d_window[...] = jnp.zeros_like(d_window)
    scale = HD ** (-0.5)
    z, y, x, c = place()
    t = 2 * z + c
    items = []
    for s in range(token_count // STRETCH):
        starts = []
        for j in range(NBR):
            name = chosen[s * NBR + j]
            away = (name // OWN_DEV - t + 2 + seq_count) % seq_count
            here = away % 2 == 0
            local = (name % OWN_DEV) * RET
            place_here = jnp.where(away == 4, 1, away)
            in_tables = pl.multiple_of(jnp.where(here, place_here, 0) * OWN_ROWS + local, RET)
            other = jnp.where(away == 1, 1 - c, c)
            in_shared = pl.multiple_of(jnp.where(here, 0, other) * OWN_ROWS + local, RET)
            row = pl.multiple_of(jnp.where(here, place_here, 3 + other) * OWN_ROWS + local, RET)
            starts.append((here, in_tables, in_shared, row))
        for h in range(width // HD):
            rows = slice(len(items) * STRETCH, (len(items) + 1) * STRETCH)
            tokens = slice(s * STRETCH, (s + 1) * STRETCH)
            items.append((rows, tokens, slice(h * HD, (h + 1) * HD), slice(width + h * HD, width + (h + 1) * HD), starts))

    def picked(starts, columns):
        return jnp.concatenate(
            [
                jnp.where(here, tables[pl.ds(a, RET), columns], shared[pl.ds(b, RET), columns])
                for here, a, b, _ in starts
            ],
            axis=0,
        )

    for rows, tokens, left, right, starts in items:
        logits[rows, :] = lax.dot_general(
            queries[tokens, left], picked(starts, left), ACROSS, preferred_element_type=F32
        )
        slopes[rows, :] = lax.dot_general(
            d_attended[tokens, left], picked(starts, right), ACROSS, preferred_element_type=F32
        )
    scores = logits[...] * scale
    exponent = jnp.exp(scores - jnp.max(scores, axis=1, keepdims=True))
    soft = exponent / jnp.sum(exponent, axis=1, keepdims=True)
    d_weights = slopes[...]
    inner = jnp.sum(d_weights * soft, axis=1, keepdims=True)
    weights[...] = soft.astype(LOW)
    d_scores[...] = (soft * (d_weights - inner) * scale).astype(LOW)
    for rows, tokens, left, right, starts in items:
        d_keys = lax.dot_general(
            d_scores[rows, :], queries[tokens, left], DOWN, preferred_element_type=F32
        )
        d_values = lax.dot_general(
            weights[rows, :], d_attended[tokens, left], DOWN, preferred_element_type=F32
        )
        for j, (_, _, _, a) in enumerate(starts):
            d_window[pl.ds(a, RET), left] += d_keys[j * RET : (j + 1) * RET, :]
            d_window[pl.ds(a, RET), right] += d_values[j * RET : (j + 1) * RET, :]
    for rows, tokens, left, right, starts in items:
        attended[tokens, left] = jnp.dot(
            weights[rows, :], picked(starts, right), preferred_element_type=F32
        ).astype(LOW)
        d_queries[tokens, left] = jnp.dot(
            d_scores[rows, :], picked(starts, left), preferred_element_type=F32
        ).astype(LOW)
    d_own[...] = d_window[2 * OWN_ROWS : 3 * OWN_ROWS, :]
    d_outer[...] = d_window[0 : 2 * OWN_ROWS, :].astype(LOW)
    d_shared[...] = d_window[3 * OWN_ROWS : 5 * OWN_ROWS, :].astype(LOW)


def as_row(column):
    return jnp.transpose(jnp.broadcast_to(column, (column.shape[0], 128)))[0:1, :]


def product_kernel(*refs):
    attended, d_queries, inv_rms, normed = refs[:4]
    pieces, outs, (whole, rows_in, sems) = refs[4:-7], refs[-7:-3], refs[-3:]
    token_count, width = attended.shape
    term_rows = 2 * token_count + EXTRA
    run_copies(weight_copies(pieces, whole, 2) + [(normed, rows_in)], sems)
    total = None
    for k in range(4):
        columns = slice(k * width, (k + 1) * width)
        outs[k][0:token_count, :] = lax.dot_general(
            attended[...], whole[columns, width:], ACROSS, preferred_element_type=F32
        ).astype(LOW)
        back = lax.dot_general(
            d_queries[...], whole[columns, 0:width], ACROSS, preferred_element_type=F32
        ).astype(LOW)
        outs[k][token_count : 2 * token_count, :] = back
        part = jnp.sum(rows_in[:, columns].astype(F32) * back.astype(F32), axis=1, keepdims=True)
        total = part if total is None else total + part
    lines = []
    for column in (total / inv_rms[...], inv_rms[...]):
        line = as_row(column)
        high = line.astype(LOW).astype(F32)
        lines += [high, line - high]
    lines.append(jnp.zeros((EXTRA - 4, token_count), F32))
    extra = jnp.concatenate(lines, axis=0)
    extra = jnp.concatenate([extra, jnp.zeros((EXTRA, width - token_count), F32)], axis=1).astype(LOW)
    for out in outs:
        out[term_rows - EXTRA : term_rows, :] = extra


def finish_kernel(hidden, gain, *refs):
    terms, (branch_out, grad_rows) = refs[:4], refs[4:]
    token_count, width = hidden.shape
    branch, normed_grad, extra = None, None, None
    for k, term in enumerate(terms):
        out = term[0:token_count, :].astype(F32)
        back = term[token_count : 2 * token_count, :].astype(F32)
        lines = term[2 * token_count : 2 * token_count + EXTRA, :].astype(F32)
        branch = out if k == 0 else branch + out
        normed_grad = back if k == 0 else normed_grad + back
        extra = lines if k == 0 else extra + lines
        if k == 0:
            inv_row = lines[2:3, 0:token_count] + lines[3:4, 0:token_count]
    branch_out[...] = branch.astype(LOW)
    stat_row = extra[0:1, 0:token_count] + extra[1:2, 0:token_count]

    def as_column(row):
        return jnp.transpose(jnp.broadcast_to(row, (128, token_count)))[:, 0:1]

    statistic = as_column(stat_row) / (4 * width)
    inv_rms = as_column(inv_row)
    rows = hidden[...].astype(F32)
    grad_rows[...] = (
        inv_rms * gain[...].astype(F32)[None, :] * normed_grad - rows * inv_rms * inv_rms * inv_rms * statistic
    ).astype(LOW)


def encoding_kernel(own, from_core, up, down, whole, *outs):
    width = whole.shape[1] // 2
    own_low = own[...] + from_core[0:OWN_ROWS, :].astype(F32)
    own_low = (own_low + up[...].astype(F32) + down[...].astype(F32)).astype(LOW)
    for k, out in enumerate(outs):
        out[...] = lax.dot_general(
            own_low, whole[k * width : (k + 1) * width, :], ACROSS, preferred_element_type=F32
        ).astype(LOW)


def call(kernel, operands, specs, outs, scratch=(), copies=0, out_specs=None):
    scratch = list(scratch)
    if copies:
        scratch.append(pltpu.SemaphoreType.DMA((copies,)))
    return pl.pallas_call(
        kernel,
        out_shape=[jax.ShapeDtypeStruct(shape, dtype) for shape, dtype in outs],
        in_specs=specs,
        out_specs=out_specs or [VMEM] * len(outs),
        scratch_shapes=scratch,
        compiler_params=pltpu.CompilerParams(vmem_limit_bytes=16 * 1024 * 1024),
    )(*operands)


def join(parts):
    rows = sum(part.shape[0] for part in parts)
    return call(
        join_kernel,
        parts,
        [ANY] * len(parts),
        [((rows, parts[0].shape[1]), LOW)],
        copies=len(parts),
        out_specs=[ANY],
    )[0]


def shards(hidden_rows, norm_gain, encodings, w_query, w_key, w_value, w_out, neighbours, grad_out):
    seq_count = lax.axis_size("seq")
    z, y, x, c = place()
    g = 2 * x + y
    token_count, width = hidden_rows.shape
    full_width = 4 * width
    ids = neighbours.size
    wide = 2 * width

    own_enc = encodings.reshape(OWN_ROWS, width)
    weights = move(jnp.concatenate([w_key, w_value, w_query, w_out.T], axis=0), spread(0))
    enc_below, enc_above = move(own_enc, ring_up), move(own_enc, ring_down)
    id_row = jnp.pad(neighbours.reshape(1, ids).astype(LOW), ((1, EXTRA - 2), (0, width - ids)))
    extra = jnp.pad(norm_gain[None, :], ((0, EXTRA - 1), (0, 0))) + id_row
    parts = [jnp.concatenate([hidden_rows, extra], axis=0), jnp.concatenate([grad_out, own_enc], axis=0)]
    packed = join(parts + [move(part, flip_core) for part in parts])
    weights, enc_below, enc_above = tie(weights, enc_below, enc_above)
    below_other = move(enc_below, flip_core)
    packed, below_other = tie(packed, below_other)
    tokens = [move(packed, spread(0)), move(packed, spread(2))]
    outer = jnp.concatenate([enc_below, enc_above, below_other, move(enc_above, flip_core)], axis=0)
    if seq_count == 8:
        below, above = move(weights, ring_up), move(weights, ring_down)
        below, above, *tokens = tie(below, above, *tokens)
    outers = [move(outer, spread(0)), move(outer, spread(2))]
    normed, inv_rms = call(
        lambda *refs: norm_kernel(token_count, *refs),
        tokens,
        [ANY] * 2,
        [((token_count, full_width), LOW), ((token_count, 1), F32)],
        [pltpu.VMEM((4, token_count + EXTRA, width), LOW)],
        4,
    )
    if seq_count == 8:
        two = move(jnp.where(z % 2 == 0, below, above), lambda z, y, x, c: (z ^ 1, y, x, c))
        pieces = [weights, below, above, two]
        others = [move(piece, flip_core) for piece in pieces[:3]]
        two, normed, *outers = tie(two, normed, *outers)
        kv_pieces = qo_pieces = pieces[:3] + [two] + others + [move(two, flip_core)]
    else:
        kv_pieces, qo_pieces = any_weights(weights, c, g)
    piece_count = len(kv_pieces)

    chosen = tokens[0][token_count + 1, :ids].astype(jnp.int32)
    tables, shared = call(
        lambda *refs: table_kernel(token_count, *refs),
        tokens + outers + kv_pieces,
        [ANY] * (4 + piece_count),
        [((3 * OWN_ROWS, wide), LOW), ((2 * OWN_ROWS, wide), LOW)],
        [pltpu.VMEM((full_width, wide), LOW), pltpu.VMEM((3 * OWN_ROWS, full_width), LOW)],
        8 + 2 * piece_count,
    )
    shared = move(shared, flip_core)
    queries, d_attended = call(
        lambda *refs: query_kernel(token_count, *refs),
        [normed] + tokens + qo_pieces,
        [ANY] * (3 + piece_count),
        [((token_count, width), LOW), ((token_count, width), LOW)],
        [pltpu.VMEM((full_width, wide), LOW)] + [pltpu.VMEM((token_count, full_width), LOW)] * 2,
        5 + 2 * piece_count,
    )
    attended, d_queries, d_own, d_outer, d_shared = call(
        lambda *refs: attention_kernel(seq_count, *refs),
        [chosen, tables, shared, queries, d_attended],
        [SMEM, VMEM, VMEM, VMEM, VMEM],
        [
            ((token_count, width), LOW),
            ((token_count, width), LOW),
            ((OWN_ROWS, wide), F32),
            ((2 * OWN_ROWS, wide), LOW),
            ((2 * OWN_ROWS, wide), LOW),
        ],
        [pltpu.VMEM((5 * OWN_ROWS, wide), F32)]
        + [pltpu.VMEM((token_count * width // HD, NBR * RET), dtype) for dtype in (F32, F32, LOW, LOW)],
    )
    from_core = move(d_shared, flip_core)
    shared_grad = from_core[OWN_ROWS:].astype(F32)
    to_below = (d_outer[:OWN_ROWS] + jnp.where(c == 1, shared_grad, 0.0)).astype(LOW)
    to_above = (d_outer[OWN_ROWS:] + jnp.where(c == 0, shared_grad, 0.0)).astype(LOW)
    terms = call(
        product_kernel,
        [attended, d_queries, inv_rms] + [in_hbm(o) for o in [normed] + qo_pieces],
        [VMEM, VMEM, VMEM] + [ANY] * (1 + piece_count),
        [((2 * token_count + EXTRA, width), LOW)] * 4,
        [
            pltpu.VMEM((full_width, wide), LOW),
            pltpu.VMEM((token_count, full_width), LOW),
        ],
        1 + 2 * piece_count,
    )
    to_below, to_above, *terms = tie(to_below, to_above, *terms)
    up, down = move(to_above, ring_up), move(to_below, ring_down)
    terms = [move(term, gather_back(k)) for k, term in enumerate(terms)]
    branch_out, grad_rows = call(
        finish_kernel,
        [hidden_rows, norm_gain] + terms,
        [VMEM] * 6,
        [((token_count, width), LOW), ((token_count, width), LOW)],
    )
    (whole,) = call(
        whole_kernel,
        [in_hbm(piece) for piece in kv_pieces],
        [ANY] * piece_count,
        [((full_width, wide), LOW)],
        copies=2 * piece_count,
    )
    enc_terms = call(
        encoding_kernel,
        [d_own, from_core, up, down, whole],
        [VMEM] * 5,
        [((OWN_ROWS, width), LOW)] * 4,
    )
    enc_terms = [move(term, gather_back(k)) for k, term in enumerate(enc_terms)]
    enc_terms = [term.astype(F32) for term in enc_terms]
    grad_encodings = (enc_terms[0] + enc_terms[1] + enc_terms[2] + enc_terms[3]).astype(LOW)
    return (branch_out, grad_rows, grad_encodings.reshape(encodings.shape))


def solution(mesh):
    placed = (
        P("seq", "mp"),
        P("mp"),
        P("seq", None, "mp"),
        P("seq", "mp"),
        P("seq", "mp"),
        P("seq", "mp"),
        P("mp", "seq"),
        P("seq", None),
        P("seq", "mp"),
    )
    return jax.shard_map(
        shards,
        mesh=mesh,
        in_specs=placed,
        out_specs=(P("seq", "mp"), P("seq", "mp"), P("seq", None, "mp")),
        check_vma=False,
    )
```
